128 devices in a mesh: grp: 2 (over x_lo), dp: 64 (over x_hi, z, y, core).
Axes of the slice: x: 4 (x_hi: 2, x_lo: 2; x = x_hi * 2 + x_lo), y: 4, z: 4, core: 2. Of those that a mesh axis runs over, the one named last changes fastest.
Arguments:
- attn_out: bfloat16 [32768, 1408], P(('grp', 'dp'))
- out_grad: bfloat16 [32768, 1408], P(('grp', 'dp'))
- image_counts: int32 [128], replicated, may hold values from 1 to 1, as said below
- column_owner: int32 [64], replicated, may hold values from 0 to 63, each once
- damping: float32 [2], replicated, may hold values from 1 to 4
Outputs:
- factors: float32 [2, 1408, 1408], P(None, 'dp')
- preconditioned: float32 [1408, 1408], P(None, 'dp')
The draws below stay inside these ranges and needn't reach their ends.
Inputs may be any that keep to these rules, and one draw needn't show every extreme that they name: image_counts[e] counts the real images of the device at place e of the order grp, dp; some device holds 1 images and some device holds 1. `column_owner`: a permutation.
All inputs are finite; a program needn't handle non-finite values.
Results may differ from the reference program's by a relative error of at most 0.007.
The reference program's roundings to bfloat16 on the way count: a program that leaves them out, or rounds other values in their place, can miss the bound.
Values may be sent and summed in bfloat16 or wider, within the bound.
No kernel may reach another device: no remote copies, remote signals or barrier semaphores. Data moves between devices by JAX's collectives and lax.ppermute only.
A program may use at most 128 MiB of HBM per device.

```python
import math
import jax
import jax.numpy as jnp
from jax import lax

D = 1408
IMG = 1
TOK = 256
ROWS = 32768
N_GRP = 2
N_DP = 64


def mixed_rows(key, scale_top):
    keys = jax.random.split(key, 5)
    rows = ROWS
    noise = jax.random.normal(keys[0], (rows, D + 4), jnp.float32)
    coefs = jax.random.uniform(keys[1], (4, D), jnp.float32, -0.7, 0.7)
    mixed = noise[:, 0:D]
    mixed = mixed + coefs[1] * noise[:, 1:D + 1] + coefs[2] * noise[:, 2:D + 2] + coefs[3] * noise[:, 4:D + 4]
    common = jax.random.normal(keys[2], (rows, 2), jnp.float32)
    loads = jax.random.normal(keys[3], (2, D), jnp.float32) * 0.6
    mixed = mixed + common[:, 0:1] * loads[0] + common[:, 1:2] * loads[1]
    scales = jnp.exp(jax.random.uniform(keys[4], (D,), jnp.float32, 0.0, jnp.log(scale_top)))
    return jnp.clip(mixed * scales * 0.5, -40.0, 40.0)


def draw_attn_out(key, part):
    key = jax.random.fold_in(key, 11)
    values = mixed_rows(key, 5.0)
    return values.astype(jnp.bfloat16)


def draw_out_grad(key, part):
    key = jax.random.fold_in(key, 12)
    values = mixed_rows(key, 5.0)
    return values.astype(jnp.bfloat16)


def draw_image_counts(key, part):
    key = jax.random.fold_in(key, 13)
    keys = jax.random.split(key, 3)
    count = N_GRP * N_DP
    values = jax.random.randint(keys[0], (count,), 1, IMG + 1)
    first = jax.random.randint(keys[1], (), 0, count)
    second = (first + jax.random.randint(keys[2], (), 1, count)) % count
    values = values.at[first].set(IMG)
    values = values.at[second].set(1)
    return values.astype(jnp.int32)


def setup_inputs(seed: int = 0) -> dict:
    splits = jax.random.split(jax.random.key(seed), 6)
    attn_out = draw_attn_out(jax.random.fold_in(splits[5], 71), 0)
    out_grad = draw_out_grad(jax.random.fold_in(splits[5], 71), 0)
    image_counts = draw_image_counts(jax.random.fold_in(splits[5], 71), 0)
    column_owner = jax.random.permutation(splits[3], N_DP).astype(jnp.int32)
    damping = jnp.clip(jnp.exp(jax.random.uniform(splits[4], (2,), jnp.float32, math.log(1.0), math.log(4.0))), 1.0, 4.0)
    return dict(attn_out=attn_out, out_grad=out_grad, image_counts=image_counts, column_owner=column_owner, damping=damping)


def chol_apply(low, rhs):
    inner = lax.linalg.triangular_solve(low, rhs, left_side=True, lower=True)
    return lax.linalg.triangular_solve(low, inner, left_side=True, lower=True, transpose_a=True)

def reference(attn_out, out_grad, image_counts, column_owner, damping):
    per_dev = IMG * TOK
    shards = N_GRP * N_DP
    acts = attn_out.reshape(shards, per_dev, D)
    grads = out_grad.reshape(shards, per_dev, D)
    highest = lax.Precision.HIGHEST
    slots = jnp.arange(per_dev) // TOK

    def accumulate(carry, inputs):
        act_blk, grad_blk, count = inputs
        keep = (slots < count).astype(jnp.float32)[:, None]
        act_f = act_blk.astype(jnp.float32)
        grad_f = grad_blk.astype(jnp.float32)
        act_m = act_f * keep
        grad_m = grad_f * keep
        sum_a = carry[0] + jnp.dot(act_m.T, act_f, precision=highest)
        sum_g = carry[1] + jnp.dot(grad_m.T, grad_f, precision=highest)
        sum_w = carry[2] + jnp.dot(grad_m.T, act_f, precision=highest)
        return ((sum_a, sum_g, sum_w), None)
    zeros = jnp.zeros((D, D), jnp.float32)
    (sum_a, sum_g, sum_w), _ = lax.scan(accumulate, (zeros, zeros, zeros), (acts, grads, image_counts))
    total = (TOK * jnp.sum(image_counts)).astype(jnp.float32)
    cov_a = sum_a / total
    cov_g = sum_g / total
    grad_w = sum_w / total
    factors = jnp.stack([cov_a, cov_g])
    identity = jnp.eye(D, dtype=jnp.float32)
    damp_a = lax.optimization_barrier((cov_a + damping[0] * identity).astype(jnp.bfloat16))
    damp_g = lax.optimization_barrier((cov_g + damping[1] * identity).astype(jnp.bfloat16))
    low_a = lax.optimization_barrier(jnp.linalg.cholesky(damp_a.astype(jnp.float32)).astype(jnp.bfloat16)).astype(jnp.float32)
    low_g = lax.optimization_barrier(jnp.linalg.cholesky(damp_g.astype(jnp.float32)).astype(jnp.bfloat16)).astype(jnp.float32)
    right_done = chol_apply(low_a, grad_w.T).T
    precond = chol_apply(low_g, right_done)
    width = D // N_DP
    blocks = precond.reshape(D, N_DP, width)
    preconditioned = blocks[:, column_owner, :].reshape(D, D)
    return (factors, preconditioned)
```

```python
import jax
import jax.numpy as jnp
from jax import lax
from jax.experimental import pallas as pl
from jax.experimental.pallas import tpu as pltpu
from jax.sharding import PartitionSpec as P

TOK = 256
B = 128
HALF = 64
SLAB = 16
ROWS = 24
F32 = jnp.float32
BF16 = jnp.bfloat16
NT = (((1,), (1,)), ((), ()))
NN = (((1,), (0,)), ((), ()))
TN = (((0,), (0,)), ((), ()))
VM = pl.BlockSpec(memory_space=pltpu.VMEM)
SM = pl.BlockSpec(memory_space=pltpu.SMEM)
PARAMS = pltpu.CompilerParams(vmem_limit_bytes=48 * 1024 * 1024)


def dot(a, b, dims=NT):
    return lax.dot_general(a, b, dims, preferred_element_type=F32)


def split(x):
    hi = x.astype(BF16)
    return hi, (x - hi.astype(F32)).astype(BF16)


def row(x, t):
    return jnp.broadcast_to(x[..., t : t + 1, :], x.shape)


def col(x, c):
    return jnp.broadcast_to(x[..., c : c + 1], x.shape)


def rounded(x):
    return x.astype(BF16).astype(F32)


def tri(i, j):
    return i * (i + 1) // 2 + j


def gram_kernel(core_ref, *refs):
    pieces, out_ref, tmp_ref = refs[:-2], refs[-2], refs[-1]
    nb = pieces[0].shape[1] // B
    start = pl.multiple_of(core_ref[0] * HALF, HALF)
    for i in range(nb):
        wide = (i + 1) * B
        acc = None
        for ref in pieces:
            p = dot(ref[:, i * B : wide], ref[:, :wide], TN)
            acc = p if acc is None else acc + p
        tmp_ref[:, :wide] = acc
        for j in range(i + 1):
            t = tri(i, j)
            out_ref[t * HALF : (t + 1) * HALF, :] = tmp_ref[pl.ds(start, HALF), j * B : (j + 1) * B]
    used = tri(nb, 0) * HALF
    out_ref[used:, :] = jnp.zeros((out_ref.shape[0] - used, B), F32)


def gram(core, pieces, slots):
    width = pieces[0].shape[1]
    return pl.pallas_call(
        gram_kernel,
        out_shape=jax.ShapeDtypeStruct((slots * SLAB, B), F32),
        in_specs=[SM] + [VM] * len(pieces),
        out_specs=VM,
        scratch_shapes=[pltpu.VMEM((B, width), F32)],
        compiler_params=PARAMS,
        name="gram",
    )(core, *pieces)


def factor_diag(block):
    a = block.reshape(16, 8, B)
    lane = lax.broadcasted_iota(jnp.int32, (8, B), 1)
    sub = lax.broadcasted_iota(jnp.int32, (8, B), 0)
    x = jnp.stack([(lane == sub + 8 * g).astype(F32) for g in range(16)])
    inv, inv_r = [], []
    for g in range(16):
        here = (lane >= 8 * g) & (lane < 8 * g + 8)
        cg = [col(a[0], 8 * g + t) for t in range(8)]
        v = jnp.where(here, (lane == sub + 8 * g).astype(F32), a[0])
        xg = x[0]
        rest = a[1:]
        xr = x[1:]
        if g < 15:
            cr = [col(rest, 8 * g + t) for t in range(8)]
            rest = jnp.where(here[None], 0.0, rest)
        for t in range(8):
            p = row(cg[t], t)
            r = lax.rsqrt(p)
            lt = jnp.where(sub > t, cg[t] * r, 0.0)
            vn = row(v, t) * r
            v = jnp.where(sub == t, vn, v - lt * vn)
            xn = row(xg, t) / rounded(p * r)
            xg = jnp.where(sub == t, xn, xg - rounded(lt) * xn)
            cs = {s: row(cg[s], t) * r for s in range(t + 1, 8)}
            for s in range(t + 1, 8):
                cg[s] = cg[s] - lt * cs[s]
            if g < 15:
                lr = cr[t] * r[None]
                rest = rest - lr * vn[None]
                xr = xr - rounded(lr) * xn[None]
                for s in range(t + 1, 8):
                    cr[s] = cr[s] - lr * cs[s][None]
        inv.append(jnp.where(lane <= sub + 8 * g, v, 0.0))
        inv_r.append(xg)
        a, x = rest, xr
    return jnp.concatenate(inv, 0), jnp.concatenate(inv_r, 0)


def chol_kernel(core_ref, mine_ref, other_ref, low_ref, inv_ref, lo_ref, s_ref, w_ref):
    n = low_ref.shape[0]
    nb = n // B
    first = core_ref[0] == 0

    def block(i, j):
        t = tri(i, j) * HALF
        mine = mine_ref[t : t + HALF, :].astype(F32)
        other = other_ref[t : t + HALF, :].astype(F32)
        return jnp.concatenate([jnp.where(first, mine, other), jnp.where(first, other, mine)], 0)

    def update(kk):
        r0 = kk * B
        s = jnp.concatenate([block(i, kk) for i in range(kk, nb)], 0)
        if kk:
            wts = jnp.concatenate([low_ref[r0 : r0 + B, :r0], lo_ref[r0 : r0 + B, :r0]], 0)
            pr = dot(low_ref[r0:, :r0], wts)
            s = s - (pr[:, :B] + pr[:, B:] + dot(lo_ref[r0:, :r0], low_ref[r0 : r0 + B, :r0]))
        s_ref[r0:, :] = s

    def panel(kk):
        r0 = kk * B
        r1 = r0 + B
        shi, slo = split(s_ref[r1:, :])
        pr = dot(shi, w_ref[...])
        lp = pr[:, :B] + pr[:, B:] + dot(slo, w_ref[:B, :])
        hi, lo = split(lp)
        low_ref[r1:, r0:r1] = hi
        lo_ref[r1:, r0:r1] = lo

    def step(k, _):
        for kk in range(nb):
            pl.when(k == kk)(lambda kk=kk: update(kk))
        r0 = pl.multiple_of(k * B, B)
        linv, lrinv = factor_diag(s_ref[pl.ds(r0, B), :])
        inv_ref[pl.ds(r0, B), :] = lrinv
        hi, lo = split(linv)
        w_ref[:B, :] = hi
        w_ref[B:, :] = lo
        for kk in range(nb - 1):
            pl.when(k == kk)(lambda kk=kk: panel(kk))
        return 0

    lax.fori_loop(0, nb, step, 0)


def chol(core, mine, other, n):
    return pl.pallas_call(
        chol_kernel,
        out_shape=(jax.ShapeDtypeStruct((n, n), BF16), jax.ShapeDtypeStruct((n, B), F32)),
        in_specs=[SM, VM, VM],
        out_specs=(VM, VM),
        scratch_shapes=[
            pltpu.VMEM((n, n), BF16),
            pltpu.VMEM((n, B), F32),
            pltpu.VMEM((2 * B, B), BF16),
        ],
        compiler_params=PARAMS,
        name="cholesky",
    )(core, mine, other)


def solve_kernel(rhs_ref, low_ref, inv_ref, out_ref):
    n = low_ref.shape[0]
    nb = n // B
    m = rhs_ref.shape[0]

    def stacked(x):
        return jnp.concatenate(split(x), 0)

    def fold(p):
        return p[:m] + p[m:]

    acc = [rhs_ref[:, b * B : (b + 1) * B] for b in range(nb)]
    for b in range(nb):
        r0, r1 = b * B, (b + 1) * B
        w = stacked(inv_ref[r0:r1, :])
        p = fold(dot(stacked(acc[b]), w))
        y = p[:, :B] + p[:, B:]
        acc[b] = y
        ys = stacked(y)
        for c in range(b + 1, nb):
            acc[c] = acc[c] - fold(dot(ys, low_ref[c * B : (c + 1) * B, r0:r1]))
    for b in reversed(range(nb)):
        r0, r1 = b * B, (b + 1) * B
        w = jnp.concatenate(split(inv_ref[r0:r1, :]), 1)
        p = fold(dot(stacked(acc[b]), w, NN))
        z = p[:, :B] + p[:, B:]
        out_ref[:, r0:r1] = z
        zs = stacked(z)
        for c in range(b):
            acc[c] = acc[c] - fold(dot(zs, low_ref[r0:r1, c * B : (c + 1) * B], NN))


def solve(rhs, low, inv):
    return pl.pallas_call(
        solve_kernel,
        out_shape=jax.ShapeDtypeStruct(rhs.shape, F32),
        in_specs=[VM] * 3,
        out_specs=VM,
        compiler_params=PARAMS,
        name="solve",
    )(rhs, low, inv)


def rows_kernel(at_ref, all_ref, out_ref, s_ref):
    m, n = out_ref.shape
    nb = n // B
    for i in range(nb):
        for j in range(i + 1):
            t = tri(i, j) * HALF
            blk = jnp.concatenate([all_ref[0, t : t + HALF, :], all_ref[1, t : t + HALF, :]], 0)
            s_ref[i * B : (i + 1) * B, j * B : (j + 1) * B] = blk
            if i > j:
                s_ref[j * B : (j + 1) * B, i * B : (i + 1) * B] = blk.T
    at = at_ref[0]
    window = s_ref[pl.ds(pl.multiple_of(at // 8 * 8, 8), 32), :]
    shift = at % 8
    out = window[:m]
    for k in range(1, 8):
        out = jnp.where(shift == k, window[k : k + m], out)
    out_ref[...] = out


def rows_of(at, both, n, m):
    return pl.pallas_call(
        rows_kernel,
        out_shape=jax.ShapeDtypeStruct((m, n), F32),
        in_specs=[SM, VM],
        out_specs=VM,
        scratch_shapes=[pltpu.VMEM((n + 8, n), F32)],
        compiler_params=PARAMS,
        name="rows",
    )(at, both)


def per_device(attn_out, out_grad, image_counts, column_owner, damping):
    n_dp = lax.axis_size("dp")
    dp_index = lax.axis_index("dp")
    grp_index = lax.axis_index("grp")
    place = grp_index * n_dp + dp_index
    per_dev, width = attn_out.shape
    block = width // n_dp
    chips = n_dp // 2
    core = dp_index % 2
    chip = dp_index // 2
    nb = width // B
    used = tri(nb, 0) * HALF // SLAB
    per_chip = -(-used // chips)
    same_core = [list(range(c, n_dp, 2)) for c in range(2)]
    swap_core = [(d, d ^ 1) for d in range(n_dp)]
    swap_grp = [(0, 1), (1, 0)]
    core_arr = core.astype(jnp.int32)[None]
    is_a = grp_index == 0

    count = lax.dynamic_index_in_dim(image_counts, place, 0, keepdims=False)
    keep = (jnp.arange(per_dev) // TOK < count).astype(BF16)[:, None]
    act = attn_out * keep
    grad = out_grad * keep
    own = jnp.where(is_a, act, grad)
    other = jnp.where(is_a, grad, act)
    from_grp = lax.ppermute(other, "grp", swap_grp)
    act_c = lax.ppermute(act, "dp", swap_core)
    grad_c = lax.ppermute(grad, "dp", swap_core)
    own_c = jnp.where(is_a, act_c, grad_c)
    from_grp_c = lax.ppermute(from_grp, "dp", swap_core)

    total = (TOK * jnp.sum(image_counts)).astype(F32)
    part = gram(core_arr, [own, own_c, from_grp, from_grp_c], chips * per_chip)
    part = part.reshape(chips, per_chip * SLAB, B)
    got = lax.all_to_all(part, "dp", split_axis=0, concat_axis=0, tiled=True, axis_index_groups=same_core)
    slabs = jnp.sum(got, axis=0) / total

    flat = chip * (per_chip * SLAB) + jnp.arange(per_chip * SLAB)
    t = flat // HALF
    on_diag = jnp.zeros(t.shape, bool)
    for i in range(nb):
        on_diag = on_diag | (t == tri(i, i))
    in_row = core * HALF + flat % HALF
    diag = (on_diag & (flat < used * SLAB))[:, None] & (in_row[:, None] == jnp.arange(B)[None, :])
    damp = jnp.where(is_a, damping[0], damping[1])
    damped = (slabs + damp * diag.astype(F32)).astype(BF16)
    spread = jnp.broadcast_to(damped[None], (chips,) + damped.shape)
    mine = lax.all_to_all(spread, "dp", split_axis=0, concat_axis=0, tiled=True, axis_index_groups=same_core)
    mine = mine.reshape(chips * per_chip * SLAB, B)
    theirs = lax.ppermute(mine, "dp", swap_core)
    low, inv = chol(core_arr, mine, theirs, width)

    every = lax.all_gather(slabs, "dp", axis=0, tiled=False)
    every = every.reshape(chips, 2, per_chip * SLAB, B).transpose(1, 0, 2, 3).reshape(2, -1, B)
    at = (dp_index * block).astype(jnp.int32)[None]
    my_rows = rows_of(at, every, width, ROWS)[:block]
    their_rows = lax.ppermute(my_rows, "grp", swap_grp)
    factors = jnp.stack([jnp.where(is_a, my_rows, their_rows), jnp.where(is_a, their_rows, my_rows)])

    part_w = lax.dot_general(
        jnp.concatenate([grad, grad_c]), jnp.concatenate([act, act_c]), TN, preferred_element_type=F32
    )
    part_w = jnp.pad(part_w, ((0, n_dp * ROWS - width), (0, 0))).reshape(chips, 2, ROWS, width)
    part_w = lax.dynamic_index_in_dim(part_w, core, 1, keepdims=False)
    got_w = lax.all_to_all(part_w, "dp", split_axis=0, concat_axis=0, tiled=True, axis_index_groups=same_core)
    rows_w = jnp.sum(got_w, axis=0)
    rows_w = (rows_w + lax.ppermute(rows_w, "grp", swap_grp)) / total

    right = solve(rows_w, low, inv)
    routed = right.T.reshape(n_dp, block, ROWS)[column_owner]
    routed = lax.ppermute(routed, "grp", [(0, 1)])
    columns = lax.all_to_all(routed, "dp", split_axis=0, concat_axis=0, tiled=True)
    columns = columns.transpose(1, 0, 2).reshape(block, n_dp * ROWS)[:, :width]
    columns = jnp.pad(columns, ((0, ROWS - block), (0, 0)))
    left = solve(columns, low, inv)[:block]
    back = lax.ppermute(left, "grp", [(1, 0)])
    preconditioned = jnp.where(is_a, back, left).T
    return (factors, preconditioned)


def solution(mesh):
    placed = (P(("grp", "dp"), None), P(("grp", "dp"), None), P(), P(), P())
    return jax.shard_map(
        per_device,
        mesh=mesh,
        in_specs=placed,
        out_specs=(P(None, "dp", None), P(None, "dp")),
        check_vma=False,
    )
```

```python
import jax
import jax.numpy as jnp
from jax import lax
from jax.experimental import pallas as pl
from jax.experimental.pallas import tpu as pltpu
from jax.sharding import PartitionSpec as P

TOK = 256
B = 128
HALF = 64
SLAB = 16
ROWS = 24
F32 = jnp.float32
BF16 = jnp.bfloat16
NT = (((1,), (1,)), ((), ()))
NN = (((1,), (0,)), ((), ()))
TN = (((0,), (0,)), ((), ()))
VM = pl.BlockSpec(memory_space=pltpu.VMEM)
ANY = pl.BlockSpec(memory_space=pl.ANY)
SM = pl.BlockSpec(memory_space=pltpu.SMEM)
MIB = 1024 * 1024


def params(mib):
    return pltpu.CompilerParams(vmem_limit_bytes=mib * MIB)


def cost(micros):
    return pl.CostEstimate(flops=int(micros * 1.1e9), bytes_accessed=MIB, transcendentals=0)


def dot(a, b, dims=NT):
    return lax.dot_general(a, b, dims, preferred_element_type=F32)


def split(x):
    hi = x.astype(BF16)
    return hi, (x - hi.astype(F32)).astype(BF16)


def row(x, t):
    return jnp.broadcast_to(x[..., t : t + 1, :], x.shape)


def col(x, c):
    return jnp.broadcast_to(x[..., c : c + 1], x.shape)


def rounded(x):
    return x.astype(BF16).astype(F32)


def tri(i, j):
    return i * (i + 1) // 2 + j


def gram_kernel(core_ref, keep_ref, *refs):
    pieces, out_ref, tmp_ref = refs[:-2], refs[-2], refs[-1]
    nb = pieces[0].shape[1] // B
    start = pl.multiple_of(core_ref[0] * HALF, HALF)
    for i in range(nb):
        wide = (i + 1) * B
        acc = None
        for k, ref in enumerate(pieces):
            p = dot(ref[:, i * B : wide] * keep_ref[k].astype(BF16), ref[:, :wide], TN)
            acc = p if acc is None else acc + p
        tmp_ref[:, :wide] = acc
        for j in range(i + 1):
            t = tri(i, j)
            out_ref[t * HALF : (t + 1) * HALF, :] = tmp_ref[pl.ds(start, HALF), j * B : (j + 1) * B]
    used = tri(nb, 0) * HALF
    out_ref[used:, :] = jnp.zeros((out_ref.shape[0] - used, B), F32)


def gram(core, keeps, pieces, slots):
    width = pieces[0].shape[1]
    return pl.pallas_call(
        gram_kernel,
        out_shape=jax.ShapeDtypeStruct((slots * SLAB, B), F32),
        in_specs=[SM, SM] + [VM] * len(pieces),
        out_specs=VM,
        scratch_shapes=[pltpu.VMEM((B, width), F32)],
        compiler_params=params(24),
        cost_estimate=cost(3),
        name="gram",
    )(core, keeps, *pieces)


def factor_diag(block):
    a = block.reshape(16, 8, B)
    lane = lax.broadcasted_iota(jnp.int32, (8, B), 1)
    sub = lax.broadcasted_iota(jnp.int32, (8, B), 0)
    x = jnp.stack([(lane == sub + 8 * g).astype(F32) for g in range(16)])
    inv, inv_r = [], []
    for g in range(16):
        here = (lane >= 8 * g) & (lane < 8 * g + 8)
        cg = [col(a[0], 8 * g + t) for t in range(8)]
        v = jnp.where(here, (lane == sub + 8 * g).astype(F32), a[0])
        xg = x[0]
        rest = a[1:]
        xr = x[1:]
        if g < 15:
            cr = [col(rest, 8 * g + t) for t in range(8)]
            rest = jnp.where(here[None], 0.0, rest)
        for t in range(8):
            p = row(cg[t], t)
            r = lax.rsqrt(p)
            lt = jnp.where(sub > t, cg[t] * r, 0.0)
            vn = row(v, t) * r
            v = jnp.where(sub == t, vn, v - lt * vn)
            xn = row(xg, t) / rounded(p * r)
            xg = jnp.where(sub == t, xn, xg - rounded(lt) * xn)
            cs = {s: row(cg[s], t) * r for s in range(t + 1, 8)}
            for s in range(t + 1, 8):
                cg[s] = cg[s] - lt * cs[s]
            if g < 15:
                lr = cr[t] * r[None]
                rest = rest - lr * vn[None]
                xr = xr - rounded(lr) * xn[None]
                for s in range(t + 1, 8):
                    cr[s] = cr[s] - lr * cs[s][None]
        inv.append(jnp.where(lane <= sub + 8 * g, v, 0.0))
        inv_r.append(xg)
        a, x = rest, xr
    return jnp.concatenate(inv, 0), jnp.concatenate(inv_r, 0)


def chol_kernel(core_ref, mine_ref, other_ref, low_ref, inv_ref, lo_ref, s_ref, w_ref):
    n = low_ref.shape[0]
    nb = n // B
    first = core_ref[0] == 0

    def block(i, j):
        t = tri(i, j) * HALF
        mine = mine_ref[t : t + HALF, :].astype(F32)
        other = other_ref[t : t + HALF, :].astype(F32)
        return jnp.concatenate([jnp.where(first, mine, other), jnp.where(first, other, mine)], 0)

    def update(kk):
        r0 = kk * B
        s = jnp.concatenate([block(i, kk) for i in range(kk, nb)], 0)
        if kk:
            wts = jnp.concatenate([low_ref[r0 : r0 + B, :r0], lo_ref[r0 : r0 + B, :r0]], 0)
            pr = dot(low_ref[r0:, :r0], wts)
            s = s - (pr[:, :B] + pr[:, B:] + dot(lo_ref[r0:, :r0], low_ref[r0 : r0 + B, :r0]))
        s_ref[r0:, :] = s

    def panel(kk):
        r0 = kk * B
        r1 = r0 + B
        shi, slo = split(s_ref[r1:, :])
        pr = dot(shi, w_ref[...])
        lp = pr[:, :B] + pr[:, B:] + dot(slo, w_ref[:B, :])
        hi, lo = split(lp)
        low_ref[r1:, r0:r1] = hi
        lo_ref[r1:, r0:r1] = lo

    def step(k, _):
        for kk in range(nb):
            pl.when(k == kk)(lambda kk=kk: update(kk))
        r0 = pl.multiple_of(k * B, B)
        linv, lrinv = factor_diag(s_ref[pl.ds(r0, B), :])
        inv_ref[pl.ds(r0, B), :] = lrinv
        hi, lo = split(linv)
        w_ref[:B, :] = hi
        w_ref[B:, :] = lo
        for kk in range(nb - 1):
            pl.when(k == kk)(lambda kk=kk: panel(kk))
        return 0

    lax.fori_loop(0, nb, step, 0)


def chol(core, mine, other, n):
    return pl.pallas_call(
        chol_kernel,
        out_shape=(jax.ShapeDtypeStruct((n, n), BF16), jax.ShapeDtypeStruct((n, B), F32)),
        in_specs=[SM, VM, VM],
        out_specs=(VM, VM),
        scratch_shapes=[
            pltpu.VMEM((n, n), BF16),
            pltpu.VMEM((n, B), F32),
            pltpu.VMEM((2 * B, B), BF16),
        ],
        compiler_params=params(24),
        cost_estimate=cost(57),
        name="cholesky",
    )(core, mine, other)


def solve_kernel(rhs_ref, low_ref, inv_ref, after_ref, out_ref):
    n = low_ref.shape[0]
    nb = n // B
    m = rhs_ref.shape[0]

    def stacked(x):
        return jnp.concatenate(split(x), 0)

    def fold(p):
        return p[:m] + p[m:]

    acc = [rhs_ref[:, b * B : (b + 1) * B] for b in range(nb)]
    for b in range(nb):
        r0, r1 = b * B, (b + 1) * B
        w = stacked(inv_ref[r0:r1, :])
        p = fold(dot(stacked(acc[b]), w))
        y = p[:, :B] + p[:, B:]
        acc[b] = y
        ys = stacked(y)
        for c in range(b + 1, nb):
            acc[c] = acc[c] - fold(dot(ys, low_ref[c * B : (c + 1) * B, r0:r1]))
    for b in reversed(range(nb)):
        r0, r1 = b * B, (b + 1) * B
        w = jnp.concatenate(split(inv_ref[r0:r1, :]), 1)
        p = fold(dot(stacked(acc[b]), w, NN))
        z = p[:, :B] + p[:, B:]
        out_ref[:, r0:r1] = z
        zs = stacked(z)
        for c in range(b):
            acc[c] = acc[c] - fold(dot(zs, low_ref[r0:r1, c * B : (c + 1) * B], NN))


def solve(rhs, low, inv, after):
    return pl.pallas_call(
        solve_kernel,
        out_shape=jax.ShapeDtypeStruct(rhs.shape, F32),
        in_specs=[VM] * 3 + [ANY],
        out_specs=VM,
        compiler_params=params(16),
        cost_estimate=cost(7),
        name="solve",
    )(rhs, low, inv, after)


def sum_kernel(parts_ref, after_ref, out_ref):
    acc = parts_ref[0]
    for k in range(1, parts_ref.shape[0]):
        acc = acc + parts_ref[k]
    out_ref[...] = acc


def sum_parts(parts, after):
    return pl.pallas_call(
        sum_kernel,
        out_shape=jax.ShapeDtypeStruct(parts.shape[1:], F32),
        in_specs=[VM, ANY],
        out_specs=VM,
        compiler_params=params(16),
        cost_estimate=cost(3),
        name="sum_parts",
    )(parts, after)


def rows_kernel(at_ref, all_ref, out_ref, s_ref):
    m, n = out_ref.shape
    nb = n // B
    per = all_ref.shape[1]
    for i in range(nb):
        for j in range(i + 1):
            t = tri(i, j) * HALF
            blk = jnp.concatenate(
                [all_ref[2 * (f // per) + c, f % per : f % per + SLAB, :]
                 for c in range(2) for f in range(t, t + HALF, SLAB)], 0)
            s_ref[i * B : (i + 1) * B, j * B : (j + 1) * B] = blk
            if i > j:
                s_ref[j * B : (j + 1) * B, i * B : (i + 1) * B] = blk.T
    at = at_ref[0]
    window = s_ref[pl.ds(pl.multiple_of(at // 8 * 8, 8), 32), :]
    shift = at % 8
    out = window[:m]
    for k in range(1, 8):
        out = jnp.where(shift == k, window[k : k + m], out)
    out_ref[...] = out


def rows_of(at, both, n, m):
    return pl.pallas_call(
        rows_kernel,
        out_shape=jax.ShapeDtypeStruct((m, n), F32),
        in_specs=[SM, VM],
        out_specs=VM,
        scratch_shapes=[pltpu.VMEM((n + 8, n), F32)],
        compiler_params=params(24),
        cost_estimate=cost(3),
        name="rows",
    )(at, both)


def per_device(attn_out, out_grad, image_counts, column_owner, damping):
    n_dp = lax.axis_size("dp")
    dp_index = lax.axis_index("dp")
    grp_index = lax.axis_index("grp")
    per_dev, width = attn_out.shape
    block = width // n_dp
    chips = n_dp // 2
    core = dp_index % 2
    chip = dp_index // 2
    nb = width // B
    used = tri(nb, 0) * HALF // SLAB
    per_chip = -(-used // chips)
    same_core = [list(range(c, n_dp, 2)) for c in range(2)]
    swap_core = [(d, d ^ 1) for d in range(n_dp)]
    swap_grp = [(0, 1), (1, 0)]
    core_arr = core.astype(jnp.int32)[None]
    is_a = grp_index == 0

    def keep_of(grp, dp):
        return (lax.dynamic_index_in_dim(image_counts, grp * n_dp + dp, 0, keepdims=False) > 0).astype(F32)

    flip = n_dp // 2
    near = [(g * n_dp + d, (1 - g) * n_dp + d) for g in range(2) for d in range(n_dp)]
    far = [(g * n_dp + d, (1 - g) * n_dp + d ^ flip) for g in range(2) for d in range(n_dp)]
    both = ("grp", "dp")
    half = per_dev // 2

    def cross(perm, rows):
        to_a = lax.ppermute(attn_out[rows], both, [p for p in perm if p[1] < n_dp])
        to_g = lax.ppermute(out_grad[rows], both, [p for p in perm if p[1] >= n_dp])
        return jnp.where(is_a, to_a, to_g)

    from_near = cross(near, slice(0, half))
    from_far = cross(far, slice(half, None))
    act_c = lax.ppermute(attn_out, "dp", swap_core)
    grad_c = lax.ppermute(out_grad, "dp", swap_core)
    own = jnp.where(is_a, attn_out, out_grad)
    own_c = jnp.where(is_a, act_c, grad_c)
    near_c = lax.ppermute(from_near, "dp", swap_core)
    far_c = lax.ppermute(from_far, "dp", swap_core)
    over, mate, away = 1 - grp_index, dp_index ^ 1, dp_index ^ flip
    keeps = jnp.stack([
        keep_of(grp_index, dp_index),
        keep_of(grp_index, mate),
        keep_of(over, dp_index),
        keep_of(over, away),
        keep_of(over, mate),
        keep_of(over, away ^ 1),
    ])
    pieces = [own, own_c, from_near, from_far, near_c, far_c]

    total = (TOK * jnp.sum(image_counts)).astype(F32)
    part = gram(core_arr, keeps, pieces, chips * per_chip)
    part = part.reshape(chips, per_chip * SLAB, B)
    got = lax.all_to_all(part, "dp", split_axis=0, concat_axis=0, tiled=True, axis_index_groups=same_core)
    slabs = jnp.sum(got, axis=0) / total

    flat = chip * (per_chip * SLAB) + jnp.arange(per_chip * SLAB)
    t = flat // HALF
    on_diag = jnp.zeros(t.shape, bool)
    for i in range(nb):
        on_diag = on_diag | (t == tri(i, i))
    in_row = core * HALF + flat % HALF
    diag = (on_diag & (flat < used * SLAB))[:, None] & (in_row[:, None] == jnp.arange(B)[None, :])
    damp = jnp.where(is_a, damping[0], damping[1])
    damped = (slabs + damp * diag.astype(F32)).astype(BF16)
    spread = jnp.broadcast_to(damped[None], (chips,) + damped.shape)
    mine = lax.all_to_all(spread, "dp", split_axis=0, concat_axis=0, tiled=True, axis_index_groups=same_core)
    mine = mine.reshape(chips * per_chip * SLAB, B)
    theirs = lax.ppermute(mine, "dp", swap_core)
    low, inv = chol(core_arr, mine, theirs, width)

    slabs, mine = lax.optimization_barrier((slabs, mine))
    every = lax.all_gather(slabs, "dp", axis=0, tiled=False)
    at = (dp_index * block).astype(jnp.int32)[None]
    my_rows = rows_of(at, every, width, ROWS)[:block]
    their_rows = lax.ppermute(my_rows, "grp", swap_grp)
    factors = jnp.stack([jnp.where(is_a, my_rows, their_rows), jnp.where(is_a, their_rows, my_rows)])

    kept = jnp.concatenate([out_grad * keeps[0].astype(BF16), grad_c * keeps[1].astype(BF16)])
    part_w = dot(kept, jnp.concatenate([attn_out, act_c]), TN)
    part_w = jnp.pad(part_w, ((0, n_dp * ROWS - width), (0, 0))).reshape(chips, 2, ROWS, width)
    part_w = lax.dynamic_index_in_dim(part_w, core, 1, keepdims=False)
    got_w = lax.all_to_all(part_w, "dp", split_axis=0, concat_axis=0, tiled=True, axis_index_groups=same_core)
    rows_w = sum_parts(got_w, inv)
    rows_w = (rows_w + lax.ppermute(rows_w, "grp", swap_grp)) / total

    right = solve(rows_w, low, inv, inv)
    routed = right.T.reshape(n_dp, block, ROWS)[column_owner]
    routed = lax.ppermute(routed, "grp", [(0, 1)])
    columns = lax.all_to_all(routed, "dp", split_axis=0, concat_axis=0, tiled=True)
    columns = columns.transpose(1, 0, 2).reshape(block, n_dp * ROWS)[:, :width]
    columns = jnp.pad(columns, ((0, ROWS - block), (0, 0)))
    left = solve(columns, low, inv, my_rows)[:block]
    back = lax.ppermute(left, "grp", [(1, 0)])
    preconditioned = jnp.where(is_a, back, left).T
    return (factors, preconditioned)


def solution(mesh):
    placed = (P(("grp", "dp"), None), P(("grp", "dp"), None), P(), P(), P())
    return jax.shard_map(
        per_device,
        mesh=mesh,
        in_specs=placed,
        out_specs=(P(None, "dp", None), P(None, "dp")),
        check_vma=False,
    )
```

```python
import jax
import jax.numpy as jnp
from jax import lax
from jax.experimental import pallas as pl
from jax.experimental.pallas import tpu as pltpu
from jax.sharding import PartitionSpec as P

TOK = 256
B = 128
HALF = 64
SLAB = 16
ROWS = 24
F32 = jnp.float32
BF16 = jnp.bfloat16
NT = (((1,), (1,)), ((), ()))
NN = (((1,), (0,)), ((), ()))
TN = (((0,), (0,)), ((), ()))
VM = pl.BlockSpec(memory_space=pltpu.VMEM)
ANY = pl.BlockSpec(memory_space=pl.ANY)
SM = pl.BlockSpec(memory_space=pltpu.SMEM)
MIB = 1024 * 1024


def params(mib):
    return pltpu.CompilerParams(vmem_limit_bytes=mib * MIB)


def cost(micros):
    return pl.CostEstimate(flops=int(micros * 1.1e9), bytes_accessed=MIB, transcendentals=0)


def dot(a, b, dims=NT):
    return lax.dot_general(a, b, dims, preferred_element_type=F32)


def split(x):
    hi = x.astype(BF16)
    return hi, (x - hi.astype(F32)).astype(BF16)


def row(x, t):
    return jnp.broadcast_to(x[..., t : t + 1, :], x.shape)


def col(x, c):
    return jnp.broadcast_to(x[..., c : c + 1], x.shape)


def rounded(x):
    return x.astype(BF16).astype(F32)


def token(x):
    return x[(0,) * (x.ndim - 2)][:8, :B]


def tri(i, j):
    return i * (i + 1) // 2 + j


def columns_of(group, cols, keep_ref=None):
    parts = [ref[:, cols] if keep_ref is None else ref[:, cols] * keep_ref[k].astype(BF16) for k, ref in group]
    return parts[0] if len(parts) == 1 else jnp.concatenate(parts, 0)


def grouped(refs):
    pairs = list(enumerate(refs))
    return [pairs[0:1], pairs[1:2], pairs[2:4], pairs[4:6]]


def gram_kernel(core_ref, keep_ref, *refs):
    pieces, out_ref, tmp_ref = grouped(refs[:6]), refs[6], refs[7]
    nb = refs[0].shape[1] // B
    start = pl.multiple_of(core_ref[0] * HALF, HALF)
    for i in range(nb):
        wide = (i + 1) * B
        acc = None
        for group in pieces:
            p = dot(columns_of(group, slice(i * B, wide), keep_ref), columns_of(group, slice(0, wide)), TN)
            acc = p if acc is None else acc + p
        tmp_ref[:, :wide] = acc
        for j in range(i + 1):
            t = tri(i, j)
            out_ref[t * HALF : (t + 1) * HALF, :] = tmp_ref[pl.ds(start, HALF), j * B : (j + 1) * B]
    used = tri(nb, 0) * HALF
    out_ref[used:, :] = jnp.zeros((out_ref.shape[0] - used, B), F32)


def gram(core, keeps, pieces, slots):
    width = pieces[0].shape[1]
    return pl.pallas_call(
        gram_kernel,
        out_shape=jax.ShapeDtypeStruct((slots * SLAB, B), F32),
        in_specs=[SM, SM] + [VM] * len(pieces),
        out_specs=VM,
        scratch_shapes=[pltpu.VMEM((B, width), F32)],
        compiler_params=params(24),
        cost_estimate=cost(4),
        name="gram",
    )(core, keeps, *pieces)


def cross_kernel(core_ref, keep_ref, after_ref, *refs):
    left, right, out_ref, tmp_ref = grouped(refs[:6]), grouped(refs[6:12]), refs[12], refs[13]
    n = refs[0].shape[1]
    for i in range(n // B):
        acc = None
        for lg, rg in zip(left, right):
            p = dot(columns_of(lg, slice(i * B, (i + 1) * B), keep_ref), columns_of(rg, slice(0, n)), TN)
            acc = p if acc is None else acc + p
        tmp_ref[i * B : (i + 1) * B, :] = acc
    tmp_ref[n:, :] = jnp.zeros((tmp_ref.shape[0] - n, n), F32)
    for q in range(out_ref.shape[0]):
        out_ref[q] = tmp_ref[pl.ds(pl.multiple_of((2 * q + core_ref[0]) * ROWS, 8), ROWS), :]


def cross(core, keeps, after, left, right, chips):
    width = left[0].shape[1]
    return pl.pallas_call(
        cross_kernel,
        out_shape=jax.ShapeDtypeStruct((chips, ROWS, width), F32),
        in_specs=[SM, SM, ANY] + [VM] * 12,
        out_specs=VM,
        scratch_shapes=[pltpu.VMEM((2 * chips * ROWS, width), F32)],
        compiler_params=params(32),
        cost_estimate=cost(8),
        name="cross",
    )(core, keeps, after, *left, *right)


def factor_diag(block):
    a = block.reshape(16, 8, B)
    lane = lax.broadcasted_iota(jnp.int32, (8, B), 1)
    sub = lax.broadcasted_iota(jnp.int32, (8, B), 0)
    x = jnp.stack([(lane == sub + 8 * g).astype(F32) for g in range(16)])
    inv, inv_r = [], []
    for g in range(16):
        here = (lane >= 8 * g) & (lane < 8 * g + 8)
        cg = [col(a[0], 8 * g + t) for t in range(8)]
        v = jnp.where(here, (lane == sub + 8 * g).astype(F32), a[0])
        xg = x[0]
        rest = a[1:]
        xr = x[1:]
        if g < 15:
            cr = [col(rest, 8 * g + t) for t in range(8)]
            rest = jnp.where(here[None], 0.0, rest)
        for t in range(8):
            p = row(cg[t], t)
            r = lax.rsqrt(p)
            lt = jnp.where(sub > t, cg[t] * r, 0.0)
            vn = row(v, t) * r
            v = jnp.where(sub == t, vn, v - lt * vn)
            xn = row(xg, t) / rounded(p * r)
            xg = jnp.where(sub == t, xn, xg - rounded(lt) * xn)
            cs = {s: row(cg[s], t) * r for s in range(t + 1, 8)}
            for s in range(t + 1, 8):
                cg[s] = cg[s] - lt * cs[s]
            if g < 15:
                lr = cr[t] * r[None]
                rest = rest - lr * vn[None]
                xr = xr - rounded(lr) * xn[None]
                for s in range(t + 1, 8):
                    cr[s] = cr[s] - lr * cs[s][None]
        inv.append(jnp.where(lane <= sub + 8 * g, v, 0.0))
        inv_r.append(xg)
        a, x = rest, xr
    return jnp.concatenate(inv, 0), jnp.concatenate(inv_r, 0)


def block_of(mine_ref, other_ref, first, i, j):
    t = tri(i, j) * HALF
    mine = mine_ref[t : t + HALF, :].astype(F32)
    other = other_ref[t : t + HALF, :].astype(F32)
    return jnp.concatenate([jnp.where(first, mine, other), jnp.where(first, other, mine)], 0)


def chol_kernel(core_ref, mine_ref, other_ref, low_ref, inv_ref, lo_ref, s_ref, w_ref):
    n = low_ref.shape[0]
    nb = n // B
    first = core_ref[0] == 0

    def update(kk):
        r0 = kk * B
        s = jnp.concatenate([block_of(mine_ref, other_ref, first, i, kk) for i in range(kk, nb)], 0)
        if kk:
            wts = jnp.concatenate([low_ref[r0 : r0 + B, :r0], lo_ref[r0 : r0 + B, :r0]], 0)
            pr = dot(low_ref[r0:, :r0], wts)
            s = s - (pr[:, :B] + pr[:, B:] + dot(lo_ref[r0:, :r0], low_ref[r0 : r0 + B, :r0]))
        s_ref[r0:, :] = s

    def panel(kk):
        r0 = kk * B
        r1 = r0 + B
        shi, slo = split(s_ref[r1:, :])
        pr = dot(shi, w_ref[...])
        lp = pr[:, :B] + pr[:, B:] + dot(slo, w_ref[:B, :])
        hi, lo = split(lp)
        low_ref[r1:, r0:r1] = hi
        lo_ref[r1:, r0:r1] = lo

    def step(k, _):
        for kk in range(nb):
            pl.when(k == kk)(lambda kk=kk: update(kk))
        r0 = pl.multiple_of(k * B, B)
        linv, lrinv = factor_diag(s_ref[pl.ds(r0, B), :])
        inv_ref[pl.ds(r0, B), :] = lrinv
        hi, lo = split(linv)
        w_ref[:B, :] = hi
        w_ref[B:, :] = lo
        for kk in range(nb - 1):
            pl.when(k == kk)(lambda kk=kk: panel(kk))
        return 0

    lax.fori_loop(0, nb, step, 0)


def chol(core, mine, other, n):
    return pl.pallas_call(
        chol_kernel,
        out_shape=(jax.ShapeDtypeStruct((n, n), BF16), jax.ShapeDtypeStruct((n, B), F32)),
        in_specs=[SM, VM, VM],
        out_specs=(VM, VM),
        scratch_shapes=[
            pltpu.VMEM((n, n), BF16),
            pltpu.VMEM((n, B), F32),
            pltpu.VMEM((2 * B, B), BF16),
        ],
        compiler_params=params(16),
        cost_estimate=cost(57),
        name="cholesky",
    )(core, mine, other)


def solve_kernel(total_ref, parts_ref, low_ref, inv_ref, after_ref, out_ref):
    n = low_ref.shape[0]
    nb = n // B
    m = parts_ref.shape[1]
    total = total_ref[0]

    def stacked(x):
        return jnp.concatenate(split(x), 0)

    def fold(p):
        return p[:m] + p[m:]

    def rhs(b):
        cols = slice(b * B, (b + 1) * B)
        s = parts_ref[0, :, cols]
        for k in range(1, parts_ref.shape[0]):
            s = s + parts_ref[k, :, cols]
        return s / total

    acc = [rhs(b) for b in range(nb)]
    for b in range(nb):
        r0, r1 = b * B, (b + 1) * B
        w = stacked(inv_ref[r0:r1, :])
        p = fold(dot(stacked(acc[b]), w))
        y = p[:, :B] + p[:, B:]
        acc[b] = y
        ys = stacked(y)
        for c in range(b + 1, nb):
            acc[c] = acc[c] - fold(dot(ys, low_ref[c * B : (c + 1) * B, r0:r1]))
    for b in reversed(range(nb)):
        r0, r1 = b * B, (b + 1) * B
        w = jnp.concatenate(split(inv_ref[r0:r1, :]), 1)
        p = fold(dot(stacked(acc[b]), w, NN))
        z = p[:, :B] + p[:, B:]
        out_ref[:, r0:r1] = z
        zs = stacked(z)
        for c in range(b):
            acc[c] = acc[c] - fold(dot(zs, low_ref[r0:r1, c * B : (c + 1) * B], NN))


def solve(total, parts, low, inv, after):
    return pl.pallas_call(
        solve_kernel,
        out_shape=jax.ShapeDtypeStruct(parts.shape[1:], F32),
        in_specs=[SM] + [VM] * 3 + [ANY],
        out_specs=VM,
        compiler_params=params(14),
        cost_estimate=cost(7),
        name="solve",
    )(total, parts, low, inv, after)


def sum_kernel(parts_ref, after_ref, out_ref):
    acc = parts_ref[0]
    for k in range(1, parts_ref.shape[0]):
        acc = acc + parts_ref[k]
    out_ref[...] = acc


def sum_parts(parts, after):
    return pl.pallas_call(
        sum_kernel,
        out_shape=jax.ShapeDtypeStruct(parts.shape[1:], F32),
        in_specs=[VM, ANY],
        out_specs=VM,
        compiler_params=params(16),
        cost_estimate=cost(3),
        name="sum_parts",
    )(parts, after)


def rows_kernel(at_ref, core_ref, mine_ref, other_ref, diag_ref, out_ref, s_ref):
    m, n = out_ref.shape
    nb = n // B
    first = core_ref[0] == 0
    for i in range(nb):
        for j in range(i + 1):
            blk = block_of(mine_ref, other_ref, first, i, j)
            s_ref[i * B : (i + 1) * B, j * B : (j + 1) * B] = blk
            if i > j:
                s_ref[j * B : (j + 1) * B, i * B : (i + 1) * B] = blk.T
    at = at_ref[0]
    window = s_ref[pl.ds(pl.multiple_of(at // 8 * 8, 8), 32), :]
    shift = at % 8
    out = window[:m]
    for k in range(1, 8):
        out = jnp.where(shift == k, window[k : k + m], out)
    ri = lax.broadcasted_iota(jnp.int32, (m, n), 0)
    ci = lax.broadcasted_iota(jnp.int32, (m, n), 1)
    out_ref[...] = jnp.where(ci == ri + at, diag_ref[...], out)


def rows_of(at, core, mine, other, diag, n, m):
    return pl.pallas_call(
        rows_kernel,
        out_shape=jax.ShapeDtypeStruct((m, n), F32),
        in_specs=[SM, SM, VM, VM, VM],
        out_specs=VM,
        scratch_shapes=[pltpu.VMEM((n + 8, n), F32)],
        compiler_params=params(14),
        cost_estimate=cost(3),
        name="rows",
    )(at, core, mine, other, diag)


def per_device(attn_out, out_grad, image_counts, column_owner, damping):
    n_dp = lax.axis_size("dp")
    dp_index = lax.axis_index("dp")
    grp_index = lax.axis_index("grp")
    per_dev, width = attn_out.shape
    block = width // n_dp
    chips = n_dp // 2
    core = dp_index % 2
    chip = dp_index // 2
    nb = width // B
    used = tri(nb, 0) * HALF // SLAB
    per_chip = -(-used // chips)
    same_core = [list(range(c, n_dp, 2)) for c in range(2)]
    swap_core = [(d, d ^ 1) for d in range(n_dp)]
    swap_grp = [(0, 1), (1, 0)]
    core_arr = core.astype(jnp.int32)[None]
    is_a = grp_index == 0

    def keep_of(grp, dp):
        return (lax.dynamic_index_in_dim(image_counts, grp * n_dp + dp, 0, keepdims=False) > 0).astype(F32)

    flip = n_dp // 2
    near = [(g * n_dp + d, (1 - g) * n_dp + d) for g in range(2) for d in range(n_dp)]
    far = [(g * n_dp + d, (1 - g) * n_dp + d ^ flip) for g in range(2) for d in range(n_dp)]
    both = ("grp", "dp")
    half = per_dev // 2

    def to_a(perm):
        return [p for p in perm if p[1] < n_dp]

    other = jnp.where(is_a, out_grad, attn_out)
    from_near = lax.ppermute(other[:half], both, near)
    from_far = lax.ppermute(other[half:], both, far)
    act_c = lax.ppermute(attn_out, "dp", swap_core)
    grad_c = lax.ppermute(out_grad, "dp", swap_core)
    own = jnp.where(is_a, attn_out, out_grad)
    own_c = jnp.where(is_a, act_c, grad_c)
    near_c = lax.ppermute(from_near, "dp", swap_core)
    far_c = lax.ppermute(from_far, "dp", swap_core)
    over, mate, away = 1 - grp_index, dp_index ^ 1, dp_index ^ flip
    keeps = jnp.stack([
        keep_of(grp_index, dp_index),
        keep_of(grp_index, mate),
        keep_of(over, dp_index),
        keep_of(over, away),
        keep_of(over, mate),
        keep_of(over, away ^ 1),
    ])
    pieces = [own, own_c, from_near, from_far, near_c, far_c]

    total = (TOK * jnp.sum(image_counts)).astype(F32)
    part = gram(core_arr, keeps, pieces, chips * per_chip)
    got = lax.all_to_all(
        part.reshape(chips, per_chip * SLAB, B), "dp", split_axis=0, concat_axis=0, tiled=True, axis_index_groups=same_core
    )

    out_grad_, _ = lax.optimization_barrier((out_grad, from_near))
    grad_near = lax.ppermute(out_grad_[:half], both, to_a(near))
    grad_far = lax.ppermute(out_grad_[half:], both, to_a(far))
    grads = [
        out_grad, grad_c, grad_near, grad_far,
        lax.ppermute(grad_near, "dp", swap_core), lax.ppermute(grad_far, "dp", swap_core),
    ]
    acts = [attn_out, act_c, from_near, from_far, near_c, far_c]
    part_w = cross(core_arr, keeps, token(part), grads, acts, chips)

    slabs = sum_parts(got, token(part_w)) / total

    flat = chip * (per_chip * SLAB) + jnp.arange(per_chip * SLAB)
    t = flat // HALF
    on_diag = jnp.zeros(t.shape, bool)
    for i in range(nb):
        on_diag = on_diag | (t == tri(i, i))
    in_row = core * HALF + flat % HALF
    diag = (on_diag & (flat < used * SLAB))[:, None] & (in_row[:, None] == jnp.arange(B)[None, :])
    damp = jnp.where(is_a, damping[0], damping[1])
    damped = (slabs + damp * diag.astype(F32)).astype(BF16)
    spread = jnp.broadcast_to(damped[None], (chips,) + damped.shape)
    mine = lax.all_to_all(spread, "dp", split_axis=0, concat_axis=0, tiled=True, axis_index_groups=same_core)
    mine = mine.reshape(chips * per_chip * SLAB, B)
    theirs = lax.ppermute(mine, "dp", swap_core)
    low, inv = chol(core_arr, mine, theirs, width)

    got_w = lax.all_to_all(part_w, "dp", split_axis=0, concat_axis=0, tiled=True, axis_index_groups=same_core)

    squares = jnp.stack([attn_out, out_grad]).astype(F32)
    squares = jnp.sum(squares * squares, axis=1) * keeps[0]
    diags = lax.psum(squares, both) / total
    at = (dp_index * block).astype(jnp.int32)[None]
    my_diag = jnp.where(is_a, diags[0], diags[1])[None]
    my_rows = rows_of(at, core_arr, mine, theirs, my_diag, width, ROWS)[:block]
    their_rows = lax.ppermute(my_rows, "grp", swap_grp)
    factors = jnp.stack([jnp.where(is_a, my_rows, their_rows), jnp.where(is_a, their_rows, my_rows)])

    right = solve(total[None], got_w, low, inv, token(inv))
    order = column_owner.reshape(chips, 2).T.reshape(n_dp)
    routed = right.T.reshape(n_dp, block, ROWS)[order].reshape(2, chips, block, ROWS)
    mine_t = lax.dynamic_index_in_dim(routed, core, 0, keepdims=False)
    other_t = lax.dynamic_index_in_dim(routed, 1 - core, 0, keepdims=False)
    same = lax.ppermute(mine_t, both, [(d, n_dp + d) for d in range(n_dp)])
    cross_t = lax.ppermute(other_t, both, [(d, n_dp + (d ^ 1)) for d in range(n_dp)])
    is_first = core == 0
    pair = jnp.concatenate([jnp.where(is_first, same, cross_t), jnp.where(is_first, cross_t, same)], axis=2)
    columns = lax.all_to_all(pair, "dp", split_axis=0, concat_axis=0, tiled=True, axis_index_groups=same_core)
    columns = columns.transpose(1, 0, 2).reshape(block, n_dp * ROWS)[:, :width]
    columns = jnp.pad(columns, ((0, ROWS - block), (0, 0)))
    left = solve(jnp.ones((1,), F32), columns[None], low, inv, token(my_rows))[:block]
    back = lax.ppermute(left, "grp", [(1, 0)])
    preconditioned = jnp.where(is_a, back, left).T
    return (factors, preconditioned)


def solution(mesh):
    placed = (P(("grp", "dp"), None), P(("grp", "dp"), None), P(), P(), P())
    return jax.shard_map(
        per_device,
        mesh=mesh,
        in_specs=placed,
        out_specs=(P(None, "dp", None), P(None, "dp")),
        check_vma=False,
    )
```

```python
import functools

import jax
import jax.numpy as jnp
from jax import lax
from jax.experimental import pallas as pl
from jax.experimental.pallas import tpu as pltpu
from jax.sharding import PartitionSpec as P

TOK = 256
B = 128
HALF = 64
SLAB = 16
ROWS = 24
F32 = jnp.float32
BF16 = jnp.bfloat16
NT = (((1,), (1,)), ((), ()))
NN = (((1,), (0,)), ((), ()))
TN = (((0,), (0,)), ((), ()))
VM = pl.BlockSpec(memory_space=pltpu.VMEM)
ANY = pl.BlockSpec(memory_space=pl.ANY)
SM = pl.BlockSpec(memory_space=pltpu.SMEM)
TOKEN = jax.ShapeDtypeStruct((8, B), F32)
MIB = 1024 * 1024


def params(mib):
    return pltpu.CompilerParams(vmem_limit_bytes=mib * MIB)


def cost(micros):
    return pl.CostEstimate(flops=int(micros * 1.1e9), bytes_accessed=MIB, transcendentals=0)


def dot(a, b, dims=NT):
    return lax.dot_general(a, b, dims, preferred_element_type=F32)


def split(x):
    hi = x.astype(BF16)
    return hi, (x - hi.astype(F32)).astype(BF16)


def row(x, t):
    return jnp.broadcast_to(x[..., t : t + 1, :], x.shape)


def col(x, c):
    return jnp.broadcast_to(x[..., c : c + 1], x.shape)


def rounded(x):
    return x.astype(BF16).astype(F32)


def tri(i, j):
    return i * (i + 1) // 2 + j


def pieces_of(refs):
    own, mate, near, far, near_mate, far_mate = refs
    return [[(0, own)], [(1, mate)], [(2, near), (3, far)], [(4, near_mate), (5, far_mate)]]


def columns_of(group, which, cols, keep_ref=None):
    parts = [
        ref[which, :, cols] if keep_ref is None else ref[which, :, cols] * keep_ref[k].astype(BF16) for k, ref in group
    ]
    return parts[0] if len(parts) == 1 else jnp.concatenate(parts, 0)


def gram_kernel(core_ref, keep_ref, *refs):
    pieces, (out_ref, token_ref, tmp_ref) = pieces_of(refs[:6]), refs[6:]
    token_ref[...] = jnp.zeros_like(token_ref)
    nb = refs[0].shape[2] // B
    start = pl.multiple_of(core_ref[0] * HALF, HALF)
    for i in range(nb):
        wide = (i + 1) * B
        acc = None
        for group in pieces:
            p = dot(columns_of(group, 0, slice(i * B, wide), keep_ref), columns_of(group, 0, slice(0, wide)), TN)
            acc = p if acc is None else acc + p
        tmp_ref[:, :wide] = acc
        for j in range(i + 1):
            t = tri(i, j)
            out_ref[t * HALF : (t + 1) * HALF, :] = tmp_ref[pl.ds(start, HALF), j * B : (j + 1) * B]
    used = tri(nb, 0) * HALF
    out_ref[used:, :] = jnp.zeros((out_ref.shape[0] - used, B), F32)


def gram(core, keeps, pieces, slots):
    width = pieces[0].shape[2]
    return pl.pallas_call(
        gram_kernel,
        out_shape=(jax.ShapeDtypeStruct((slots * SLAB, B), F32), TOKEN),
        in_specs=[SM, SM] + [VM] * 6,
        out_specs=(VM, VM),
        scratch_shapes=[pltpu.VMEM((B, width), F32)],
        compiler_params=params(12),
        cost_estimate=cost(4),
        name="gram",
    )(core, keeps, *pieces)


def cross_kernel(core_ref, grp_ref, keep_ref, after_ref, *refs):
    pieces, (out_ref, token_ref, tmp_ref) = pieces_of(refs[:6]), refs[6:]
    token_ref[...] = jnp.zeros_like(token_ref)
    n = refs[0].shape[2]
    wide = out_ref.shape[2]
    grp = grp_ref[0]
    cols = pl.ds(pl.multiple_of(grp * (n - wide), B), wide)
    for i in range(n // B):
        acc = None
        for group in pieces:
            p = dot(columns_of(group, 1 - grp, slice(i * B, (i + 1) * B), keep_ref), columns_of(group, grp, cols), TN)
            acc = p if acc is None else acc + p
        tmp_ref[i * B : (i + 1) * B, :] = acc
    tmp_ref[n:, :] = jnp.zeros((tmp_ref.shape[0] - n, wide), F32)
    for q in range(out_ref.shape[0]):
        out_ref[q] = tmp_ref[pl.ds(pl.multiple_of((2 * q + core_ref[0]) * ROWS, 8), ROWS), :]


def cross(core, grp, keeps, after, pieces, chips, wide):
    return pl.pallas_call(
        cross_kernel,
        out_shape=(jax.ShapeDtypeStruct((chips, ROWS, wide), F32), TOKEN),
        in_specs=[SM, SM, SM, ANY] + [VM] * 6,
        out_specs=(VM, VM),
        scratch_shapes=[pltpu.VMEM((2 * chips * ROWS, wide), F32)],
        compiler_params=params(14),
        cost_estimate=cost(7),
        name="cross",
    )(core, grp, keeps, after, *pieces)


def factor_diag(block):
    a = [block[8 * i : 8 * i + 8, :] for i in range(16)]
    lane = lax.broadcasted_iota(jnp.int32, (8, B), 1)
    sub = lax.broadcasted_iota(jnp.int32, (8, B), 0)
    x = [(lane == sub + 8 * g).astype(F32) for g in range(16)]
    inv, inv_r = [], []
    cg = [col(a[0], t) for t in range(8)]
    for g in range(16):
        here = (lane >= 8 * g) & (lane < 8 * g + 8)
        v = jnp.where(here, (lane == sub + 8 * g).astype(F32), a[g])
        xg = x[g]
        if g < 15:
            near = a[g + 1]
            cr = [col(near, 8 * g + t) for t in range(8)]
            nxt = [col(near, 8 * g + 8 + t) for t in range(8)]
            near, xr = jnp.where(here, 0.0, near), x[g + 1]
        rs, vs, xs, css = [], [], [], []
        for t in range(8):
            p = row(cg[t], t)
            r = lax.rsqrt(p)
            lt = jnp.where(sub > t, cg[t] * r, 0.0)
            vn = row(v, t) * r
            v = jnp.where(sub == t, vn, v - lt * vn)
            xn = row(xg, t) / rounded(p * r)
            xg = jnp.where(sub == t, xn, xg - rounded(lt) * xn)
            cs = {s: row(cg[s], t) * r for s in range(t + 1, 8)}
            for s in range(t + 1, 8):
                cg[s] = cg[s] - lt * cs[s]
            rs.append(r)
            vs.append(vn)
            xs.append(xn)
            css.append(cs)
            if g < 15:
                lr = cr[t] * r
                for s in range(8):
                    nxt[s] = nxt[s] - lr * row(lr, s)
                near = near - lr * vn
                xr = xr - rounded(lr) * xn
                for s in range(t + 1, 8):
                    cr[s] = cr[s] - lr * cs[s]
        inv.append(jnp.where(lane <= sub + 8 * g, v, 0.0))
        inv_r.append(xg)
        if g < 15:
            a[g + 1], x[g + 1] = near, xr
            cg = nxt
        for i in range(g + 2, 16):
            c = [col(a[i], 8 * g + t) for t in range(8)]
            ai, xi = jnp.where(here, 0.0, a[i]), x[i]
            for t in range(8):
                l = c[t] * rs[t]
                ai = ai - l * vs[t]
                xi = xi - rounded(l) * xs[t]
                for s in range(t + 1, 8):
                    c[s] = c[s] - l * css[t][s]
            a[i], x[i] = ai, xi
    return jnp.concatenate(inv, 0), jnp.concatenate(inv_r, 0)


def block_of(mine_ref, other_ref, first, i, j):
    t = tri(i, j) * HALF
    mine = mine_ref[t : t + HALF, :].astype(F32)
    other = other_ref[t : t + HALF, :].astype(F32)
    return jnp.concatenate([jnp.where(first, mine, other), jnp.where(first, other, mine)], 0)


def chol_kernel(core_ref, mine_ref, other_ref, low_ref, inv_ref, lo_ref, s_ref, w_ref):
    n = low_ref.shape[0]
    nb = n // B
    first = core_ref[0] == 0

    def update(kk):
        r0 = kk * B
        s = jnp.concatenate([block_of(mine_ref, other_ref, first, i, kk) for i in range(kk, nb)], 0)
        if kk:
            wts = jnp.concatenate([low_ref[r0 : r0 + B, :r0], lo_ref[r0 : r0 + B, :r0]], 0)
            pr = dot(low_ref[r0:, :r0], wts)
            s = s - (pr[:, :B] + pr[:, B:] + dot(lo_ref[r0:, :r0], low_ref[r0 : r0 + B, :r0]))
        s_ref[r0:, :] = s

    def panel(kk):
        r0 = kk * B
        r1 = r0 + B
        shi, slo = split(s_ref[r1:, :])
        pr = dot(shi, w_ref[...])
        lp = pr[:, :B] + pr[:, B:] + dot(slo, w_ref[:B, :])
        hi, lo = split(lp)
        low_ref[r1:, r0:r1] = hi
        lo_ref[r1:, r0:r1] = lo

    def step(k, _):
        for kk in range(nb):
            pl.when(k == kk)(lambda kk=kk: update(kk))
        r0 = pl.multiple_of(k * B, B)
        linv, lrinv = factor_diag(s_ref[pl.ds(r0, B), :])
        inv_ref[pl.ds(r0, B), :] = lrinv
        hi, lo = split(linv)
        w_ref[:B, :] = hi
        w_ref[B:, :] = lo
        for kk in range(nb - 1):
            pl.when(k == kk)(lambda kk=kk: panel(kk))
        return 0

    lax.fori_loop(0, nb, step, 0)


def chol(core, mine, other, n):
    return pl.pallas_call(
        chol_kernel,
        out_shape=(jax.ShapeDtypeStruct((n, n), BF16), jax.ShapeDtypeStruct((n, B), F32)),
        in_specs=[SM, VM, VM],
        out_specs=(VM, VM),
        scratch_shapes=[
            pltpu.VMEM((n, n), BF16),
            pltpu.VMEM((n, B), F32),
            pltpu.VMEM((2 * B, B), BF16),
        ],
        compiler_params=params(14),
        cost_estimate=cost(57),
        name="cholesky",
    )(core, mine, other)


def solve_into(rhs, m, low_ref, inv_ref, out_ref):
    nb = low_ref.shape[0] // B

    def stacked(x):
        return jnp.concatenate(split(x), 0)

    def fold(p):
        return p[:m] + p[m:]

    acc = [rhs(b) for b in range(nb)]
    for b in range(nb):
        r0, r1 = b * B, (b + 1) * B
        w = stacked(inv_ref[r0:r1, :])
        p = fold(dot(stacked(acc[b]), w))
        y = p[:, :B] + p[:, B:]
        acc[b] = y
        ys = stacked(y)
        for c in range(b + 1, nb):
            acc[c] = acc[c] - fold(dot(ys, low_ref[c * B : (c + 1) * B, r0:r1]))
    for b in reversed(range(nb)):
        r0, r1 = b * B, (b + 1) * B
        w = jnp.concatenate(split(inv_ref[r0:r1, :]), 1)
        p = fold(dot(stacked(acc[b]), w, NN))
        z = p[:, :B] + p[:, B:]
        out_ref[:, r0:r1] = z
        zs = stacked(z)
        for c in range(b):
            acc[c] = acc[c] - fold(dot(zs, low_ref[r0:r1, c * B : (c + 1) * B], NN))


def solve_kernel(rhs_ref, low_ref, inv_ref, after_ref, out_ref):
    solve_into(lambda b: rhs_ref[:, b * B : (b + 1) * B], rhs_ref.shape[0], low_ref, inv_ref, out_ref)


def solve(rhs, low, inv, after):
    return pl.pallas_call(
        solve_kernel,
        out_shape=jax.ShapeDtypeStruct(rhs.shape, F32),
        in_specs=[VM] * 3 + [ANY],
        out_specs=VM,
        compiler_params=params(8),
        cost_estimate=cost(7),
        name="solve",
    )(rhs, low, inv, after)


def route_kernel(block, owner_ref, first_ref, last_ref, low_ref, inv_ref, out_ref, t_ref, r_ref):
    n = low_ref.shape[0]
    m, wide = first_ref.shape

    def rhs(b):
        at = b * B
        return first_ref[:, at : at + B] if at < wide else last_ref[:, at - (n - wide) : at - (n - wide) + B]

    solve_into(rhs, m, low_ref, inv_ref, t_ref)
    t_ref[:, n:] = jnp.zeros((m, t_ref.shape[1] - n), F32)
    lane = lax.broadcasted_iota(jnp.int32, (m, 2 * B), 1)
    for h in range(2):
        for q in range(owner_ref.shape[1]):
            to, off = block * q // B * B, block * q % B
            src = owner_ref[h, q] * block
            win = t_ref[:, pl.ds(pl.multiple_of(src // B * B, B), 2 * B)]
            win = pltpu.roll(win, (off + 2 * B - src % B) % (2 * B), 1)
            old = r_ref[h, :, to : to + 2 * B]
            r_ref[h, :, to : to + 2 * B] = jnp.where((lane >= off) & (lane < off + block), win, old)
        out_ref[h] = r_ref[h, :, : out_ref.shape[2]]


def solve_and_route(owner, first, last, low, inv, block):
    m, n = first.shape[0], low.shape[0]
    wide = -(-owner.shape[1] * block // B) * B
    return pl.pallas_call(
        functools.partial(route_kernel, block),
        out_shape=jax.ShapeDtypeStruct((2, m, wide), F32),
        in_specs=[SM] + [VM] * 4,
        out_specs=VM,
        scratch_shapes=[pltpu.VMEM((m, n + B), F32), pltpu.VMEM((2, m, wide + B), F32)],
        compiler_params=params(8),
        cost_estimate=cost(9),
        name="solve_and_route",
    )(owner, first, last, low, inv)


def sum_kernel(parts_ref, after_ref, out_ref):
    acc = parts_ref[0]
    for k in range(1, parts_ref.shape[0]):
        acc = acc + parts_ref[k]
    out_ref[...] = acc


def sum_parts(parts, after):
    return pl.pallas_call(
        sum_kernel,
        out_shape=jax.ShapeDtypeStruct(parts.shape[1:], F32),
        in_specs=[VM, ANY],
        out_specs=VM,
        compiler_params=params(8),
        cost_estimate=cost(3),
        name="sum_parts",
    )(parts, after)


def rows_kernel(at_ref, core_ref, mine_ref, other_ref, diag_ref, out_ref, s_ref):
    m, n = out_ref.shape
    nb = n // B
    first = core_ref[0] == 0
    for i in range(nb):
        for j in range(i + 1):
            blk = block_of(mine_ref, other_ref, first, i, j)
            s_ref[i * B : (i + 1) * B, j * B : (j + 1) * B] = blk
            if i > j:
                s_ref[j * B : (j + 1) * B, i * B : (i + 1) * B] = blk.T
    at = at_ref[0]
    window = s_ref[pl.ds(pl.multiple_of(at // 8 * 8, 8), 32), :]
    shift = at % 8
    out = window[:m]
    for k in range(1, 8):
        out = jnp.where(shift == k, window[k : k + m], out)
    ri = lax.broadcasted_iota(jnp.int32, (m, n), 0)
    ci = lax.broadcasted_iota(jnp.int32, (m, n), 1)
    out_ref[...] = jnp.where(ci == ri + at, diag_ref[...], out)


def rows_of(at, core, mine, other, diag, n, m):
    return pl.pallas_call(
        rows_kernel,
        out_shape=jax.ShapeDtypeStruct((m, n), F32),
        in_specs=[SM, SM, VM, VM, VM],
        out_specs=VM,
        scratch_shapes=[pltpu.VMEM((n + 8, n), F32)],
        compiler_params=params(12),
        cost_estimate=cost(3),
        name="rows",
    )(at, core, mine, other, diag)


def per_device(attn_out, out_grad, image_counts, column_owner, damping):
    n_dp = lax.axis_size("dp")
    dp_index = lax.axis_index("dp")
    grp_index = lax.axis_index("grp")
    per_dev, width = attn_out.shape
    block = width // n_dp
    chips = n_dp // 2
    core = dp_index % 2
    chip = dp_index // 2
    nb = width // B
    used = tri(nb, 0) * HALF // SLAB
    per_chip = -(-used // chips)
    same_core = [list(range(c, n_dp, 2)) for c in range(2)]
    swap_core = [(d, d ^ 1) for d in range(n_dp)]
    swap_grp = [(0, 1), (1, 0)]
    core_arr = core.astype(jnp.int32)[None]
    is_a = grp_index == 0

    def keep_of(grp, dp):
        return (lax.dynamic_index_in_dim(image_counts, grp * n_dp + dp, 0, keepdims=False) > 0).astype(F32)

    flip = n_dp // 2
    near = [(g * n_dp + d, (1 - g) * n_dp + d) for g in range(2) for d in range(n_dp)]
    far = [(g * n_dp + d, (1 - g) * n_dp + d ^ flip) for g in range(2) for d in range(n_dp)]
    both = ("grp", "dp")
    half = per_dev // 2

    own = jnp.stack([jnp.where(is_a, attn_out, out_grad), jnp.where(is_a, out_grad, attn_out)])
    from_near = lax.ppermute(own[::-1, :half], both, near)
    from_far = lax.ppermute(own[::-1, half:], both, far)
    pieces = [own, lax.ppermute(own, "dp", swap_core), from_near, from_far]
    pieces += [lax.ppermute(from_near, "dp", swap_core), lax.ppermute(from_far, "dp", swap_core)]
    over, mate, away = 1 - grp_index, dp_index ^ 1, dp_index ^ flip
    keeps = jnp.stack([
        keep_of(grp_index, dp_index),
        keep_of(grp_index, mate),
        keep_of(over, dp_index),
        keep_of(over, away),
        keep_of(over, mate),
        keep_of(over, away ^ 1),
    ])
    total = (TOK * jnp.sum(image_counts)).astype(F32)
    part, gram_done = gram(core_arr, keeps, pieces, chips * per_chip)
    got = lax.all_to_all(
        part.reshape(chips, per_chip * SLAB, B), "dp", split_axis=0, concat_axis=0, tiled=True, axis_index_groups=same_core
    )

    wide = (nb + 2) // 2 * B
    part_w, cross_done = cross(core_arr, grp_index.astype(jnp.int32)[None], keeps, gram_done, pieces, chips, wide)

    slabs = sum_parts(got, cross_done) / total

    flat = chip * (per_chip * SLAB) + jnp.arange(per_chip * SLAB)
    t = flat // HALF
    on_diag = jnp.zeros(t.shape, bool)
    for i in range(nb):
        on_diag = on_diag | (t == tri(i, i))
    in_row = core * HALF + flat % HALF
    diag = (on_diag & (flat < used * SLAB))[:, None] & (in_row[:, None] == jnp.arange(B)[None, :])
    damp = jnp.where(is_a, damping[0], damping[1])
    damped = (slabs + damp * diag.astype(F32)).astype(BF16)
    spread = jnp.broadcast_to(damped[None], (chips,) + damped.shape)
    mine = lax.all_to_all(spread, "dp", split_axis=0, concat_axis=0, tiled=True, axis_index_groups=same_core)
    mine = mine.reshape(chips * per_chip * SLAB, B)
    theirs = lax.ppermute(mine, "dp", swap_core)
    low, inv = chol(core_arr, mine, theirs, width)

    got_w = lax.all_to_all(part_w, "dp", split_axis=0, concat_axis=0, tiled=True, axis_index_groups=same_core)

    pad = 256 - per_chip * SLAB
    diags = jnp.pad(jnp.sum(slabs * diag.astype(F32), axis=1), (0, pad)).reshape(2, B)
    diags = lax.all_gather(diags, "dp", axis=0, tiled=False).reshape(chips, 2, 256)[:, :, : per_chip * SLAB]
    diags = diags.transpose(1, 0, 2).reshape(2, -1)
    my_diag = jnp.concatenate([diags[c, tri(i, i) * HALF : tri(i, i) * HALF + HALF] for i in range(nb) for c in range(2)])[None]
    at = (dp_index * block).astype(jnp.int32)[None]
    my_rows = rows_of(at, core_arr, mine, theirs, my_diag, width, ROWS)[:block]
    their_rows = lax.ppermute(my_rows, "grp", swap_grp)
    factors = jnp.stack([jnp.where(is_a, my_rows, their_rows), jnp.where(is_a, their_rows, my_rows)])

    order = column_owner.reshape(chips, 2)
    order = jnp.stack([jnp.where(core == 0, order[:, 0], order[:, 1]), jnp.where(core == 0, order[:, 1], order[:, 0])])
    my_w = sum_parts(got_w, inv) / total
    last_w = lax.ppermute(my_w, "grp", [(1, 0)])
    routed = solve_and_route(order, my_w, last_w, low, inv, block)
    same = lax.ppermute(routed[0], both, [(d, n_dp + d) for d in range(n_dp)])
    cross_t = lax.ppermute(routed[1], both, [(d, n_dp + (d ^ 1)) for d in range(n_dp)])
    is_first = core == 0
    pair = jnp.concatenate([jnp.where(is_first, same, cross_t), jnp.where(is_first, cross_t, same)])
    pair = pair[:, : chips * block].reshape(2 * ROWS, chips, block).transpose(1, 2, 0)
    columns = lax.all_to_all(pair, "dp", split_axis=0, concat_axis=0, tiled=True, axis_index_groups=same_core)
    columns = columns.transpose(1, 0, 2).reshape(block, n_dp * ROWS)[:, :width]
    columns = jnp.pad(columns, ((0, ROWS - block), (0, 0)))
    left = solve(columns, low, inv, my_rows)[:block]
    back = lax.ppermute(left, "grp", [(1, 0)])
    preconditioned = jnp.where(is_a, back, left).T
    return (factors, preconditioned)


def solution(mesh):
    placed = (P(("grp", "dp"), None), P(("grp", "dp"), None), P(), P(), P())
    return jax.shard_map(
        per_device,
        mesh=mesh,
        in_specs=placed,
        out_specs=(P(None, "dp", None), P(None, "dp")),
        check_vma=False,
    )
```

```python
import functools

import jax
import jax.numpy as jnp
from jax import lax
from jax.experimental import pallas as pl
from jax.experimental.pallas import tpu as pltpu
from jax.sharding import PartitionSpec as P

TOK = 256
B = 128
HALF = 64
SLAB = 16
ROWS = 24
F32 = jnp.float32
BF16 = jnp.bfloat16
NT = (((1,), (1,)), ((), ()))
NN = (((1,), (0,)), ((), ()))
TN = (((0,), (0,)), ((), ()))
VM = pl.BlockSpec(memory_space=pltpu.VMEM)
ANY = pl.BlockSpec(memory_space=pl.ANY)
HBM = pl.BlockSpec(memory_space=pltpu.HBM)
SM = pl.BlockSpec(memory_space=pltpu.SMEM)
TOKEN = jax.ShapeDtypeStruct((8, B), F32)
MIB = 1024 * 1024


def params(mib):
    return pltpu.CompilerParams(vmem_limit_bytes=mib * MIB)


def cost(micros):
    return pl.CostEstimate(flops=int(micros * 1.1e9), bytes_accessed=MIB, transcendentals=0)


def dot(a, b, dims=NT):
    return lax.dot_general(a, b, dims, preferred_element_type=F32)


def split(x):
    hi = x.astype(BF16)
    return hi, (x - hi.astype(F32)).astype(BF16)


def row(x, t):
    return jnp.broadcast_to(x[..., t : t + 1, :], x.shape)


def col(x, c):
    return jnp.broadcast_to(x[..., c : c + 1], x.shape)


def rounded(x):
    return x.astype(BF16).astype(F32)


def tri(i, j):
    return i * (i + 1) // 2 + j


def pieces_of(refs):
    own, mate, near, far, near_mate, far_mate = refs
    return [[(0, own)], [(1, mate)], [(2, near), (3, far)], [(4, near_mate), (5, far_mate)]]


def columns_of(group, cols, keep_ref=None):
    parts = [ref[:, cols] if keep_ref is None else ref[:, cols] * keep_ref[k].astype(BF16) for k, ref in group]
    return parts[0] if len(parts) == 1 else jnp.concatenate(parts, 0)


def gram_kernel(core_ref, keep_ref, *refs):
    pieces, (hbm_ref, squares_ref, out_ref, tmp_ref, sem) = pieces_of(refs[:6]), refs[6:]
    nb = refs[0].shape[1] // B
    start = pl.multiple_of(core_ref[0] * HALF, HALF)
    on = lax.broadcasted_iota(jnp.int32, (B, B), 0) == lax.broadcasted_iota(jnp.int32, (B, B), 1)
    copies = []

    def send(lo, hi):
        copies.append(pltpu.make_async_copy(out_ref.at[lo:hi], hbm_ref.at[lo:hi], sem.at[len(copies)]))
        copies[-1].start()

    used = tri(nb, 0) * HALF
    out_ref[used:, :] = jnp.zeros((out_ref.shape[0] - used, B), F32)
    send(used, out_ref.shape[0])
    for i in range(nb):
        wide = (i + 1) * B
        acc = None
        for group in pieces:
            p = dot(columns_of(group, slice(i * B, wide), keep_ref), columns_of(group, slice(0, wide)), TN)
            acc = p if acc is None else acc + p
        tmp_ref[:, :wide] = acc
        diag = jnp.sum(jnp.where(on, acc[:, i * B :], 0.0), axis=0, keepdims=True)
        squares_ref[:, i * B : wide] = jnp.broadcast_to(diag, (8, B))
        for j in range(i + 1):
            t = tri(i, j)
            out_ref[t * HALF : (t + 1) * HALF, :] = tmp_ref[pl.ds(start, HALF), j * B : (j + 1) * B]
        send(tri(i, 0) * HALF, tri(i + 1, 0) * HALF)
    for copy in copies:
        copy.wait()


def gram(core, keeps, pieces, slots):
    width = pieces[0].shape[1]
    return pl.pallas_call(
        gram_kernel,
        out_shape=(jax.ShapeDtypeStruct((slots * SLAB, B), F32), jax.ShapeDtypeStruct((8, width), F32)),
        in_specs=[SM, SM] + [VM] * 6,
        out_specs=(HBM, VM),
        scratch_shapes=[
            pltpu.VMEM((slots * SLAB, B), F32),
            pltpu.VMEM((B, width), F32),
            pltpu.SemaphoreType.DMA((width // B + 1,)),
        ],
        compiler_params=params(56),
        cost_estimate=cost(4),
        name="gram",
    )(core, keeps, *pieces)


def cross_kernel(core_ref, grp_ref, keep_ref, after_ref, *refs):
    mine, other, (out_ref, tmp_ref) = pieces_of(refs[:6]), pieces_of(refs[6:12]), refs[12:]
    n = refs[0].shape[1]
    wide = out_ref.shape[2]

    def run(left, right, first):
        for i in range(n // B):
            acc = None
            for lg, rg in zip(left, right):
                p = dot(columns_of(lg, slice(i * B, (i + 1) * B), keep_ref), columns_of(rg, slice(first, first + wide)), TN)
                acc = p if acc is None else acc + p
            tmp_ref[i * B : (i + 1) * B, :] = acc

    pl.when(grp_ref[0] == 0)(lambda: run(other, mine, 0))
    pl.when(grp_ref[0] == 1)(lambda: run(mine, other, n - wide))
    tmp_ref[n:, :] = jnp.zeros((tmp_ref.shape[0] - n, wide), F32)
    for q in range(out_ref.shape[0]):
        out_ref[q] = tmp_ref[pl.ds(pl.multiple_of((2 * q + core_ref[0]) * ROWS, 8), ROWS), :]


def cross(core, grp, keeps, after, mine, other, chips, wide):
    return pl.pallas_call(
        cross_kernel,
        out_shape=jax.ShapeDtypeStruct((chips, ROWS, wide), F32),
        in_specs=[SM, SM, SM, ANY] + [VM] * 12,
        out_specs=VM,
        scratch_shapes=[pltpu.VMEM((2 * chips * ROWS, wide), F32)],
        compiler_params=params(56),
        cost_estimate=cost(30),
        name="cross",
    )(core, grp, keeps, after, *mine, *other)


def factor_diag(block):
    a = [block[8 * i : 8 * i + 8, :] for i in range(16)]
    lane = lax.broadcasted_iota(jnp.int32, (8, B), 1)
    sub = lax.broadcasted_iota(jnp.int32, (8, B), 0)
    x = [(lane == sub + 8 * g).astype(F32) for g in range(16)]
    inv, inv_r = [], []
    cg = [col(a[0], t) for t in range(8)]
    for g in range(16):
        here = (lane >= 8 * g) & (lane < 8 * g + 8)
        v = jnp.where(here, (lane == sub + 8 * g).astype(F32), a[g])
        xg = x[g]
        if g < 15:
            near = a[g + 1]
            cr = [col(near, 8 * g + t) for t in range(8)]
            nxt = [col(near, 8 * g + 8 + t) for t in range(8)]
            near, xr = jnp.where(here, 0.0, near), x[g + 1]
        rs, vs, xs, css = [], [], [], []
        for t in range(8):
            p = row(cg[t], t)
            r = lax.rsqrt(p)
            lt = jnp.where(sub > t, cg[t] * r, 0.0)
            vn = row(v, t) * r
            v = jnp.where(sub == t, vn, v - lt * vn)
            xn = row(xg, t) / rounded(p * r)
            xg = jnp.where(sub == t, xn, xg - rounded(lt) * xn)
            cs = {s: row(cg[s], t) * r for s in range(t + 1, 8)}
            for s in range(t + 1, 8):
                cg[s] = cg[s] - lt * cs[s]
            rs.append(r)
            vs.append(vn)
            xs.append(xn)
            css.append(cs)
            if g < 15:
                lr = cr[t] * r
                for s in range(8):
                    nxt[s] = nxt[s] - lr * row(lr, s)
                near = near - lr * vn
                xr = xr - rounded(lr) * xn
                for s in range(t + 1, 8):
                    cr[s] = cr[s] - lr * cs[s]
        inv.append(jnp.where(lane <= sub + 8 * g, v, 0.0))
        inv_r.append(xg)
        if g < 15:
            a[g + 1], x[g + 1] = near, xr
            cg = nxt
        for i in range(g + 2, 16):
            c = [col(a[i], 8 * g + t) for t in range(8)]
            ai, xi = jnp.where(here, 0.0, a[i]), x[i]
            for t in range(8):
                l = c[t] * rs[t]
                ai = ai - l * vs[t]
                xi = xi - rounded(l) * xs[t]
                for s in range(t + 1, 8):
                    c[s] = c[s] - l * css[t][s]
            a[i], x[i] = ai, xi
    return jnp.concatenate(inv, 0), jnp.concatenate(inv_r, 0)


def block_of(mine_ref, other_ref, first, i, j):
    t = tri(i, j) * HALF
    mine = mine_ref[t : t + HALF, :].astype(F32)
    other = other_ref[t : t + HALF, :].astype(F32)
    return jnp.concatenate([jnp.where(first, mine, other), jnp.where(first, other, mine)], 0)


def chol_kernel(core_ref, mine_ref, other_ref, low_hbm, inv_hbm, done_ref, low_ref, inv_ref, lo_ref, s_ref, w_ref, sem):
    done_ref[...] = jnp.zeros_like(done_ref)
    n = low_ref.shape[0]
    nb = n // B
    first = core_ref[0] == 0

    def update(kk):
        r0 = kk * B
        s = jnp.concatenate([block_of(mine_ref, other_ref, first, i, kk) for i in range(kk, nb)], 0)
        if kk:
            wts = jnp.concatenate([low_ref[r0 : r0 + B, :r0], lo_ref[r0 : r0 + B, :r0]], 0)
            pr = dot(low_ref[r0:, :r0], wts)
            s = s - (pr[:, :B] + pr[:, B:] + dot(lo_ref[r0:, :r0], low_ref[r0 : r0 + B, :r0]))
        s_ref[r0:, :] = s

    def panel(kk):
        r0 = kk * B
        r1 = r0 + B
        shi, slo = split(s_ref[r1:, :])
        pr = dot(shi, w_ref[...])
        lp = pr[:, :B] + pr[:, B:] + dot(slo, w_ref[:B, :])
        hi, lo = split(lp)
        low_ref[r1:, r0:r1] = hi
        lo_ref[r1:, r0:r1] = lo

    def step(k, _):
        for kk in range(nb):
            pl.when(k == kk)(lambda kk=kk: update(kk))
        r0 = pl.multiple_of(k * B, B)
        rows = pl.ds(r0, B)
        pltpu.make_async_copy(low_ref.at[rows], low_hbm.at[rows], sem.at[0, k]).start()
        linv, lrinv = factor_diag(s_ref[pl.ds(r0, B), :])
        inv_ref[rows, :] = lrinv
        pltpu.make_async_copy(inv_ref.at[rows], inv_hbm.at[rows], sem.at[1, k]).start()
        hi, lo = split(linv)
        w_ref[:B, :] = hi
        w_ref[B:, :] = lo
        for kk in range(nb - 1):
            pl.when(k == kk)(lambda kk=kk: panel(kk))
        return 0

    lax.fori_loop(0, nb, step, 0)
    for k in range(nb):
        rows = slice(k * B, (k + 1) * B)
        pltpu.make_async_copy(low_ref.at[rows], low_hbm.at[rows], sem.at[0, k]).wait()
        pltpu.make_async_copy(inv_ref.at[rows], inv_hbm.at[rows], sem.at[1, k]).wait()


def chol(core, mine, other, n):
    return pl.pallas_call(
        chol_kernel,
        out_shape=(jax.ShapeDtypeStruct((n, n), BF16), jax.ShapeDtypeStruct((n, B), F32), TOKEN),
        in_specs=[SM, VM, VM],
        out_specs=(HBM, HBM, VM),
        scratch_shapes=[
            pltpu.VMEM((n, n), BF16),
            pltpu.VMEM((n, B), F32),
            pltpu.VMEM((n, n), BF16),
            pltpu.VMEM((n, B), F32),
            pltpu.VMEM((2 * B, B), BF16),
            pltpu.SemaphoreType.DMA((2, n // B)),
        ],
        compiler_params=params(56),
        cost_estimate=cost(57),
        name="cholesky",
    )(core, mine, other)


def solve_into(rhs, m, low_hbm, inv_hbm, out_ref, low_ref, inv_ref, sem):
    nb = low_ref.shape[0] // B
    copies = [pltpu.make_async_copy(inv_hbm, inv_ref, sem.at[0])]
    for b in range(1, nb):
        part = (slice(b * B, (b + 1) * B), slice(0, b * B))
        copies.append(pltpu.make_async_copy(low_hbm.at[part], low_ref.at[part], sem.at[b]))
    for copy in copies:
        copy.start()

    def stacked(x):
        return jnp.concatenate(split(x), 0)

    def fold(p):
        return p[:m] + p[m:]

    acc, ys = [], []
    for b in range(nb):
        r0, r1 = b * B, (b + 1) * B
        copies[b].wait()
        s = rhs(b)
        if b > 1:
            s = s - fold(dot(jnp.concatenate(ys[:-1], 1), low_ref[r0:r1, : r0 - B]))
        if b:
            s = s - fold(dot(ys[-1], low_ref[r0:r1, r0 - B : r0]))
        p = fold(dot(stacked(s), stacked(inv_ref[r0:r1, :])))
        y = p[:, :B] + p[:, B:]
        acc.append(y)
        ys.append(stacked(y))
    for b in reversed(range(nb)):
        r0, r1 = b * B, (b + 1) * B
        w = jnp.concatenate(split(inv_ref[r0:r1, :]), 1)
        p = fold(dot(stacked(acc[b]), w, NN))
        z = p[:, :B] + p[:, B:]
        out_ref[:, r0:r1] = z
        zs = stacked(z)
        for c in range(b):
            acc[c] = acc[c] - fold(dot(zs, low_ref[r0:r1, c * B : (c + 1) * B], NN))


def solve_scratch(n):
    return [pltpu.VMEM((n, n), BF16), pltpu.VMEM((n, B), F32), pltpu.SemaphoreType.DMA((n // B,))]


def solve_kernel(rhs_ref, low_ref, inv_ref, after_ref, out_ref, *scratch):
    solve_into(lambda b: rhs_ref[:, b * B : (b + 1) * B], rhs_ref.shape[0], low_ref, inv_ref, out_ref, *scratch)


def solve(rhs, low, inv, after):
    return pl.pallas_call(
        solve_kernel,
        out_shape=jax.ShapeDtypeStruct(rhs.shape, F32),
        in_specs=[VM, HBM, HBM, ANY],
        out_specs=VM,
        scratch_shapes=solve_scratch(low.shape[0]),
        compiler_params=params(56),
        cost_estimate=cost(7),
        name="solve",
    )(rhs, low, inv, after)


def route_kernel(block, owner_ref, first_ref, last_ref, low_ref, inv_ref, out_ref, t_ref, r_ref, *scratch):
    n = low_ref.shape[0]
    m, wide = first_ref.shape

    def rhs(b):
        at = b * B
        return first_ref[:, at : at + B] if at < wide else last_ref[:, at - (n - wide) : at - (n - wide) + B]

    solve_into(rhs, m, low_ref, inv_ref, t_ref, *scratch)
    t_ref[:, n:] = jnp.zeros((m, t_ref.shape[1] - n), F32)
    lane = lax.broadcasted_iota(jnp.int32, (m, 2 * B), 1)
    for h in range(2):
        for q in range(owner_ref.shape[1]):
            to, off = block * q // B * B, block * q % B
            src = owner_ref[h, q] * block
            win = t_ref[:, pl.ds(pl.multiple_of(src // B * B, B), 2 * B)]
            win = pltpu.roll(win, (off + 2 * B - src % B) % (2 * B), 1)
            old = r_ref[h, :, to : to + 2 * B]
            r_ref[h, :, to : to + 2 * B] = jnp.where((lane >= off) & (lane < off + block), win, old)
        out_ref[h] = r_ref[h, :, : out_ref.shape[2]]


def solve_and_route(owner, first, last, low, inv, block):
    m, n = first.shape[0], low.shape[0]
    wide = -(-owner.shape[1] * block // B) * B
    return pl.pallas_call(
        functools.partial(route_kernel, block),
        out_shape=jax.ShapeDtypeStruct((2, m, wide), F32),
        in_specs=[SM, VM, VM, HBM, HBM],
        out_specs=VM,
        scratch_shapes=[pltpu.VMEM((m, n + B), F32), pltpu.VMEM((2, m, wide + B), F32)] + solve_scratch(n),
        compiler_params=params(56),
        cost_estimate=cost(9),
        name="solve_and_route",
    )(owner, first, last, low, inv)


def sum_kernel(parts_ref, *refs):
    out_ref = refs[-1]
    acc = parts_ref[0]
    for k in range(1, parts_ref.shape[0]):
        acc = acc + parts_ref[k]
    out_ref[...] = acc


def sum_parts(parts, *after):
    return pl.pallas_call(
        sum_kernel,
        out_shape=jax.ShapeDtypeStruct(parts.shape[1:], F32),
        in_specs=[VM] + [ANY] * len(after),
        out_specs=VM,
        compiler_params=params(24),
        cost_estimate=cost(3),
        name="sum_parts",
    )(parts, *after)


def rows_kernel(at_ref, core_ref, mine_ref, other_ref, out_ref, s_ref):
    m, n = out_ref.shape
    nb = n // B
    first = core_ref[0] == 0
    for i in range(nb):
        for j in range(i + 1):
            blk = block_of(mine_ref, other_ref, first, i, j)
            s_ref[i * B : (i + 1) * B, j * B : (j + 1) * B] = blk
            if i > j:
                s_ref[j * B : (j + 1) * B, i * B : (i + 1) * B] = blk.T
    at = at_ref[0]
    window = s_ref[pl.ds(pl.multiple_of(at // 8 * 8, 8), 32), :]
    shift = at % 8
    out = window[:m]
    for k in range(1, 8):
        out = jnp.where(shift == k, window[k : k + m], out)
    out_ref[...] = out


def rows_of(at, core, mine, other, n, m):
    return pl.pallas_call(
        rows_kernel,
        out_shape=jax.ShapeDtypeStruct((m, n), F32),
        in_specs=[SM, SM, VM, VM],
        out_specs=VM,
        scratch_shapes=[pltpu.VMEM((n + 8, n), F32)],
        compiler_params=params(40),
        cost_estimate=cost(3),
        name="rows",
    )(at, core, mine, other)


def per_device(attn_out, out_grad, image_counts, column_owner, damping):
    n_dp = lax.axis_size("dp")
    dp_index = lax.axis_index("dp")
    grp_index = lax.axis_index("grp")
    per_dev, width = attn_out.shape
    block = width // n_dp
    chips = n_dp // 2
    core = dp_index % 2
    chip = dp_index // 2
    nb = width // B
    used = tri(nb, 0) * HALF // SLAB
    per_chip = -(-used // chips)
    same_core = [list(range(c, n_dp, 2)) for c in range(2)]
    swap_core = [(d, d ^ 1) for d in range(n_dp)]
    swap_grp = [(0, 1), (1, 0)]
    core_arr = core.astype(jnp.int32)[None]
    is_a = grp_index == 0

    def keep_of(grp, dp):
        return (lax.dynamic_index_in_dim(image_counts, grp * n_dp + dp, 0, keepdims=False) > 0).astype(F32)

    flip = n_dp // 2
    near = [(g * n_dp + d, (1 - g) * n_dp + d) for g in range(2) for d in range(n_dp)]
    far = [(g * n_dp + d, (1 - g) * n_dp + d ^ flip) for g in range(2) for d in range(n_dp)]
    both = ("grp", "dp")
    half = per_dev // 2

    first = jnp.where(is_a, attn_out, out_grad)
    second = jnp.where(is_a, out_grad, attn_out)

    def around(own, sent):
        mate = lax.ppermute(own, "dp", swap_core)
        from_near = lax.ppermute(sent[:half], both, near)
        from_far = lax.ppermute(sent[half:], both, far)
        near_mate = lax.ppermute(from_near, "dp", swap_core)
        return [own, mate, from_near, from_far, near_mate, lax.ppermute(from_far, "dp", swap_core)]

    mine_rows = around(first, second)
    over, mate, away = 1 - grp_index, dp_index ^ 1, dp_index ^ flip
    keeps = jnp.stack([
        keep_of(grp_index, dp_index),
        keep_of(grp_index, mate),
        keep_of(over, dp_index),
        keep_of(over, away),
        keep_of(over, mate),
        keep_of(over, away ^ 1),
    ])
    total = (TOK * jnp.sum(image_counts)).astype(F32)
    part, squares = gram(core_arr, keeps, mine_rows, chips * per_chip)
    got = lax.all_to_all(
        part.reshape(chips, per_chip * SLAB, B), "dp", split_axis=0, concat_axis=0, tiled=True, axis_index_groups=same_core
    )
    other_rows = around(second, first)
    slabs = sum_parts(got, *[rows[:SLAB, :B] for rows in other_rows[1:]]) / total

    flat = chip * (per_chip * SLAB) + jnp.arange(per_chip * SLAB)
    t = flat // HALF
    on_diag = jnp.zeros(t.shape, bool)
    for i in range(nb):
        on_diag = on_diag | (t == tri(i, i))
    in_row = core * HALF + flat % HALF
    diag = (on_diag & (flat < used * SLAB))[:, None] & (in_row[:, None] == jnp.arange(B)[None, :])
    damp = jnp.where(is_a, damping[0], damping[1])
    damped = (slabs + damp * diag.astype(F32)).astype(BF16)
    spread = jnp.broadcast_to(damped[None], (chips,) + damped.shape)
    mine = lax.all_to_all(spread, "dp", split_axis=0, concat_axis=0, tiled=True, axis_index_groups=same_core)
    mine = mine.reshape(chips * per_chip * SLAB, B)
    wide = (nb + 2) // 2 * B
    part_w = cross(core_arr, grp_index.astype(jnp.int32)[None], keeps, damped[:SLAB], mine_rows, other_rows, chips, wide)
    mine, part_w = lax.optimization_barrier((mine, part_w))
    theirs = lax.ppermute(mine, "dp", swap_core)
    low, inv, chol_done = chol(core_arr, mine, theirs, width)

    got_w = lax.all_to_all(part_w, "dp", split_axis=0, concat_axis=0, tiled=True, axis_index_groups=same_core)

    at = (dp_index * block).astype(jnp.int32)[None]
    my_rows = rows_of(at, core_arr, mine, theirs, width, ROWS)

    order = column_owner.reshape(chips, 2)
    order = jnp.stack([jnp.where(core == 0, order[:, 0], order[:, 1]), jnp.where(core == 0, order[:, 1], order[:, 0])])
    my_w = sum_parts(got_w, chol_done) / total
    last_w = lax.ppermute(my_w, "grp", [(1, 0)])
    routed = solve_and_route(order, my_w, last_w, low, inv, block)
    same = lax.ppermute(routed[0], both, [(d, n_dp + d) for d in range(n_dp)])
    cross_t = lax.ppermute(routed[1], both, [(d, n_dp + (d ^ 1)) for d in range(n_dp)])
    is_first = core == 0
    pair = jnp.concatenate([jnp.where(is_first, same, cross_t), jnp.where(is_first, cross_t, same)])
    pair = pair[:, : chips * block].reshape(2 * ROWS, chips, block).transpose(1, 2, 0)
    squares = lax.dynamic_index_in_dim(squares[0].reshape(chips, 2, block), core, 1, keepdims=False)
    pair = jnp.concatenate([pair, squares[:, :, None]], axis=2)
    columns = lax.all_to_all(pair, "dp", split_axis=0, concat_axis=0, tiled=True, axis_index_groups=same_core)
    squares = jnp.sum(columns[:, :, 2 * ROWS], axis=0) / total
    columns = columns[:, :, : 2 * ROWS].transpose(1, 0, 2).reshape(block, n_dp * ROWS)[:, :width]
    columns = jnp.pad(columns, ((0, ROWS - block), (0, 0)))
    left = solve(columns, low, inv, my_rows)[:block]
    here = (dp_index * block + jnp.arange(block))[:, None] == jnp.arange(width)[None, :]
    my_rows = jnp.where(here, squares[:, None], my_rows[:block])
    their_rows = lax.ppermute(my_rows, "grp", swap_grp)
    factors = jnp.stack([jnp.where(is_a, my_rows, their_rows), jnp.where(is_a, their_rows, my_rows)])
    back = lax.ppermute(left, "grp", [(1, 0)])
    preconditioned = jnp.where(is_a, back, left).T
    return (factors, preconditioned)


def solution(mesh):
    placed = (P(("grp", "dp"), None), P(("grp", "dp"), None), P(), P(), P())
    return jax.shard_map(
        per_device,
        mesh=mesh,
        in_specs=placed,
        out_specs=(P(None, "dp", None), P(None, "dp")),
        check_vma=False,
    )
```

```python
import functools

import jax
import jax.numpy as jnp
from jax import lax
from jax.experimental import pallas as pl
from jax.experimental.pallas import tpu as pltpu
from jax.sharding import PartitionSpec as P

TOK = 256
B = 128
HALF = 64
SLAB = 16
ROWS = 24
WIDE = 14336
F32 = jnp.float32
BF16 = jnp.bfloat16
NT = (((1,), (1,)), ((), ()))
NN = (((1,), (0,)), ((), ()))
TN = (((0,), (0,)), ((), ()))
VM = pl.BlockSpec(memory_space=pltpu.VMEM)
ANY = pl.BlockSpec(memory_space=pl.ANY)
HBM = pl.BlockSpec(memory_space=pltpu.HBM)
SM = pl.BlockSpec(memory_space=pltpu.SMEM)
TOKEN = jax.ShapeDtypeStruct((8, B), F32)
MIB = 1024 * 1024


def params(mib):
    return pltpu.CompilerParams(vmem_limit_bytes=mib * MIB)


def cost(micros):
    return pl.CostEstimate(flops=int(micros * 1.1e9), bytes_accessed=MIB, transcendentals=0)


def dot(a, b, dims=NT):
    return lax.dot_general(a, b, dims, preferred_element_type=F32)


def split(x):
    hi = x.astype(BF16)
    return hi, (x - hi.astype(F32)).astype(BF16)


def row(x, t):
    return jnp.broadcast_to(x[..., t : t + 1, :], x.shape)


def col(x, c):
    return jnp.broadcast_to(x[..., c : c + 1], x.shape)


def rounded(x):
    return x.astype(BF16).astype(F32)


def tri(i, j):
    return i * (i + 1) // 2 + j


def pieces_of(refs):
    own, mate, near, far, near_mate, far_mate = refs
    return [[(0, own)], [(1, mate)], [(2, near), (3, far)], [(4, near_mate), (5, far_mate)]]


def columns_of(group, cols, keep_ref=None):
    parts = [ref[:, cols] if keep_ref is None else ref[:, cols] * keep_ref[k].astype(BF16) for k, ref in group]
    return parts[0] if len(parts) == 1 else jnp.concatenate(parts, 0)


def gram_kernel(core_ref, keep_ref, *refs):
    pieces, (hbm_ref, squares_ref, out_ref, tmp_ref, sem) = pieces_of(refs[:6]), refs[6:]
    nb = refs[0].shape[1] // B
    start = pl.multiple_of(core_ref[0] * HALF, HALF)
    on = lax.broadcasted_iota(jnp.int32, (B, B), 0) == lax.broadcasted_iota(jnp.int32, (B, B), 1)
    copies = []

    def send(lo, hi):
        copies.append(pltpu.make_async_copy(out_ref.at[lo:hi], hbm_ref.at[lo:hi], sem.at[len(copies)]))
        copies[-1].start()

    used = tri(nb, 0) * HALF
    out_ref[used:, :] = jnp.zeros((out_ref.shape[0] - used, B), F32)
    send(used, out_ref.shape[0])
    for i in range(nb):
        wide = (i + 1) * B
        acc = None
        for group in pieces:
            p = dot(columns_of(group, slice(i * B, wide), keep_ref), columns_of(group, slice(0, wide)), TN)
            acc = p if acc is None else acc + p
        tmp_ref[:, :wide] = acc
        diag = jnp.sum(jnp.where(on, acc[:, i * B :], 0.0), axis=0, keepdims=True)
        squares_ref[:, i * B : wide] = jnp.broadcast_to(diag, (8, B))
        for j in range(i + 1):
            t = tri(i, j)
            out_ref[t * HALF : (t + 1) * HALF, :] = tmp_ref[pl.ds(start, HALF), j * B : (j + 1) * B]
        send(tri(i, 0) * HALF, tri(i + 1, 0) * HALF)
    for copy in copies:
        copy.wait()


def gram(core, keeps, pieces, slots):
    width = pieces[0].shape[1]
    return pl.pallas_call(
        gram_kernel,
        out_shape=(jax.ShapeDtypeStruct((slots * SLAB, B), F32), jax.ShapeDtypeStruct((8, width), F32)),
        in_specs=[SM, SM] + [VM] * 6,
        out_specs=(HBM, VM),
        scratch_shapes=[
            pltpu.VMEM((slots * SLAB, B), F32),
            pltpu.VMEM((B, width), F32),
            pltpu.SemaphoreType.DMA((width // B + 1,)),
        ],
        compiler_params=params(24),
        cost_estimate=cost(4),
        name="gram",
    )(core, keeps, *pieces)


def cross_kernel(core_ref, keep_ref, after_ref, grad_ref, grad_mate_ref, act_ref, act_mate_ref, out_ref, tmp_ref):
    n = act_ref.shape[1]
    for i in range(n // B):
        cols = slice(i * B, (i + 1) * B)
        own = dot(grad_ref[:, cols] * keep_ref[0].astype(BF16), act_ref[...], TN)
        tmp_ref[cols, :] = own + dot(grad_mate_ref[:, cols] * keep_ref[1].astype(BF16), act_mate_ref[...], TN)
    tmp_ref[n:, :] = jnp.zeros((tmp_ref.shape[0] - n, n), F32)
    for q in range(out_ref.shape[0]):
        out_ref[q] = tmp_ref[pl.ds(pl.multiple_of((2 * q + core_ref[0]) * ROWS, 8), ROWS), :]


def cross(core, keeps, after, grads, acts, chips):
    width = acts[0].shape[1]
    return pl.pallas_call(
        cross_kernel,
        out_shape=jax.ShapeDtypeStruct((chips, ROWS, width), F32),
        in_specs=[SM, SM, ANY] + [VM] * 4,
        out_specs=VM,
        scratch_shapes=[pltpu.VMEM((2 * chips * ROWS, width), F32)],
        compiler_params=params(32),
        cost_estimate=cost(30),
        name="cross",
    )(core, keeps, after, *grads, *acts)


def factor_diag(block):
    a = [block[8 * i : 8 * i + 8, :] for i in range(16)]
    lane = lax.broadcasted_iota(jnp.int32, (8, B), 1)
    sub = lax.broadcasted_iota(jnp.int32, (8, B), 0)
    x = [(lane == sub + 8 * g).astype(F32) for g in range(16)]
    inv, inv_r = [], []
    cg = [col(a[0], t) for t in range(8)]
    for g in range(16):
        here = (lane >= 8 * g) & (lane < 8 * g + 8)
        v = jnp.where(here, (lane == sub + 8 * g).astype(F32), a[g])
        xg = x[g]
        if g < 15:
            near = a[g + 1]
            cr = [col(near, 8 * g + t) for t in range(8)]
            nxt = [col(near, 8 * g + 8 + t) for t in range(8)]
            near, xr = jnp.where(here, 0.0, near), x[g + 1]
        rs, vs, xs, css = [], [], [], []
        for t in range(8):
            p = row(cg[t], t)
            r = lax.rsqrt(p)
            lt = jnp.where(sub > t, cg[t] * r, 0.0)
            vn = row(v, t) * r
            v = jnp.where(sub == t, vn, v - lt * vn)
            xn = row(xg, t) / rounded(p * r)
            xg = jnp.where(sub == t, xn, xg - rounded(lt) * xn)
            cs = {s: row(cg[s], t) * r for s in range(t + 1, 8)}
            for s in range(t + 1, 8):
                cg[s] = cg[s] - lt * cs[s]
            rs.append(r)
            vs.append(vn)
            xs.append(xn)
            css.append(cs)
            if g < 15:
                lr = cr[t] * r
                for s in range(8):
                    nxt[s] = nxt[s] - lr * row(lr, s)
                near = near - lr * vn
                xr = xr - rounded(lr) * xn
                for s in range(t + 1, 8):
                    cr[s] = cr[s] - lr * cs[s]
        inv.append(jnp.where(lane <= sub + 8 * g, v, 0.0))
        inv_r.append(xg)
        if g < 15:
            a[g + 1], x[g + 1] = near, xr
            cg = nxt
        for i in range(g + 2, 16):
            c = [col(a[i], 8 * g + t) for t in range(8)]
            ai, xi = jnp.where(here, 0.0, a[i]), x[i]
            for t in range(8):
                l = c[t] * rs[t]
                ai = ai - l * vs[t]
                xi = xi - rounded(l) * xs[t]
                for s in range(t + 1, 8):
                    c[s] = c[s] - l * css[t][s]
            a[i], x[i] = ai, xi
    return jnp.concatenate(inv, 0), jnp.concatenate(inv_r, 0)


def block_of(mine_ref, other_ref, first, i, j):
    t = tri(i, j) * HALF
    mine = mine_ref[t : t + HALF, :].astype(F32)
    other = other_ref[t : t + HALF, :].astype(F32)
    return jnp.concatenate([jnp.where(first, mine, other), jnp.where(first, other, mine)], 0)


def chol_kernel(core_ref, mine_ref, other_ref, low_hbm, inv_hbm, done_ref, low_ref, inv_ref, lo_ref, s_ref, w_ref, sem):
    done_ref[...] = jnp.zeros_like(done_ref)
    n = low_ref.shape[0]
    nb = n // B
    first = core_ref[0] == 0

    def update(kk):
        r0 = kk * B
        s = jnp.concatenate([block_of(mine_ref, other_ref, first, i, kk) for i in range(kk, nb)], 0)
        if kk:
            wts = jnp.concatenate([low_ref[r0 : r0 + B, :r0], lo_ref[r0 : r0 + B, :r0]], 0)
            pr = dot(low_ref[r0:, :r0], wts)
            s = s - (pr[:, :B] + pr[:, B:] + dot(lo_ref[r0:, :r0], low_ref[r0 : r0 + B, :r0]))
        s_ref[r0:, :] = s

    def panel(kk):
        r0 = kk * B
        r1 = r0 + B
        shi, slo = split(s_ref[r1:, :])
        pr = dot(shi, w_ref[...])
        lp = pr[:, :B] + pr[:, B:] + dot(slo, w_ref[:B, :])
        hi, lo = split(lp)
        low_ref[r1:, r0:r1] = hi
        lo_ref[r1:, r0:r1] = lo

    def step(k, _):
        for kk in range(nb):
            pl.when(k == kk)(lambda kk=kk: update(kk))
        r0 = pl.multiple_of(k * B, B)
        rows = pl.ds(r0, B)
        pltpu.make_async_copy(low_ref.at[rows], low_hbm.at[rows, :n], sem.at[0, k]).start()
        linv, lrinv = factor_diag(s_ref[pl.ds(r0, B), :])
        inv_ref[rows, :] = lrinv
        pltpu.make_async_copy(inv_ref.at[rows], inv_hbm.at[rows], sem.at[1, k]).start()
        hi, lo = split(linv)
        w_ref[:B, :] = hi
        w_ref[B:, :] = lo
        for kk in range(nb - 1):
            pl.when(k == kk)(lambda kk=kk: panel(kk))
        return 0

    lax.fori_loop(0, nb, step, 0)
    for k in range(nb):
        rows = slice(k * B, (k + 1) * B)
        pltpu.make_async_copy(low_ref.at[rows], low_hbm.at[rows, :n], sem.at[0, k]).wait()
        pltpu.make_async_copy(inv_ref.at[rows], inv_hbm.at[rows], sem.at[1, k]).wait()


def chol(core, mine, other, n):
    return pl.pallas_call(
        chol_kernel,
        out_shape=(jax.ShapeDtypeStruct((n, WIDE), BF16), jax.ShapeDtypeStruct((n, B), F32), TOKEN),
        in_specs=[SM, VM, VM],
        out_specs=(HBM, HBM, VM),
        scratch_shapes=[
            pltpu.VMEM((n, n), BF16),
            pltpu.VMEM((n, B), F32),
            pltpu.VMEM((n, n), BF16),
            pltpu.VMEM((n, B), F32),
            pltpu.VMEM((2 * B, B), BF16),
            pltpu.SemaphoreType.DMA((2, n // B)),
        ],
        compiler_params=params(28),
        cost_estimate=cost(57),
        name="cholesky",
    )(core, mine, other)


def solve_into(rhs, m, low_hbm, inv_hbm, out_ref, low_ref, inv_ref, sem):
    nb = low_ref.shape[0] // B
    copies = [pltpu.make_async_copy(inv_hbm, inv_ref, sem.at[nb - 1])]
    for b in range(nb - 1):
        part = (slice((b + 1) * B, nb * B), slice(b * B, (b + 1) * B))
        copies.append(pltpu.make_async_copy(low_hbm.at[part], low_ref.at[part], sem.at[b]))
    for copy in copies:
        copy.start()

    def stacked(x):
        return jnp.concatenate(split(x), 0)

    def fold(p):
        return p[:m] + p[m:]

    acc = [rhs(b) for b in range(nb)]
    copies[0].wait()
    for b in range(nb):
        r0, r1 = b * B, (b + 1) * B
        p = fold(dot(stacked(acc[b]), stacked(inv_ref[r0:r1, :])))
        y = p[:, :B] + p[:, B:]
        acc[b] = y
        ys = stacked(y)
        if b < nb - 1:
            copies[b + 1].wait()
        for c in range(b + 1, nb):
            acc[c] = acc[c] - fold(dot(ys, low_ref[c * B : (c + 1) * B, r0:r1]))
    for b in reversed(range(nb)):
        r0, r1 = b * B, (b + 1) * B
        w = jnp.concatenate(split(inv_ref[r0:r1, :]), 1)
        p = fold(dot(stacked(acc[b]), w, NN))
        z = p[:, :B] + p[:, B:]
        out_ref[:, r0:r1] = z
        zs = stacked(z)
        for c in range(b):
            acc[c] = acc[c] - fold(dot(zs, low_ref[r0:r1, c * B : (c + 1) * B], NN))


def solve_scratch(n):
    return [pltpu.VMEM((n, n), BF16), pltpu.VMEM((n, B), F32), pltpu.SemaphoreType.DMA((n // B,))]


def solve_kernel(rhs_ref, low_ref, inv_ref, after_ref, out_ref, *scratch):
    solve_into(lambda b: rhs_ref[:, b * B : (b + 1) * B], rhs_ref.shape[0], low_ref, inv_ref, out_ref, *scratch)


def solve(rhs, low, inv, after):
    return pl.pallas_call(
        solve_kernel,
        out_shape=jax.ShapeDtypeStruct(rhs.shape, F32),
        in_specs=[VM, HBM, HBM, ANY],
        out_specs=VM,
        scratch_shapes=solve_scratch(low.shape[0]),
        compiler_params=params(16),
        cost_estimate=cost(7),
        name="solve",
    )(rhs, low, inv, after)


def route_kernel(block, owner_ref, total_ref, one_ref, two_ref, low_ref, inv_ref, same_ref, cross_ref, t_ref, r_ref, *scratch):
    n = low_ref.shape[0]
    m = one_ref.shape[0]
    total = total_ref[0]

    def rhs(b):
        cols = slice(b * B, (b + 1) * B)
        return (one_ref[:, cols] + two_ref[:, cols]) / total

    solve_into(rhs, m, low_ref, inv_ref, t_ref, *scratch)
    t_ref[:, n:] = jnp.zeros((m, t_ref.shape[1] - n), F32)
    lane = lax.broadcasted_iota(jnp.int32, (m, 2 * B), 1)
    for h, out_ref in enumerate((same_ref, cross_ref)):
        for q in range(owner_ref.shape[1]):
            to, off = block * q // B * B, block * q % B
            src = owner_ref[h, q] * block
            win = t_ref[:, pl.ds(pl.multiple_of(src // B * B, B), 2 * B)]
            win = pltpu.roll(win, (off + 2 * B - src % B) % (2 * B), 1)
            old = r_ref[:, to : to + 2 * B]
            r_ref[:, to : to + 2 * B] = jnp.where((lane >= off) & (lane < off + block), win, old)
        out_ref[...] = r_ref[:, : out_ref.shape[1]]


def solve_and_route(owner, total, one, two, low, inv, block):
    m, n = one.shape
    wide = -(-owner.shape[1] * block // B) * B
    out = jax.ShapeDtypeStruct((m, wide), F32)
    return pl.pallas_call(
        functools.partial(route_kernel, block),
        out_shape=(out, out),
        in_specs=[SM, SM, VM, VM, HBM, HBM],
        out_specs=(VM, VM),
        scratch_shapes=[pltpu.VMEM((m, n + B), F32), pltpu.VMEM((m, wide + B), F32)] + solve_scratch(n),
        compiler_params=params(16),
        cost_estimate=cost(9),
        name="solve_and_route",
    )(owner, total, one, two, low, inv)


def sum_kernel(parts_ref, *refs):
    out_ref = refs[-1]
    acc = parts_ref[0]
    for k in range(1, parts_ref.shape[0]):
        acc = acc + parts_ref[k]
    out_ref[...] = acc


def sum_parts(parts, *after):
    return pl.pallas_call(
        sum_kernel,
        out_shape=jax.ShapeDtypeStruct(parts.shape[1:], F32),
        in_specs=[VM] + [ANY] * len(after),
        out_specs=VM,
        compiler_params=params(16),
        cost_estimate=cost(3),
        name="sum_parts",
    )(parts, *after)


def rows_kernel(at_ref, core_ref, mine_ref, other_ref, out_ref, s_ref):
    m, n = out_ref.shape
    nb = n // B
    first = core_ref[0] == 0
    for i in range(nb):
        for j in range(i + 1):
            blk = block_of(mine_ref, other_ref, first, i, j)
            s_ref[i * B : (i + 1) * B, j * B : (j + 1) * B] = blk
            if i > j:
                s_ref[j * B : (j + 1) * B, i * B : (i + 1) * B] = blk.T
    at = at_ref[0]
    window = s_ref[pl.ds(pl.multiple_of(at // 8 * 8, 8), 32), :]
    shift = at % 8
    out = window[:m]
    for k in range(1, 8):
        out = jnp.where(shift == k, window[k : k + m], out)
    out_ref[...] = out


def rows_of(at, core, mine, other, n, m):
    return pl.pallas_call(
        rows_kernel,
        out_shape=jax.ShapeDtypeStruct((m, n), F32),
        in_specs=[SM, SM, VM, VM],
        out_specs=VM,
        scratch_shapes=[pltpu.VMEM((n + 8, n), F32)],
        compiler_params=params(16),
        cost_estimate=cost(3),
        name="rows",
    )(at, core, mine, other)


def per_device(attn_out, out_grad, image_counts, column_owner, damping):
    n_dp = lax.axis_size("dp")
    dp_index = lax.axis_index("dp")
    grp_index = lax.axis_index("grp")
    per_dev, width = attn_out.shape
    block = width // n_dp
    chips = n_dp // 2
    core = dp_index % 2
    chip = dp_index // 2
    nb = width // B
    used = tri(nb, 0) * HALF // SLAB
    per_chip = -(-used // chips)
    same_core = [list(range(c, n_dp, 2)) for c in range(2)]
    swap_core = [(d, d ^ 1) for d in range(n_dp)]
    swap_grp = [(0, 1), (1, 0)]
    core_arr = core.astype(jnp.int32)[None]
    is_a = grp_index == 0

    def keep_of(grp, dp):
        return (lax.dynamic_index_in_dim(image_counts, grp * n_dp + dp, 0, keepdims=False) > 0).astype(F32)

    flip = n_dp // 2
    near = [(g * n_dp + d, (1 - g) * n_dp + d) for g in range(2) for d in range(n_dp)]
    far = [(g * n_dp + d, (1 - g) * n_dp + d ^ flip) for g in range(2) for d in range(n_dp)]
    both = ("grp", "dp")
    half = per_dev // 2

    sent = jnp.where(is_a, out_grad, attn_out)
    from_near = lax.ppermute(sent[:half], both, near)
    from_far = lax.ppermute(sent[half:], both, far)
    act_mate = lax.ppermute(attn_out, "dp", swap_core)
    grad_mate = lax.ppermute(out_grad, "dp", swap_core)
    mine_rows = [
        jnp.where(is_a, attn_out, out_grad), jnp.where(is_a, act_mate, grad_mate), from_near, from_far,
        lax.ppermute(from_near, "dp", swap_core), lax.ppermute(from_far, "dp", swap_core),
    ]
    over, mate, away = 1 - grp_index, dp_index ^ 1, dp_index ^ flip
    keeps = jnp.stack([
        keep_of(grp_index, dp_index),
        keep_of(grp_index, mate),
        keep_of(over, dp_index),
        keep_of(over, away),
        keep_of(over, mate),
        keep_of(over, away ^ 1),
    ])
    total = (TOK * jnp.sum(image_counts)).astype(F32)
    part, squares = gram(core_arr, keeps, mine_rows, chips * per_chip)
    got = lax.all_to_all(
        part.reshape(chips, per_chip * SLAB, B), "dp", split_axis=0, concat_axis=0, tiled=True, axis_index_groups=same_core
    )
    slabs = sum_parts(got) / total

    flat = chip * (per_chip * SLAB) + jnp.arange(per_chip * SLAB)
    t = flat // HALF
    on_diag = jnp.zeros(t.shape, bool)
    for i in range(nb):
        on_diag = on_diag | (t == tri(i, i))
    in_row = core * HALF + flat % HALF
    diag = (on_diag & (flat < used * SLAB))[:, None] & (in_row[:, None] == jnp.arange(B)[None, :])
    damp = jnp.where(is_a, damping[0], damping[1])
    damped = (slabs + damp * diag.astype(F32)).astype(BF16)
    spread = jnp.broadcast_to(damped[None], (chips,) + damped.shape)
    mine = lax.all_to_all(spread, "dp", split_axis=0, concat_axis=0, tiled=True, axis_index_groups=same_core)
    mine = mine.reshape(chips * per_chip * SLAB, B)
    part_w = cross(core_arr, keeps, damped[:SLAB], [out_grad, grad_mate], [attn_out, act_mate], chips)
    mine, part_w = lax.optimization_barrier((mine, part_w))
    theirs = lax.ppermute(mine, "dp", swap_core)
    low, inv, chol_done = chol(core_arr, mine, theirs, width)

    got_w = lax.all_to_all(part_w, "dp", split_axis=0, concat_axis=0, tiled=True, axis_index_groups=same_core)

    at = (dp_index * block).astype(jnp.int32)[None]
    my_rows = rows_of(at, core_arr, mine, theirs, width, ROWS)

    order = column_owner.reshape(chips, 2)
    order = jnp.stack([jnp.where(core == 0, order[:, 0], order[:, 1]), jnp.where(core == 0, order[:, 1], order[:, 0])])
    my_w = sum_parts(got_w, chol_done)
    their_w = lax.ppermute(my_w, "grp", [(1, 0)])
    same, cross_t = solve_and_route(order, total[None], my_w, their_w, low, inv, block)
    same = lax.ppermute(same, both, [(d, n_dp + d) for d in range(n_dp)])
    cross_t = lax.ppermute(cross_t, both, [(d, n_dp + (d ^ 1)) for d in range(n_dp)])
    is_first = core == 0
    pair = jnp.concatenate([jnp.where(is_first, same, cross_t), jnp.where(is_first, cross_t, same)])
    pair = pair[:, : chips * block].reshape(2 * ROWS, chips, block).transpose(1, 2, 0)
    squares = lax.dynamic_index_in_dim(squares[0].reshape(chips, 2, block), core, 1, keepdims=False)
    pair = jnp.concatenate([pair, squares[:, :, None]], axis=2)
    columns = lax.all_to_all(pair, "dp", split_axis=0, concat_axis=0, tiled=True, axis_index_groups=same_core)
    squares = jnp.sum(columns[:, :, 2 * ROWS], axis=0) / total
    columns = columns[:, :, : 2 * ROWS].transpose(1, 0, 2).reshape(block, n_dp * ROWS)[:, :width]
    columns = jnp.pad(columns, ((0, ROWS - block), (0, 0)))
    left = solve(columns, low, inv, my_rows)[:block]
    here = (dp_index * block + jnp.arange(block))[:, None] == jnp.arange(width)[None, :]
    my_rows = jnp.where(here, squares[:, None], my_rows[:block])
    their_rows = lax.ppermute(my_rows, "grp", swap_grp)
    factors = jnp.stack([jnp.where(is_a, my_rows, their_rows), jnp.where(is_a, their_rows, my_rows)])
    back = lax.ppermute(left, "grp", [(1, 0)])
    preconditioned = jnp.where(is_a, back, left).T
    return (factors, preconditioned)


def solution(mesh):
    placed = (P(("grp", "dp"), None), P(("grp", "dp"), None), P(), P(), P())
    return jax.shard_map(
        per_device,
        mesh=mesh,
        in_specs=placed,
        out_specs=(P(None, "dp", None), P(None, "dp")),
        check_vma=False,
    )
```

```python
import functools

import jax
import jax.numpy as jnp
from jax import lax
from jax.experimental import pallas as pl
from jax.experimental.pallas import tpu as pltpu
from jax.sharding import PartitionSpec as P

TOK = 256
B = 128
HALF = 64
SLAB = 16
ROWS = 24
WIDE = 14336
STEP = 512
F32 = jnp.float32
BF16 = jnp.bfloat16
NT = (((1,), (1,)), ((), ()))
NN = (((1,), (0,)), ((), ()))
TN = (((0,), (0,)), ((), ()))
VM = pl.BlockSpec(memory_space=pltpu.VMEM)
ANY = pl.BlockSpec(memory_space=pl.ANY)
HBM = pl.BlockSpec(memory_space=pltpu.HBM)
SM = pl.BlockSpec(memory_space=pltpu.SMEM)
TOKEN = jax.ShapeDtypeStruct((8, B), F32)
MIB = 1024 * 1024


def params(mib):
    return pltpu.CompilerParams(vmem_limit_bytes=mib * MIB)


def cost(micros):
    return pl.CostEstimate(flops=int(micros * 1.1e9), bytes_accessed=MIB, transcendentals=0)


def dot(a, b, dims=NT):
    return lax.dot_general(a, b, dims, preferred_element_type=F32)


def split(x):
    hi = x.astype(BF16)
    return hi, (x - hi.astype(F32)).astype(BF16)


def row(x, t):
    return jnp.broadcast_to(x[..., t : t + 1, :], x.shape)


def col(x, c):
    return jnp.broadcast_to(x[..., c : c + 1], x.shape)


def rounded(x):
    return x.astype(BF16).astype(F32)


def tri(i, j):
    return i * (i + 1) // 2 + j


def pieces_of(refs):
    own, mate, near, far, near_mate, far_mate = refs
    return [[(0, own)], [(1, mate)], [(2, near), (3, far)], [(4, near_mate), (5, far_mate)]]


def columns_of(group, cols, keep_ref=None):
    parts = [ref[:, cols] if keep_ref is None else ref[:, cols] * keep_ref[k].astype(BF16) for k, ref in group]
    return parts[0] if len(parts) == 1 else jnp.concatenate(parts, 0)


def gram_kernel(core_ref, keep_ref, *refs):
    pieces, (hbm_ref, squares_ref, out_ref, tmp_ref, sem) = pieces_of(refs[:6]), refs[6:]
    nb = refs[0].shape[1] // B
    start = pl.multiple_of(core_ref[0] * HALF, HALF)
    on = lax.broadcasted_iota(jnp.int32, (B, B), 0) == lax.broadcasted_iota(jnp.int32, (B, B), 1)
    copies = []

    def send(lo, hi):
        copies.append(pltpu.make_async_copy(out_ref.at[lo:hi], hbm_ref.at[lo:hi], sem.at[len(copies)]))
        copies[-1].start()

    used = tri(nb, 0) * HALF
    out_ref[used:, :] = jnp.zeros((out_ref.shape[0] - used, B), F32)
    send(used, out_ref.shape[0])
    for i in range(nb):
        wide = (i + 1) * B
        acc = None
        for group in pieces:
            p = dot(columns_of(group, slice(i * B, wide), keep_ref), columns_of(group, slice(0, wide)), TN)
            acc = p if acc is None else acc + p
        tmp_ref[:, :wide] = acc
        diag = jnp.sum(jnp.where(on, acc[:, i * B :], 0.0), axis=0, keepdims=True)
        squares_ref[:, i * B : wide] = jnp.broadcast_to(diag, (8, B))
        for j in range(i + 1):
            t = tri(i, j)
            out_ref[t * HALF : (t + 1) * HALF, :] = tmp_ref[pl.ds(start, HALF), j * B : (j + 1) * B]
        send(tri(i, 0) * HALF, tri(i + 1, 0) * HALF)
    for copy in copies:
        copy.wait()


def gram(core, keeps, pieces, slots):
    width = pieces[0].shape[1]
    return pl.pallas_call(
        gram_kernel,
        out_shape=(jax.ShapeDtypeStruct((slots * SLAB, B), F32), jax.ShapeDtypeStruct((8, width), F32)),
        in_specs=[SM, SM] + [VM] * 6,
        out_specs=(HBM, VM),
        scratch_shapes=[
            pltpu.VMEM((slots * SLAB, B), F32),
            pltpu.VMEM((B, width), F32),
            pltpu.SemaphoreType.DMA((width // B + 1,)),
        ],
        compiler_params=params(24),
        cost_estimate=cost(4),
        name="gram",
    )(core, keeps, *pieces)


def cross_kernel(core_ref, keep_ref, after_ref, grad_ref, grad_mate_ref, act_ref, act_mate_ref, out_ref, tmp_ref):
    n = act_ref.shape[1]
    for i in range(n // B):
        cols = slice(i * B, (i + 1) * B)
        own = dot(grad_ref[:, cols] * keep_ref[0].astype(BF16), act_ref[...], TN)
        tmp_ref[cols, :] = own + dot(grad_mate_ref[:, cols] * keep_ref[1].astype(BF16), act_mate_ref[...], TN)
    tmp_ref[n:, :] = jnp.zeros((tmp_ref.shape[0] - n, n), F32)
    for q in range(out_ref.shape[0]):
        out_ref[q] = tmp_ref[pl.ds(pl.multiple_of((2 * q + core_ref[0]) * ROWS, 8), ROWS), :]


def cross(core, keeps, after, grads, acts, chips):
    width = acts[0].shape[1]
    return pl.pallas_call(
        cross_kernel,
        out_shape=jax.ShapeDtypeStruct((chips, ROWS, width), F32),
        in_specs=[SM, SM, ANY] + [VM] * 4,
        out_specs=VM,
        scratch_shapes=[pltpu.VMEM((2 * chips * ROWS, width), F32)],
        compiler_params=params(32),
        cost_estimate=cost(30),
        name="cross",
    )(core, keeps, after, *grads, *acts)


def factor_diag(block):
    a = [block[8 * i : 8 * i + 8, :] for i in range(16)]
    lane = lax.broadcasted_iota(jnp.int32, (8, B), 1)
    sub = lax.broadcasted_iota(jnp.int32, (8, B), 0)
    x = [(lane == sub + 8 * g).astype(F32) for g in range(16)]
    inv, inv_r = [], []
    cg = [col(a[0], t) for t in range(8)]
    for g in range(16):
        here = (lane >= 8 * g) & (lane < 8 * g + 8)
        v = jnp.where(here, (lane == sub + 8 * g).astype(F32), a[g])
        xg = x[g]
        if g < 15:
            near = a[g + 1]
            cr = [col(near, 8 * g + t) for t in range(8)]
            nxt = [col(near, 8 * g + 8 + t) for t in range(8)]
            near, xr = jnp.where(here, 0.0, near), x[g + 1]
        rs, vs, xs, css = [], [], [], []
        for t in range(8):
            p = row(cg[t], t)
            r = lax.rsqrt(p)
            lt = jnp.where(sub > t, cg[t] * r, 0.0)
            vn = row(v, t) * r
            v = jnp.where(sub == t, vn, v - lt * vn)
            xn = row(xg, t) / rounded(p * r)
            xg = jnp.where(sub == t, xn, xg - rounded(lt) * xn)
            cs = {s: row(cg[s], t) * r for s in range(t + 1, 8)}
            for s in range(t + 1, 8):
                cg[s] = cg[s] - lt * cs[s]
            rs.append(r)
            vs.append(vn)
            xs.append(xn)
            css.append(cs)
            if g < 15:
                lr = cr[t] * r
                for s in range(8):
                    nxt[s] = nxt[s] - lr * row(lr, s)
                near = near - lr * vn
                xr = xr - rounded(lr) * xn
                for s in range(t + 1, 8):
                    cr[s] = cr[s] - lr * cs[s]
        inv.append(jnp.where(lane <= sub + 8 * g, v, 0.0))
        inv_r.append(xg)
        if g < 15:
            a[g + 1], x[g + 1] = near, xr
            cg = nxt
        for i in range(g + 2, 16):
            c = [col(a[i], 8 * g + t) for t in range(8)]
            ai, xi = jnp.where(here, 0.0, a[i]), x[i]
            for t in range(8):
                l = c[t] * rs[t]
                ai = ai - l * vs[t]
                xi = xi - rounded(l) * xs[t]
                for s in range(t + 1, 8):
                    c[s] = c[s] - l * css[t][s]
            a[i], x[i] = ai, xi
    return jnp.concatenate(inv, 0), jnp.concatenate(inv_r, 0)


def block_of(mine_ref, other_ref, first, i, j):
    t = tri(i, j) * HALF
    mine = mine_ref[t : t + HALF, :].astype(F32)
    other = other_ref[t : t + HALF, :].astype(F32)
    return jnp.concatenate([jnp.where(first, mine, other), jnp.where(first, other, mine)], 0)


def join_inverses(low_ref, inv_ref, iv_ref):
    n = low_ref.shape[0]
    iv_ref[...] = jnp.zeros_like(iv_ref)
    for b in range(n // B):
        at = b * B % STEP
        iv_ref[b * B : (b + 1) * B, at : at + B] = inv_ref[b * B : (b + 1) * B, :]
    size = B
    while size < STEP:
        for r0 in range(0, n - size, 2 * size):
            r1 = r0 + size
            r2 = min(r1 + size, n)
            at = r0 % STEP
            left = jnp.concatenate(split(iv_ref[r0:r1, at : at + size]), 1)
            p = dot(low_ref[r1:r2, r0:r1], left, NN)
            phi, plo = split(p[:, :size] + p[:, size:])
            bhi, blo = split(iv_ref[r1:r2, at + size : at + size + r2 - r1])
            iv_ref[r1:r2, at : at + size] = -(dot(bhi, phi, NN) + dot(bhi, plo, NN) + dot(blo, phi, NN))
        size *= 2


def chol_kernel(core_ref, mine_ref, other_ref, low_hbm, done_ref, low_ref, inv_ref, lo_ref, s_ref, w_ref, iv_ref, hl_ref, sem):
    done_ref[...] = jnp.zeros_like(done_ref)
    n = low_ref.shape[0]
    nb = n // B
    first = core_ref[0] == 0

    def update(kk):
        r0 = kk * B
        s = jnp.concatenate([block_of(mine_ref, other_ref, first, i, kk) for i in range(kk, nb)], 0)
        if kk:
            wts = jnp.concatenate([low_ref[r0 : r0 + B, :r0], lo_ref[r0 : r0 + B, :r0]], 0)
            pr = dot(low_ref[r0:, :r0], wts)
            s = s - (pr[:, :B] + pr[:, B:] + dot(lo_ref[r0:, :r0], low_ref[r0 : r0 + B, :r0]))
        s_ref[r0:, :] = s

    def panel(kk):
        r0 = kk * B
        r1 = r0 + B
        shi, slo = split(s_ref[r1:, :])
        pr = dot(shi, w_ref[...])
        lp = pr[:, :B] + pr[:, B:] + dot(slo, w_ref[:B, :])
        hi, lo = split(lp)
        low_ref[r1:, r0:r1] = hi
        lo_ref[r1:, r0:r1] = lo

    def step(k, _):
        for kk in range(nb):
            pl.when(k == kk)(lambda kk=kk: update(kk))
        r0 = pl.multiple_of(k * B, B)
        rows = pl.ds(r0, B)
        pltpu.make_async_copy(low_ref.at[rows], low_hbm.at[rows, :n], sem.at[k]).start()
        linv, lrinv = factor_diag(s_ref[pl.ds(r0, B), :])
        inv_ref[rows, :] = lrinv
        hi, lo = split(linv)
        w_ref[:B, :] = hi
        w_ref[B:, :] = lo
        for kk in range(nb - 1):
            pl.when(k == kk)(lambda kk=kk: panel(kk))
        return 0

    lax.fori_loop(0, nb, step, 0)
    join_inverses(low_ref, inv_ref, iv_ref)
    hi, lo = split(iv_ref[...])
    hl_ref[:, :STEP] = hi
    hl_ref[:, STEP:] = lo
    copies = [
        pltpu.make_async_copy(low_ref.at[k * B : (k + 1) * B], low_hbm.at[k * B : (k + 1) * B, :n], sem.at[k])
        for k in range(nb)
    ]
    copies.append(pltpu.make_async_copy(hl_ref, low_hbm.at[:, n : n + 2 * STEP], sem.at[nb]))
    copies[-1].start()
    for copy in copies:
        copy.wait()


def chol(core, mine, other, n):
    return pl.pallas_call(
        chol_kernel,
        out_shape=(jax.ShapeDtypeStruct((n, WIDE), BF16), TOKEN),
        in_specs=[SM, VM, VM],
        out_specs=(HBM, VM),
        scratch_shapes=[
            pltpu.VMEM((n, n), BF16),
            pltpu.VMEM((n, B), F32),
            pltpu.VMEM((n, n), BF16),
            pltpu.VMEM((n, B), F32),
            pltpu.VMEM((2 * B, B), BF16),
            pltpu.VMEM((n, STEP), F32),
            pltpu.VMEM((n, 2 * STEP), BF16),
            pltpu.SemaphoreType.DMA((n // B + 1,)),
        ],
        compiler_params=params(28),
        cost_estimate=cost(57),
        name="cholesky",
    )(core, mine, other)


def solve_into(rhs, m, n, low_hbm, out_ref, low_ref, hl_ref, sem):
    starts = list(range(0, n, STEP))
    loads = []
    for r0 in starts:
        rows = slice(r0, min(r0 + STEP, n))
        if r0:
            loads.append((low_hbm.at[rows, :r0], low_ref.at[rows, :r0]))
        loads.append((low_hbm.at[rows, n : n + 2 * STEP], hl_ref.at[rows]))
    copies = [pltpu.make_async_copy(src, dst, sem.at[k]) for k, (src, dst) in enumerate(loads)]
    for copy in copies:
        copy.start()

    def stacked(x):
        return jnp.concatenate(split(x), 0)

    def fold(p):
        return p[:m] + p[m:]

    def inverted(x, rows, dims):
        w = rows.stop - rows.start
        xs = stacked(x)
        return fold(dot(xs, hl_ref[rows, :w], dims) + dot(xs, hl_ref[rows, STEP : STEP + w], dims))

    parts = [slice(r0, min(r0 + STEP, n)) for r0 in starts]
    acc = []
    for rows in parts:
        s = rhs(rows)
        for done, y in zip(parts, acc):
            if done is parts[0]:
                copies.pop(0).wait()
            s = s - fold(dot(stacked(y), low_ref[rows, done]))
        copies.pop(0).wait()
        acc.append(inverted(s, rows, NT))
    for k in reversed(range(len(parts))):
        z = inverted(acc[k], parts[k], NN)
        out_ref[:, parts[k]] = z
        zs = stacked(z)
        for c in range(k):
            acc[c] = acc[c] - fold(dot(zs, low_ref[parts[k], parts[c]], NN))


def solve_scratch(n):
    return [pltpu.VMEM((n, n), BF16), pltpu.VMEM((n, 2 * STEP), BF16), pltpu.SemaphoreType.DMA((2 * -(-n // STEP) - 1,))]


def solve_kernel(rhs_ref, low_ref, after_ref, out_ref, *scratch):
    m, n = rhs_ref.shape
    solve_into(lambda cols: rhs_ref[:, cols], m, n, low_ref, out_ref, *scratch)


def solve(rhs, low, after):
    return pl.pallas_call(
        solve_kernel,
        out_shape=jax.ShapeDtypeStruct(rhs.shape, F32),
        in_specs=[VM, HBM, ANY],
        out_specs=VM,
        scratch_shapes=solve_scratch(rhs.shape[1]),
        compiler_params=params(16),
        cost_estimate=cost(7),
        name="solve",
    )(rhs, low, after)


def route_kernel(block, owner_ref, total_ref, one_ref, two_ref, low_ref, same_ref, cross_ref, t_ref, r_ref, *scratch):
    m, n = one_ref.shape
    total = total_ref[0]

    def rhs(cols):
        return (one_ref[:, cols] + two_ref[:, cols]) / total

    solve_into(rhs, m, n, low_ref, t_ref, *scratch)
    t_ref[:, n:] = jnp.zeros((m, t_ref.shape[1] - n), F32)
    lane = lax.broadcasted_iota(jnp.int32, (m, 2 * B), 1)
    for h, out_ref in enumerate((same_ref, cross_ref)):
        for q in range(owner_ref.shape[1]):
            to, off = block * q // B * B, block * q % B
            src = owner_ref[h, q] * block
            win = t_ref[:, pl.ds(pl.multiple_of(src // B * B, B), 2 * B)]
            win = pltpu.roll(win, (off + 2 * B - src % B) % (2 * B), 1)
            old = r_ref[:, to : to + 2 * B]
            r_ref[:, to : to + 2 * B] = jnp.where((lane >= off) & (lane < off + block), win, old)
        out_ref[...] = r_ref[:, : out_ref.shape[1]]


def solve_and_route(owner, total, one, two, low, block):
    m, n = one.shape
    wide = -(-owner.shape[1] * block // B) * B
    out = jax.ShapeDtypeStruct((m, wide), F32)
    return pl.pallas_call(
        functools.partial(route_kernel, block),
        out_shape=(out, out),
        in_specs=[SM, SM, VM, VM, HBM],
        out_specs=(VM, VM),
        scratch_shapes=[pltpu.VMEM((m, n + B), F32), pltpu.VMEM((m, wide + B), F32)] + solve_scratch(n),
        compiler_params=params(16),
        cost_estimate=cost(9),
        name="solve_and_route",
    )(owner, total, one, two, low)


def sum_kernel(parts_ref, *refs):
    out_ref = refs[-1]
    acc = parts_ref[0]
    for k in range(1, parts_ref.shape[0]):
        acc = acc + parts_ref[k]
    out_ref[...] = acc


def damp_kernel(scale_ref, parts_ref, diag_ref, out_ref, done_ref, sum_ref, sem):
    acc = parts_ref[0]
    for k in range(1, parts_ref.shape[0]):
        acc = acc + parts_ref[k]
    sum_ref[...] = (acc / scale_ref[0] + scale_ref[1] * diag_ref[...]).astype(BF16)
    copies = [pltpu.make_async_copy(sum_ref, out_ref.at[k], sem.at[k]) for k in range(out_ref.shape[0])]
    for copy in copies:
        copy.start()
    done_ref[...] = jnp.zeros_like(done_ref)
    for copy in copies:
        copy.wait()


def damp_and_spread(scale, parts, diag):
    chips = parts.shape[0]
    return pl.pallas_call(
        damp_kernel,
        out_shape=(jax.ShapeDtypeStruct(parts.shape, BF16), TOKEN),
        in_specs=[SM, VM, VM],
        out_specs=(HBM, VM),
        scratch_shapes=[pltpu.VMEM(parts.shape[1:], BF16), pltpu.SemaphoreType.DMA((chips,))],
        compiler_params=params(16),
        cost_estimate=cost(3),
        name="damp_and_spread",
    )(scale, parts, diag)


def sum_parts(parts, *after):
    return pl.pallas_call(
        sum_kernel,
        out_shape=jax.ShapeDtypeStruct(parts.shape[1:], F32),
        in_specs=[VM] + [ANY] * len(after),
        out_specs=VM,
        compiler_params=params(16),
        cost_estimate=cost(3),
        name="sum_parts",
    )(parts, *after)


def rows_kernel(at_ref, core_ref, mine_ref, other_ref, out_ref, s_ref):
    m, n = out_ref.shape
    nb = n // B
    first = core_ref[0] == 0
    for i in range(nb):
        for j in range(i + 1):
            blk = block_of(mine_ref, other_ref, first, i, j)
            s_ref[i * B : (i + 1) * B, j * B : (j + 1) * B] = blk
            if i > j:
                s_ref[j * B : (j + 1) * B, i * B : (i + 1) * B] = blk.T
    at = at_ref[0]
    window = s_ref[pl.ds(pl.multiple_of(at // 8 * 8, 8), 32), :]
    shift = at % 8
    out = window[:m]
    for k in range(1, 8):
        out = jnp.where(shift == k, window[k : k + m], out)
    out_ref[...] = out


def rows_of(at, core, mine, other, n, m):
    return pl.pallas_call(
        rows_kernel,
        out_shape=jax.ShapeDtypeStruct((m, n), F32),
        in_specs=[SM, SM, VM, VM],
        out_specs=VM,
        scratch_shapes=[pltpu.VMEM((n + 8, n), F32)],
        compiler_params=params(16),
        cost_estimate=cost(3),
        name="rows",
    )(at, core, mine, other)


def per_device(attn_out, out_grad, image_counts, column_owner, damping):
    n_dp = lax.axis_size("dp")
    dp_index = lax.axis_index("dp")
    grp_index = lax.axis_index("grp")
    per_dev, width = attn_out.shape
    block = width // n_dp
    chips = n_dp // 2
    core = dp_index % 2
    chip = dp_index // 2
    nb = width // B
    used = tri(nb, 0) * HALF // SLAB
    per_chip = -(-used // chips)
    same_core = [list(range(c, n_dp, 2)) for c in range(2)]
    swap_core = [(d, d ^ 1) for d in range(n_dp)]
    swap_grp = [(0, 1), (1, 0)]
    core_arr = core.astype(jnp.int32)[None]
    is_a = grp_index == 0

    def keep_of(grp, dp):
        return (lax.dynamic_index_in_dim(image_counts, grp * n_dp + dp, 0, keepdims=False) > 0).astype(F32)

    flip = n_dp // 2
    near = [(g * n_dp + d, (1 - g) * n_dp + d) for g in range(2) for d in range(n_dp)]
    far = [(g * n_dp + d, (1 - g) * n_dp + d ^ flip) for g in range(2) for d in range(n_dp)]
    both = ("grp", "dp")
    half = per_dev // 2

    sent = jnp.where(is_a, out_grad, attn_out)
    from_near = lax.ppermute(sent[:half], both, near)
    from_far = lax.ppermute(sent[half:], both, far)
    act_mate = lax.ppermute(attn_out, "dp", swap_core)
    grad_mate = lax.ppermute(out_grad, "dp", swap_core)
    mine_rows = [
        jnp.where(is_a, attn_out, out_grad), jnp.where(is_a, act_mate, grad_mate), from_near, from_far,
        lax.ppermute(from_near, "dp", swap_core), lax.ppermute(from_far, "dp", swap_core),
    ]
    over, mate, away = 1 - grp_index, dp_index ^ 1, dp_index ^ flip
    keeps = jnp.stack([
        keep_of(grp_index, dp_index),
        keep_of(grp_index, mate),
        keep_of(over, dp_index),
        keep_of(over, away),
        keep_of(over, mate),
        keep_of(over, away ^ 1),
    ])
    total = (TOK * jnp.sum(image_counts)).astype(F32)
    part, squares = gram(core_arr, keeps, mine_rows, chips * per_chip)
    got = lax.all_to_all(
        part.reshape(chips, per_chip * SLAB, B), "dp", split_axis=0, concat_axis=0, tiled=True, axis_index_groups=same_core
    )
    flat = chip * (per_chip * SLAB) + jnp.arange(per_chip * SLAB)
    t = flat // HALF
    on_diag = jnp.zeros(t.shape, bool)
    for i in range(nb):
        on_diag = on_diag | (t == tri(i, i))
    in_row = core * HALF + flat % HALF
    diag = (on_diag & (flat < used * SLAB))[:, None] & (in_row[:, None] == jnp.arange(B)[None, :])
    damp = jnp.where(is_a, damping[0], damping[1])
    spread, damp_done = damp_and_spread(jnp.stack([total, damp]), got, diag.astype(F32))
    mine = lax.all_to_all(spread, "dp", split_axis=0, concat_axis=0, tiled=True, axis_index_groups=same_core)
    mine = mine.reshape(chips * per_chip * SLAB, B)
    part_w = cross(core_arr, keeps, damp_done, [out_grad, grad_mate], [attn_out, act_mate], chips)
    mine, part_w = lax.optimization_barrier((mine, part_w))
    theirs = lax.ppermute(mine, "dp", swap_core)
    low, chol_done = chol(core_arr, mine, theirs, width)

    got_w = lax.all_to_all(part_w, "dp", split_axis=0, concat_axis=0, tiled=True, axis_index_groups=same_core)

    at = (dp_index * block).astype(jnp.int32)[None]
    my_rows = rows_of(at, core_arr, mine, theirs, width, ROWS)

    order = column_owner.reshape(chips, 2)
    order = jnp.stack([jnp.where(core == 0, order[:, 0], order[:, 1]), jnp.where(core == 0, order[:, 1], order[:, 0])])
    my_w = sum_parts(got_w, chol_done)
    their_w = lax.ppermute(my_w, "grp", [(1, 0)])
    same, cross_t = solve_and_route(order, total[None], my_w, their_w, low, block)
    same = lax.ppermute(same, both, [(d, n_dp + d) for d in range(n_dp)])
    cross_t = lax.ppermute(cross_t, both, [(d, n_dp + (d ^ 1)) for d in range(n_dp)])
    is_first = core == 0
    pair = jnp.concatenate([jnp.where(is_first, same, cross_t), jnp.where(is_first, cross_t, same)])
    pair = pair[:, : chips * block].reshape(2 * ROWS, chips, block).transpose(1, 2, 0)
    squares = lax.dynamic_index_in_dim(squares[0].reshape(chips, 2, block), core, 1, keepdims=False)
    pair = jnp.concatenate([pair, squares[:, :, None]], axis=2)
    columns = lax.all_to_all(pair, "dp", split_axis=0, concat_axis=0, tiled=True, axis_index_groups=same_core)
    squares = jnp.sum(columns[:, :, 2 * ROWS], axis=0) / total
    columns = columns[:, :, : 2 * ROWS].transpose(1, 0, 2).reshape(block, n_dp * ROWS)[:, :width]
    columns = jnp.pad(columns, ((0, ROWS - block), (0, 0)))
    left = solve(columns, low, my_rows)[:block]
    here = (dp_index * block + jnp.arange(block))[:, None] == jnp.arange(width)[None, :]
    my_rows = jnp.where(here, squares[:, None], my_rows[:block])
    their_rows = lax.ppermute(my_rows, "grp", swap_grp)
    factors = jnp.stack([jnp.where(is_a, my_rows, their_rows), jnp.where(is_a, their_rows, my_rows)])
    back = lax.ppermute(left, "grp", [(1, 0)])
    preconditioned = jnp.where(is_a, back, left).T
    return (factors, preconditioned)


def solution(mesh):
    placed = (P(("grp", "dp"), None), P(("grp", "dp"), None), P(), P(), P())
    return jax.shard_map(
        per_device,
        mesh=mesh,
        in_specs=placed,
        out_specs=(P(None, "dp", None), P(None, "dp")),
        check_vma=False,
    )
```

```python
import functools

import jax
import jax.numpy as jnp
from jax import lax
from jax.experimental import pallas as pl
from jax.experimental.pallas import tpu as pltpu
from jax.sharding import PartitionSpec as P

TOK = 256
B = 128
HALF = 64
SLAB = 16
ROWS = 24
WIDE = 14336
STEP = 512
F32 = jnp.float32
BF16 = jnp.bfloat16
NT = (((1,), (1,)), ((), ()))
NN = (((1,), (0,)), ((), ()))
TN = (((0,), (0,)), ((), ()))
VM = pl.BlockSpec(memory_space=pltpu.VMEM)
ANY = pl.BlockSpec(memory_space=pl.ANY)
HBM = pl.BlockSpec(memory_space=pltpu.HBM)
SM = pl.BlockSpec(memory_space=pltpu.SMEM)
TOKEN = jax.ShapeDtypeStruct((8, B), F32)
MIB = 1024 * 1024


def params(mib):
    return pltpu.CompilerParams(vmem_limit_bytes=mib * MIB)


def cost(micros):
    return pl.CostEstimate(flops=int(micros * 1.1e9), bytes_accessed=MIB, transcendentals=0)


def dot(a, b, dims=NT):
    return lax.dot_general(a, b, dims, preferred_element_type=F32)


def split(x):
    hi = x.astype(BF16)
    return hi, (x - hi.astype(F32)).astype(BF16)


def row(x, t):
    return jnp.broadcast_to(x[..., t : t + 1, :], x.shape)


def col(x, c):
    return jnp.broadcast_to(x[..., c : c + 1], x.shape)


def rounded(x):
    return x.astype(BF16).astype(F32)


def tri(i, j):
    return i * (i + 1) // 2 + j


def pieces_of(refs):
    own, mate, near, far, near_mate, far_mate = refs
    return [[(0, own)], [(1, mate)], [(2, near), (3, far)], [(4, near_mate), (5, far_mate)]]


def columns_of(group, cols, keep_ref=None):
    parts = [ref[:, cols] if keep_ref is None else ref[:, cols] * keep_ref[k].astype(BF16) for k, ref in group]
    return parts[0] if len(parts) == 1 else jnp.concatenate(parts, 0)


def gram_kernel(core_ref, keep_ref, *refs):
    pieces, (hbm_ref, squares_ref, out_ref, tmp_ref, sem) = pieces_of(refs[:6]), refs[6:]
    nb = refs[0].shape[1] // B
    start = pl.multiple_of(core_ref[0] * HALF, HALF)
    on = lax.broadcasted_iota(jnp.int32, (B, B), 0) == lax.broadcasted_iota(jnp.int32, (B, B), 1)
    copies = []

    def send(lo, hi):
        copies.append(pltpu.make_async_copy(out_ref.at[lo:hi], hbm_ref.at[lo:hi], sem.at[len(copies)]))
        copies[-1].start()

    used = tri(nb, 0) * HALF
    out_ref[used:, :] = jnp.zeros((out_ref.shape[0] - used, B), F32)
    send(used, out_ref.shape[0])
    for i in range(nb):
        wide = (i + 1) * B
        acc = None
        for group in pieces:
            p = dot(columns_of(group, slice(i * B, wide), keep_ref), columns_of(group, slice(0, wide)), TN)
            acc = p if acc is None else acc + p
        tmp_ref[:, :wide] = acc
        diag = jnp.sum(jnp.where(on, acc[:, i * B :], 0.0), axis=0, keepdims=True)
        squares_ref[:, i * B : wide] = jnp.broadcast_to(diag, (8, B))
        for j in range(i + 1):
            t = tri(i, j)
            out_ref[t * HALF : (t + 1) * HALF, :] = tmp_ref[pl.ds(start, HALF), j * B : (j + 1) * B]
        send(tri(i, 0) * HALF, tri(i + 1, 0) * HALF)
    for copy in copies:
        copy.wait()


def gram(core, keeps, pieces, slots):
    width = pieces[0].shape[1]
    return pl.pallas_call(
        gram_kernel,
        out_shape=(jax.ShapeDtypeStruct((slots * SLAB, B), F32), jax.ShapeDtypeStruct((8, width), F32)),
        in_specs=[SM, SM] + [VM] * 6,
        out_specs=(HBM, VM),
        scratch_shapes=[
            pltpu.VMEM((slots * SLAB, B), F32),
            pltpu.VMEM((B, width), F32),
            pltpu.SemaphoreType.DMA((width // B + 1,)),
        ],
        compiler_params=params(40),
        cost_estimate=cost(4),
        name="gram",
    )(core, keeps, *pieces)


def cross_kernel(core_ref, grp_ref, keep_ref, after_ref, *refs):
    mine, other, (out_ref, tmp_ref) = pieces_of(refs[:6]), pieces_of(refs[6:12]), refs[12:]
    n = refs[0].shape[1]
    wide = out_ref.shape[2]

    def run(left, right, first):
        for i in range(n // B):
            acc = None
            for lg, rg in zip(left, right):
                p = dot(columns_of(lg, slice(i * B, (i + 1) * B), keep_ref), columns_of(rg, slice(first, first + wide)), TN)
                acc = p if acc is None else acc + p
            tmp_ref[i * B : (i + 1) * B, :] = acc

    pl.when(grp_ref[0] == 0)(lambda: run(other, mine, 0))
    pl.when(grp_ref[0] == 1)(lambda: run(mine, other, n - wide))
    tmp_ref[n:, :] = jnp.zeros((tmp_ref.shape[0] - n, wide), F32)
    for q in range(out_ref.shape[0]):
        out_ref[q] = tmp_ref[pl.ds(pl.multiple_of((2 * q + core_ref[0]) * ROWS, 8), ROWS), :]


def cross(core, grp, keeps, after, mine, other, chips, wide):
    return pl.pallas_call(
        cross_kernel,
        out_shape=jax.ShapeDtypeStruct((chips, ROWS, wide), F32),
        in_specs=[SM, SM, SM, ANY] + [VM] * 12,
        out_specs=VM,
        scratch_shapes=[pltpu.VMEM((2 * chips * ROWS, wide), F32)],
        compiler_params=params(40),
        cost_estimate=cost(30),
        name="cross",
    )(core, grp, keeps, after, *mine, *other)


def factor_diag(block):
    a = [block[8 * i : 8 * i + 8, :] for i in range(16)]
    lane = lax.broadcasted_iota(jnp.int32, (8, B), 1)
    sub = lax.broadcasted_iota(jnp.int32, (8, B), 0)
    x = [(lane == sub + 8 * g).astype(F32) for g in range(16)]
    inv, inv_r = [], []
    cg = [col(a[0], t) for t in range(8)]
    for g in range(16):
        here = (lane >= 8 * g) & (lane < 8 * g + 8)
        v = jnp.where(here, (lane == sub + 8 * g).astype(F32), a[g])
        xg = x[g]
        if g < 15:
            near = a[g + 1]
            cr = [col(near, 8 * g + t) for t in range(8)]
            nxt = [col(near, 8 * g + 8 + t) for t in range(8)]
            near, xr = jnp.where(here, 0.0, near), x[g + 1]
        rs, vs, xs, css = [], [], [], []
        for t in range(8):
            p = row(cg[t], t)
            r = lax.rsqrt(p)
            lt = jnp.where(sub > t, cg[t] * r, 0.0)
            vn = row(v, t) * r
            v = jnp.where(sub == t, vn, v - lt * vn)
            xn = row(xg, t) / rounded(p * r)
            xg = jnp.where(sub == t, xn, xg - rounded(lt) * xn)
            cs = {s: row(cg[s], t) * r for s in range(t + 1, 8)}
            for s in range(t + 1, 8):
                cg[s] = cg[s] - lt * cs[s]
            rs.append(r)
            vs.append(vn)
            xs.append(xn)
            css.append(cs)
            if g < 15:
                lr = cr[t] * r
                for s in range(8):
                    nxt[s] = nxt[s] - lr * row(lr, s)
                near = near - lr * vn
                xr = xr - rounded(lr) * xn
                for s in range(t + 1, 8):
                    cr[s] = cr[s] - lr * cs[s]
        inv.append(jnp.where(lane <= sub + 8 * g, v, 0.0))
        inv_r.append(xg)
        if g < 15:
            a[g + 1], x[g + 1] = near, xr
            cg = nxt
        for i in range(g + 2, 16):
            c = [col(a[i], 8 * g + t) for t in range(8)]
            ai, xi = jnp.where(here, 0.0, a[i]), x[i]
            for t in range(8):
                l = c[t] * rs[t]
                ai = ai - l * vs[t]
                xi = xi - rounded(l) * xs[t]
                for s in range(t + 1, 8):
                    c[s] = c[s] - l * css[t][s]
            a[i], x[i] = ai, xi
    return jnp.concatenate(inv, 0), jnp.concatenate(inv_r, 0)


def block_of(mine_ref, other_ref, first, i, j):
    t = tri(i, j) * HALF
    mine = mine_ref[t : t + HALF, :].astype(F32)
    other = other_ref[t : t + HALF, :].astype(F32)
    return jnp.concatenate([jnp.where(first, mine, other), jnp.where(first, other, mine)], 0)


def join_inverses(low_ref, inv_ref, iv_ref):
    n = low_ref.shape[0]
    iv_ref[...] = jnp.zeros_like(iv_ref)
    for b in range(n // B):
        at = b * B % STEP
        iv_ref[b * B : (b + 1) * B, at : at + B] = inv_ref[b * B : (b + 1) * B, :]
    size = B
    while size < STEP:
        for r0 in range(0, n - size, 2 * size):
            r1 = r0 + size
            r2 = min(r1 + size, n)
            at = r0 % STEP
            left = jnp.concatenate(split(iv_ref[r0:r1, at : at + size]), 1)
            p = dot(low_ref[r1:r2, r0:r1], left, NN)
            phi, plo = split(p[:, :size] + p[:, size:])
            bhi, blo = split(iv_ref[r1:r2, at + size : at + size + r2 - r1])
            iv_ref[r1:r2, at : at + size] = -(dot(bhi, phi, NN) + dot(bhi, plo, NN) + dot(blo, phi, NN))
        size *= 2


def chol_kernel(core_ref, mine_ref, other_ref, low_hbm, done_ref, low_ref, inv_ref, lo_ref, s_ref, w_ref, iv_ref, hl_ref, sem):
    done_ref[...] = jnp.zeros_like(done_ref)
    n = low_ref.shape[0]
    nb = n // B
    first = core_ref[0] == 0

    def update(kk):
        r0 = kk * B
        s = jnp.concatenate([block_of(mine_ref, other_ref, first, i, kk) for i in range(kk, nb)], 0)
        if kk:
            wts = jnp.concatenate([low_ref[r0 : r0 + B, :r0], lo_ref[r0 : r0 + B, :r0]], 0)
            pr = dot(low_ref[r0:, :r0], wts)
            s = s - (pr[:, :B] + pr[:, B:] + dot(lo_ref[r0:, :r0], low_ref[r0 : r0 + B, :r0]))
        s_ref[r0:, :] = s

    def panel(kk):
        r0 = kk * B
        r1 = r0 + B
        shi, slo = split(s_ref[r1:, :])
        pr = dot(shi, w_ref[...])
        lp = pr[:, :B] + pr[:, B:] + dot(slo, w_ref[:B, :])
        hi, lo = split(lp)
        low_ref[r1:, r0:r1] = hi
        lo_ref[r1:, r0:r1] = lo

    def step(k, _):
        for kk in range(nb):
            pl.when(k == kk)(lambda kk=kk: update(kk))
        r0 = pl.multiple_of(k * B, B)
        rows = pl.ds(r0, B)
        pltpu.make_async_copy(low_ref.at[rows], low_hbm.at[rows, :n], sem.at[k]).start()
        linv, lrinv = factor_diag(s_ref[pl.ds(r0, B), :])
        inv_ref[rows, :] = lrinv
        hi, lo = split(linv)
        w_ref[:B, :] = hi
        w_ref[B:, :] = lo
        for kk in range(nb - 1):
            pl.when(k == kk)(lambda kk=kk: panel(kk))
        return 0

    lax.fori_loop(0, nb, step, 0)
    join_inverses(low_ref, inv_ref, iv_ref)
    hi, lo = split(iv_ref[...])
    hl_ref[:, :STEP] = hi
    hl_ref[:, STEP:] = lo
    copies = [
        pltpu.make_async_copy(low_ref.at[k * B : (k + 1) * B], low_hbm.at[k * B : (k + 1) * B, :n], sem.at[k])
        for k in range(nb)
    ]
    copies.append(pltpu.make_async_copy(hl_ref, low_hbm.at[:, n : n + 2 * STEP], sem.at[nb]))
    copies[-1].start()
    for copy in copies:
        copy.wait()


def chol(core, mine, other, n):
    return pl.pallas_call(
        chol_kernel,
        out_shape=(jax.ShapeDtypeStruct((n, WIDE), BF16), TOKEN),
        in_specs=[SM, VM, VM],
        out_specs=(HBM, VM),
        scratch_shapes=[
            pltpu.VMEM((n, n), BF16),
            pltpu.VMEM((n, B), F32),
            pltpu.VMEM((n, n), BF16),
            pltpu.VMEM((n, B), F32),
            pltpu.VMEM((2 * B, B), BF16),
            pltpu.VMEM((n, STEP), F32),
            pltpu.VMEM((n, 2 * STEP), BF16),
            pltpu.SemaphoreType.DMA((n // B + 1,)),
        ],
        compiler_params=params(28),
        cost_estimate=cost(57),
        name="cholesky",
    )(core, mine, other)


def solve_into(rhs, m, n, low_hbm, out_ref, low_ref, hl_ref, sem):
    starts = list(range(0, n, STEP))
    loads = []
    for r0 in starts:
        rows = slice(r0, min(r0 + STEP, n))
        if r0:
            loads.append((low_hbm.at[rows, :r0], low_ref.at[rows, :r0]))
        loads.append((low_hbm.at[rows, n : n + 2 * STEP], hl_ref.at[rows]))
    copies = [pltpu.make_async_copy(src, dst, sem.at[k]) for k, (src, dst) in enumerate(loads)]
    for copy in copies:
        copy.start()

    def stacked(x):
        return jnp.concatenate(split(x), 0)

    def fold(p):
        return p[:m] + p[m:]

    def inverted(x, rows, dims):
        w = rows.stop - rows.start
        xs = stacked(x)
        return fold(dot(xs, hl_ref[rows, :w], dims) + dot(xs, hl_ref[rows, STEP : STEP + w], dims))

    parts = [slice(r0, min(r0 + STEP, n)) for r0 in starts]
    acc = []
    for rows in parts:
        s = rhs(rows)
        for done, y in zip(parts, acc):
            if done is parts[0]:
                copies.pop(0).wait()
            s = s - fold(dot(stacked(y), low_ref[rows, done]))
        copies.pop(0).wait()
        acc.append(inverted(s, rows, NT))
    for k in reversed(range(len(parts))):
        z = inverted(acc[k], parts[k], NN)
        out_ref[:, parts[k]] = z
        zs = stacked(z)
        for c in range(k):
            acc[c] = acc[c] - fold(dot(zs, low_ref[parts[k], parts[c]], NN))


def solve_scratch(n):
    return [pltpu.VMEM((n, n), BF16), pltpu.VMEM((n, 2 * STEP), BF16), pltpu.SemaphoreType.DMA((2 * -(-n // STEP) - 1,))]


def solve_kernel(rhs_ref, low_ref, after_ref, out_ref, *scratch):
    m, n = rhs_ref.shape
    solve_into(lambda cols: rhs_ref[:, cols], m, n, low_ref, out_ref, *scratch)


def solve(rhs, low, after):
    return pl.pallas_call(
        solve_kernel,
        out_shape=jax.ShapeDtypeStruct(rhs.shape, F32),
        in_specs=[VM, HBM, ANY],
        out_specs=VM,
        scratch_shapes=solve_scratch(rhs.shape[1]),
        compiler_params=params(16),
        cost_estimate=cost(7),
        name="solve",
    )(rhs, low, after)


def route_kernel(block, owner_ref, total_ref, one_ref, two_ref, low_ref, same_ref, cross_ref, t_ref, r_ref, *scratch):
    m, wide = one_ref.shape
    n = t_ref.shape[1] - B
    right = jnp.concatenate([one_ref[...], two_ref[:, 2 * wide - n :]], 1) / total_ref[0]

    def rhs(cols):
        return right[:, cols]

    solve_into(rhs, m, n, low_ref, t_ref, *scratch)
    t_ref[:, n:] = jnp.zeros((m, t_ref.shape[1] - n), F32)
    lane = lax.broadcasted_iota(jnp.int32, (m, 2 * B), 1)
    for h, out_ref in enumerate((same_ref, cross_ref)):
        for q in range(owner_ref.shape[1]):
            to, off = block * q // B * B, block * q % B
            src = owner_ref[h, q] * block
            win = t_ref[:, pl.ds(pl.multiple_of(src // B * B, B), 2 * B)]
            win = pltpu.roll(win, (off + 2 * B - src % B) % (2 * B), 1)
            old = r_ref[:, to : to + 2 * B]
            r_ref[:, to : to + 2 * B] = jnp.where((lane >= off) & (lane < off + block), win, old)
        out_ref[...] = r_ref[:, : out_ref.shape[1]]


def solve_and_route(owner, total, one, two, low, n, block):
    m = one.shape[0]
    wide = -(-owner.shape[1] * block // B) * B
    out = jax.ShapeDtypeStruct((m, wide), F32)
    return pl.pallas_call(
        functools.partial(route_kernel, block),
        out_shape=(out, out),
        in_specs=[SM, SM, VM, VM, HBM],
        out_specs=(VM, VM),
        scratch_shapes=[pltpu.VMEM((m, n + B), F32), pltpu.VMEM((m, wide + B), F32)] + solve_scratch(n),
        compiler_params=params(16),
        cost_estimate=cost(9),
        name="solve_and_route",
    )(owner, total, one, two, low)


def sum_kernel(parts_ref, *refs):
    out_ref = refs[-1]
    acc = parts_ref[0]
    for k in range(1, parts_ref.shape[0]):
        acc = acc + parts_ref[k]
    out_ref[...] = acc


def damp_kernel(scale_ref, parts_ref, diag_ref, out_ref, done_ref, sum_ref, sem):
    acc = parts_ref[0]
    for k in range(1, parts_ref.shape[0]):
        acc = acc + parts_ref[k]
    sum_ref[...] = (acc / scale_ref[0] + scale_ref[1] * diag_ref[...]).astype(BF16)
    copies = [pltpu.make_async_copy(sum_ref, out_ref.at[k], sem.at[k]) for k in range(out_ref.shape[0])]
    for copy in copies:
        copy.start()
    done_ref[...] = jnp.zeros_like(done_ref)
    for copy in copies:
        copy.wait()


def damp_and_spread(scale, parts, diag):
    chips = parts.shape[0]
    return pl.pallas_call(
        damp_kernel,
        out_shape=(jax.ShapeDtypeStruct(parts.shape, BF16), TOKEN),
        in_specs=[SM, VM, VM],
        out_specs=(HBM, VM),
        scratch_shapes=[pltpu.VMEM(parts.shape[1:], BF16), pltpu.SemaphoreType.DMA((chips,))],
        compiler_params=params(60),
        cost_estimate=cost(3),
        name="damp_and_spread",
    )(scale, parts, diag)


def sum_parts(parts, *after):
    return pl.pallas_call(
        sum_kernel,
        out_shape=jax.ShapeDtypeStruct(parts.shape[1:], F32),
        in_specs=[VM] + [ANY] * len(after),
        out_specs=VM,
        compiler_params=params(16),
        cost_estimate=cost(3),
        name="sum_parts",
    )(parts, *after)


def rows_kernel(at_ref, core_ref, mine_ref, other_ref, out_ref, s_ref):
    m, n = out_ref.shape
    nb = n // B
    first = core_ref[0] == 0
    for i in range(nb):
        for j in range(i + 1):
            blk = block_of(mine_ref, other_ref, first, i, j)
            s_ref[i * B : (i + 1) * B, j * B : (j + 1) * B] = blk
            if i > j:
                s_ref[j * B : (j + 1) * B, i * B : (i + 1) * B] = blk.T
    at = at_ref[0]
    window = s_ref[pl.ds(pl.multiple_of(at // 8 * 8, 8), 32), :]
    shift = at % 8
    out = window[:m]
    for k in range(1, 8):
        out = jnp.where(shift == k, window[k : k + m], out)
    out_ref[...] = out


def rows_of(at, core, mine, other, n, m):
    return pl.pallas_call(
        rows_kernel,
        out_shape=jax.ShapeDtypeStruct((m, n), F32),
        in_specs=[SM, SM, VM, VM],
        out_specs=VM,
        scratch_shapes=[pltpu.VMEM((n + 8, n), F32)],
        compiler_params=params(16),
        cost_estimate=cost(3),
        name="rows",
    )(at, core, mine, other)


def per_device(attn_out, out_grad, image_counts, column_owner, damping):
    n_dp = lax.axis_size("dp")
    dp_index = lax.axis_index("dp")
    grp_index = lax.axis_index("grp")
    per_dev, width = attn_out.shape
    block = width // n_dp
    chips = n_dp // 2
    core = dp_index % 2
    chip = dp_index // 2
    nb = width // B
    used = tri(nb, 0) * HALF // SLAB
    per_chip = -(-used // chips)
    same_core = [list(range(c, n_dp, 2)) for c in range(2)]
    swap_core = [(d, d ^ 1) for d in range(n_dp)]
    swap_grp = [(0, 1), (1, 0)]
    core_arr = core.astype(jnp.int32)[None]
    is_a = grp_index == 0

    def keep_of(grp, dp):
        return (lax.dynamic_index_in_dim(image_counts, grp * n_dp + dp, 0, keepdims=False) > 0).astype(F32)

    flip = n_dp // 2
    near = [(g * n_dp + d, (1 - g) * n_dp + d) for g in range(2) for d in range(n_dp)]
    far = [(g * n_dp + d, (1 - g) * n_dp + d ^ flip) for g in range(2) for d in range(n_dp)]
    both = ("grp", "dp")
    half = per_dev // 2

    def swap(rows):
        return lax.ppermute(rows[:half], both, near), lax.ppermute(rows[half:], both, far)

    def to_mate(rows):
        return lax.ppermute(rows, "dp", swap_core)

    first = jnp.where(is_a, attn_out, out_grad)
    second = jnp.where(is_a, out_grad, attn_out)
    from_near, from_far = swap(second)
    mine_rows = [first, to_mate(first), from_near, from_far, to_mate(from_near), to_mate(from_far)]
    first_later, _, _ = lax.optimization_barrier((first, from_near, from_far))
    next_near, next_far = swap(first_later)
    over, mate, away = 1 - grp_index, dp_index ^ 1, dp_index ^ flip
    keeps = jnp.stack([
        keep_of(grp_index, dp_index),
        keep_of(grp_index, mate),
        keep_of(over, dp_index),
        keep_of(over, away),
        keep_of(over, mate),
        keep_of(over, away ^ 1),
    ])
    total = (TOK * jnp.sum(image_counts)).astype(F32)
    part, squares = gram(core_arr, keeps, mine_rows, chips * per_chip)
    part, next_near, next_far = lax.optimization_barrier((part, next_near, next_far))
    other_rows = [second, to_mate(second), next_near, next_far, to_mate(next_near), to_mate(next_far)]
    got = lax.all_to_all(
        part.reshape(chips, per_chip * SLAB, B), "dp", split_axis=0, concat_axis=0, tiled=True, axis_index_groups=same_core
    )
    flat = chip * (per_chip * SLAB) + jnp.arange(per_chip * SLAB)
    t = flat // HALF
    on_diag = jnp.zeros(t.shape, bool)
    for i in range(nb):
        on_diag = on_diag | (t == tri(i, i))
    in_row = core * HALF + flat % HALF
    diag = (on_diag & (flat < used * SLAB))[:, None] & (in_row[:, None] == jnp.arange(B)[None, :])
    damp = jnp.where(is_a, damping[0], damping[1])
    spread, damp_done = damp_and_spread(jnp.stack([total, damp]), got, diag.astype(F32))
    mine = lax.all_to_all(spread, "dp", split_axis=0, concat_axis=0, tiled=True, axis_index_groups=same_core)
    mine = mine.reshape(chips * per_chip * SLAB, B)
    wide = (nb + 2) // 2 * B
    part_w = cross(core_arr, grp_index.astype(jnp.int32)[None], keeps, damp_done, mine_rows, other_rows, chips, wide)
    mine, part_w = lax.optimization_barrier((mine, part_w))
    theirs = lax.ppermute(mine, "dp", swap_core)
    low, chol_done = chol(core_arr, mine, theirs, width)

    got_w = lax.all_to_all(part_w, "dp", split_axis=0, concat_axis=0, tiled=True, axis_index_groups=same_core)

    at = (dp_index * block).astype(jnp.int32)[None]
    my_rows = rows_of(at, core_arr, mine, theirs, width, ROWS)

    order = column_owner.reshape(chips, 2)
    order = jnp.stack([jnp.where(core == 0, order[:, 0], order[:, 1]), jnp.where(core == 0, order[:, 1], order[:, 0])])
    my_w = sum_parts(got_w, chol_done)
    their_w = lax.ppermute(my_w, "grp", [(1, 0)])
    same, cross_t = solve_and_route(order, total[None], my_w, their_w, low, width, block)
    same = lax.ppermute(same, both, [(d, n_dp + d) for d in range(n_dp)])
    cross_t = lax.ppermute(cross_t, both, [(d, n_dp + (d ^ 1)) for d in range(n_dp)])
    is_first = core == 0
    pair = jnp.concatenate([jnp.where(is_first, same, cross_t), jnp.where(is_first, cross_t, same)])
    pair = pair[:, : chips * block].reshape(2 * ROWS, chips, block).transpose(1, 2, 0)
    squares = lax.dynamic_index_in_dim(squares[0].reshape(chips, 2, block), core, 1, keepdims=False)
    pair = jnp.concatenate([pair, squares[:, :, None]], axis=2)
    columns = lax.all_to_all(pair, "dp", split_axis=0, concat_axis=0, tiled=True, axis_index_groups=same_core)
    squares = jnp.sum(columns[:, :, 2 * ROWS], axis=0) / total
    columns = columns[:, :, : 2 * ROWS].transpose(1, 0, 2).reshape(block, n_dp * ROWS)[:, :width]
    columns = jnp.pad(columns, ((0, ROWS - block), (0, 0)))
    left = solve(columns, low, my_rows)[:block]
    here = (dp_index * block + jnp.arange(block))[:, None] == jnp.arange(width)[None, :]
    my_rows = jnp.where(here, squares[:, None], my_rows[:block])
    their_rows = lax.ppermute(my_rows, "grp", swap_grp)
    factors = jnp.stack([jnp.where(is_a, my_rows, their_rows), jnp.where(is_a, their_rows, my_rows)])
    back = lax.ppermute(left, "grp", [(1, 0)])
    preconditioned = jnp.where(is_a, back, left).T
    return (factors, preconditioned)


def solution(mesh):
    placed = (P(("grp", "dp"), None), P(("grp", "dp"), None), P(), P(), P())
    return jax.shard_map(
        per_device,
        mesh=mesh,
        in_specs=placed,
        out_specs=(P(None, "dp", None), P(None, "dp")),
        check_vma=False,
    )
```

```python
import functools

import jax
import jax.numpy as jnp
from jax import lax
from jax.experimental import pallas as pl
from jax.experimental.pallas import tpu as pltpu
from jax.sharding import PartitionSpec as P

TOK = 256
B = 128
HALF = 64
SLAB = 16
ROWS = 24
WIDE = 14336
STEP = 512
REST = 4096
F32 = jnp.float32
BF16 = jnp.bfloat16
NT = (((1,), (1,)), ((), ()))
NN = (((1,), (0,)), ((), ()))
TN = (((0,), (0,)), ((), ()))
VM = pl.BlockSpec(memory_space=pltpu.VMEM)
ANY = pl.BlockSpec(memory_space=pl.ANY)
HBM = pl.BlockSpec(memory_space=pltpu.HBM)
SM = pl.BlockSpec(memory_space=pltpu.SMEM)
TOKEN = jax.ShapeDtypeStruct((8, B), F32)
MIB = 1024 * 1024


def params(mib):
    return pltpu.CompilerParams(vmem_limit_bytes=mib * MIB)


def cost(micros):
    return pl.CostEstimate(flops=int(micros * 1.1e9), bytes_accessed=MIB, transcendentals=0)


def dot(a, b, dims=NT):
    return lax.dot_general(a, b, dims, preferred_element_type=F32)


def split(x):
    hi = x.astype(BF16)
    return hi, (x - hi.astype(F32)).astype(BF16)


def row(x, t):
    return jnp.broadcast_to(x[..., t : t + 1, :], x.shape)


def col(x, c):
    return jnp.broadcast_to(x[..., c : c + 1], x.shape)


def rounded(x):
    return x.astype(BF16).astype(F32)


def tri(i, j):
    return i * (i + 1) // 2 + j


def pieces_of(refs):
    own, mate, near, far, near_mate, far_mate = refs
    return [[(0, own)], [(1, mate)], [(2, near), (3, far)], [(4, near_mate), (5, far_mate)]]


def columns_of(group, cols, keep_ref=None):
    parts = [ref[:, cols] if keep_ref is None else ref[:, cols] * keep_ref[k].astype(BF16) for k, ref in group]
    return parts[0] if len(parts) == 1 else jnp.concatenate(parts, 0)


def gram_kernel(core_ref, keep_ref, *refs):
    pieces, (out_ref, squares_ref, tmp_ref) = pieces_of(refs[:6]), refs[6:]
    nb = refs[0].shape[1] // B
    start = pl.multiple_of(core_ref[0] * HALF, HALF)
    on = lax.broadcasted_iota(jnp.int32, (B, B), 0) == lax.broadcasted_iota(jnp.int32, (B, B), 1)
    used = tri(nb, 0) * HALF
    out_ref[used:, :] = jnp.zeros((out_ref.shape[0] - used, B), F32)
    for i in range(nb):
        wide = (i + 1) * B
        acc = None
        for group in pieces:
            p = dot(columns_of(group, slice(i * B, wide), keep_ref), columns_of(group, slice(0, wide)), TN)
            acc = p if acc is None else acc + p
        tmp_ref[:, :wide] = acc
        diag = jnp.sum(jnp.where(on, acc[:, i * B :], 0.0), axis=0, keepdims=True)
        squares_ref[:, i * B : wide] = jnp.broadcast_to(diag, (8, B))
        for j in range(i + 1):
            t = tri(i, j)
            out_ref[t * HALF : (t + 1) * HALF, :] = tmp_ref[pl.ds(start, HALF), j * B : (j + 1) * B]


def gram(core, keeps, pieces, slots):
    width = pieces[0].shape[1]
    return pl.pallas_call(
        gram_kernel,
        out_shape=(jax.ShapeDtypeStruct((slots * SLAB, B), F32), jax.ShapeDtypeStruct((8, width), F32)),
        in_specs=[SM, SM] + [VM] * 6,
        out_specs=(VM, VM),
        scratch_shapes=[pltpu.VMEM((B, width), F32)],
        compiler_params=params(40),
        cost_estimate=cost(4),
        name="gram",
    )(core, keeps, *pieces)


def cross_kernel(core_ref, grp_ref, keep_ref, after_ref, *refs):
    mine, other, (out_ref, tmp_ref) = pieces_of(refs[:6]), pieces_of(refs[6:12]), refs[12:]
    n = refs[0].shape[1]
    wide = out_ref.shape[2]

    def run(left, right, first):
        for i in range(n // B):
            acc = None
            for lg, rg in zip(left, right):
                p = dot(columns_of(lg, slice(i * B, (i + 1) * B), keep_ref), columns_of(rg, slice(first, first + wide)), TN)
                acc = p if acc is None else acc + p
            tmp_ref[i * B : (i + 1) * B, :] = acc

    pl.when(grp_ref[0] == 0)(lambda: run(other, mine, 0))
    pl.when(grp_ref[0] == 1)(lambda: run(mine, other, n - wide))
    tmp_ref[n:, :] = jnp.zeros((tmp_ref.shape[0] - n, wide), F32)
    for q in range(out_ref.shape[0]):
        out_ref[q] = tmp_ref[pl.ds(pl.multiple_of((2 * q + core_ref[0]) * ROWS, 8), ROWS), :]


def cross(core, grp, keeps, after, mine, other, chips, wide):
    return pl.pallas_call(
        cross_kernel,
        out_shape=jax.ShapeDtypeStruct((chips, ROWS, wide), F32),
        in_specs=[SM, SM, SM, ANY] + [VM] * 12,
        out_specs=VM,
        scratch_shapes=[pltpu.VMEM((2 * chips * ROWS, wide), F32)],
        compiler_params=params(40),
        cost_estimate=cost(30),
        name="cross",
    )(core, grp, keeps, after, *mine, *other)


def factor_diag(block):
    a = [block[8 * i : 8 * i + 8, :] for i in range(16)]
    lane = lax.broadcasted_iota(jnp.int32, (8, B), 1)
    sub = lax.broadcasted_iota(jnp.int32, (8, B), 0)
    x = [(lane == sub + 8 * g).astype(F32) for g in range(16)]
    inv, inv_r = [], []
    cg = [col(a[0], t) for t in range(8)]
    for g in range(16):
        here = (lane >= 8 * g) & (lane < 8 * g + 8)
        v = jnp.where(here, (lane == sub + 8 * g).astype(F32), a[g])
        xg = x[g]
        if g < 15:
            near = a[g + 1]
            cr = [col(near, 8 * g + t) for t in range(8)]
            nxt = [col(near, 8 * g + 8 + t) for t in range(8)]
            near, xr = jnp.where(here, 0.0, near), x[g + 1]
        rs, vs, xs, css = [], [], [], []
        for t in range(8):
            p = row(cg[t], t)
            r = lax.rsqrt(p)
            lt = jnp.where(sub > t, cg[t] * r, 0.0)
            vn = row(v, t) * r
            v = jnp.where(sub == t, vn, v - lt * vn)
            xn = row(xg, t) / rounded(p * r)
            xg = jnp.where(sub == t, xn, xg - rounded(lt) * xn)
            cs = {s: row(cg[s], t) * r for s in range(t + 1, 8)}
            for s in range(t + 1, 8):
                cg[s] = cg[s] - lt * cs[s]
            rs.append(r)
            vs.append(vn)
            xs.append(xn)
            css.append(cs)
            if g < 15:
                lr = cr[t] * r
                for s in range(8):
                    nxt[s] = nxt[s] - lr * row(lr, s)
                near = near - lr * vn
                xr = xr - rounded(lr) * xn
                for s in range(t + 1, 8):
                    cr[s] = cr[s] - lr * cs[s]
        inv.append(jnp.where(lane <= sub + 8 * g, v, 0.0))
        inv_r.append(xg)
        if g < 15:
            a[g + 1], x[g + 1] = near, xr
            cg = nxt
        for i in range(g + 2, 16):
            c = [col(a[i], 8 * g + t) for t in range(8)]
            ai, xi = jnp.where(here, 0.0, a[i]), x[i]
            for t in range(8):
                l = c[t] * rs[t]
                ai = ai - l * vs[t]
                xi = xi - rounded(l) * xs[t]
                for s in range(t + 1, 8):
                    c[s] = c[s] - l * css[t][s]
            a[i], x[i] = ai, xi
    return jnp.concatenate(inv, 0), jnp.concatenate(inv_r, 0)


def block_of(mine_ref, other_ref, first, i, j):
    t = tri(i, j) * HALF
    mine = mine_ref[t : t + HALF, :].astype(F32)
    other = other_ref[t : t + HALF, :].astype(F32)
    return jnp.concatenate([jnp.where(first, mine, other), jnp.where(first, other, mine)], 0)


def join_inverses(low_of, inv_ref, iv_ref, first, last):
    iv_ref[...] = jnp.zeros_like(iv_ref)
    for b in range(first, last, B):
        at = b % STEP
        iv_ref[b - first : b - first + B, at : at + B] = inv_ref[b - first : b - first + B, :]
    size = B
    while size < STEP:
        for r0 in range(first, last - size, 2 * size):
            r1 = r0 + size
            r2 = min(r1 + size, last)
            at = r0 % STEP
            i0, i1, i2 = r0 - first, r1 - first, r2 - first
            left = jnp.concatenate(split(iv_ref[i0:i1, at : at + size]), 1)
            p = dot(low_of(slice(r1, r2), slice(r0, r1)), left, NN)
            phi, plo = split(p[:, :size] + p[:, size:])
            bhi, blo = split(iv_ref[i1:i2, at + size : at + size + r2 - r1])
            iv_ref[i1:i2, at : at + size] = -(dot(bhi, phi, NN) + dot(bhi, plo, NN) + dot(blo, phi, NN))
        size *= 2


def keep_blocks(mine_ref, other_ref, low_hbm, sem, back):
    n = low_hbm.shape[0]
    copies = []
    for half, ref in enumerate((mine_ref, other_ref)):
        total = ref.shape[0]
        for p in range(-(-total // n)):
            rows = min(n, total - p * n)
            at = n + 2 * STEP + (4 * half + p) * B
            here, there = ref.at[p * n : p * n + rows], low_hbm.at[:rows, at : at + B]
            k = len(copies)
            copies.append(pltpu.make_async_copy(*((there, here) if back else (here, there)), sem.at[k]))
    for copy in copies:
        copy.start()
    return copies


def halves_of(x):
    return jnp.concatenate(split(x), 1)


def block_of(mine_ref, other_ref, first, i, j):
    t = tri(i, j) * HALF
    mine = mine_ref[t : t + HALF, :].astype(F32)
    other = other_ref[t : t + HALF, :].astype(F32)
    return jnp.concatenate([jnp.where(first, mine, other), jnp.where(first, other, mine)], 0)


def factor_steps(first, last, nb, base, block, low_ref, lo_ref, inv_ref, s_ref, w_ref, each):
    def update(kk):
        r0 = kk * B
        at = r0 - base
        s = jnp.concatenate([block(i, kk) for i in range(kk, nb)], 0)
        if kk:
            wts = jnp.concatenate([low_ref[at : at + B, :r0], lo_ref[at : at + B, :r0]], 0)
            pr = dot(low_ref[at:, :r0], wts)
            s = s - (pr[:, :B] + pr[:, B:] + dot(lo_ref[at:, :r0], low_ref[at : at + B, :r0]))
        s_ref[at:, :] = s

    def panel(kk):
        r0 = kk * B
        r1 = r0 + B
        at = r1 - base
        shi, slo = split(s_ref[at:, :])
        pr = dot(shi, w_ref[...])
        lp = pr[:, :B] + pr[:, B:] + dot(slo, w_ref[:B, :])
        hi, lo = split(lp)
        low_ref[at:, r0:r1] = hi
        lo_ref[at:, r0:r1] = lo

    def step(k, _):
        for kk in range(first, last):
            pl.when(k == kk)(lambda kk=kk: update(kk))
        rows = pl.ds(pl.multiple_of(k * B - base, B), B)
        each(k, rows)
        linv, lrinv = factor_diag(s_ref[rows, :])
        inv_ref[rows, :] = lrinv
        hi, lo = split(linv)
        w_ref[:B, :] = hi
        w_ref[B:, :] = lo
        for kk in range(first, min(last, nb - 1)):
            pl.when(k == kk)(lambda kk=kk: panel(kk))
        return 0

    lax.fori_loop(first, last, step, 0)


def chol_kernel(
    cut, core_ref, mine_ref, other_ref, low_hbm, tail_s_ref, tail_inv_ref, done_ref,
    low_ref, lo_ref, inv_ref, s_ref, w_ref, iv_ref, hl_ref, sem, keep_sem,
):
    done_ref[...] = jnp.zeros_like(done_ref)
    kept = keep_blocks(mine_ref, other_ref, low_hbm, keep_sem, False)
    n = low_ref.shape[0]
    nb = n // B
    first = core_ref[0] == 0
    whole = cut * B // STEP * STEP

    def row_copy(k, rows):
        return pltpu.make_async_copy(low_ref.at[rows], low_hbm.at[rows, :n], sem.at[k])

    factor_steps(
        0, cut, nb, 0, functools.partial(block_of, mine_ref, other_ref, first), low_ref, lo_ref, inv_ref, s_ref, w_ref,
        lambda k, rows: row_copy(k, rows).start(),
    )
    join_inverses(lambda rows, cols: low_ref[rows, cols], inv_ref, iv_ref, 0, whole)
    hl_ref[...] = halves_of(iv_ref[...])
    last = pltpu.make_async_copy(hl_ref, low_hbm.at[:whole, n : n + 2 * STEP], sem.at[cut])
    last.start()
    rest = [
        pltpu.make_async_copy(low_ref.at[cut * B :], low_hbm.at[cut * B : n, :n], keep_sem.at[8]),
        pltpu.make_async_copy(lo_ref.at[cut * B :], low_hbm.at[cut * B : n, REST : REST + n], keep_sem.at[9]),
    ]
    for copy in rest:
        copy.start()
    tail_inv_ref[...] = inv_ref[whole : cut * B, :]
    for i in range(cut, nb):
        for j in range(cut, i + 1):
            at = (slice((i - cut) * B, (i - cut + 1) * B), slice((j - cut) * B, (j - cut + 1) * B))
            tail_s_ref[at] = block_of(mine_ref, other_ref, first, i, j)
    for k in range(cut):
        row_copy(k, slice(k * B, (k + 1) * B)).wait()
    for copy in [last, *rest, *kept]:
        copy.wait()


def chol_tail_kernel(
    cut, n, tail_s_ref, tail_inv_ref, in_hbm, low_hbm,
    low_ref, lo_ref, inv_ref, s_ref, w_ref, iv_ref, hl_ref, sem,
):
    whole = cut * B // STEP * STEP
    skip = cut * B - whole
    loads = [
        pltpu.make_async_copy(in_hbm.at[whole:n, :n], low_ref, sem.at[0]),
        pltpu.make_async_copy(in_hbm.at[cut * B : n, REST : REST + n], lo_ref.at[skip:], sem.at[1]),
    ]
    for copy in loads:
        copy.start()
    for copy in loads:
        copy.wait()
    inv_ref[:skip, :] = tail_inv_ref[...]

    def block(i, j):
        return tail_s_ref[(i - cut) * B : (i - cut + 1) * B, (j - cut) * B : (j - cut + 1) * B]

    factor_steps(cut, n // B, n // B, whole, block, low_ref, lo_ref, inv_ref, s_ref, w_ref, lambda k, rows: None)
    join_inverses(lambda rows, cols: low_ref[rows.start - whole : rows.stop - whole, cols], inv_ref, iv_ref, whole, n)
    hl_ref[...] = halves_of(iv_ref[...])
    copies = [
        pltpu.make_async_copy(low_ref, low_hbm.at[whole:n, :n], sem.at[0]),
        pltpu.make_async_copy(hl_ref, low_hbm.at[whole:n, n : n + 2 * STEP], sem.at[1]),
    ]
    for copy in copies:
        copy.start()
    for copy in copies:
        copy.wait()


def chol(core, mine, other, n, cut):
    whole = cut * B // STEP * STEP
    left = n - cut * B
    return pl.pallas_call(
        functools.partial(chol_kernel, cut),
        out_shape=(
            jax.ShapeDtypeStruct((n, WIDE), BF16),
            jax.ShapeDtypeStruct((left, left), F32),
            jax.ShapeDtypeStruct((cut * B - whole, B), F32),
            TOKEN,
        ),
        in_specs=[SM, VM, VM],
        out_specs=(HBM, VM, VM, VM),
        scratch_shapes=[
            pltpu.VMEM((n, n), BF16),
            pltpu.VMEM((n, n), BF16),
            pltpu.VMEM((n, B), F32),
            pltpu.VMEM((n, B), F32),
            pltpu.VMEM((2 * B, B), BF16),
            pltpu.VMEM((whole, STEP), F32),
            pltpu.VMEM((whole, 2 * STEP), BF16),
            pltpu.SemaphoreType.DMA((cut + 1,)),
            pltpu.SemaphoreType.DMA((10,)),
        ],
        compiler_params=params(28),
        cost_estimate=cost(39),
        name="cholesky",
    )(core, mine, other)


def chol_tail(tail, low, n, cut):
    rows = n - cut * B // STEP * STEP
    return pl.pallas_call(
        functools.partial(chol_tail_kernel, cut, n),
        out_shape=jax.ShapeDtypeStruct(low.shape, BF16),
        in_specs=[VM, VM, HBM],
        out_specs=HBM,
        input_output_aliases={2: 0},
        scratch_shapes=[
            pltpu.VMEM((rows, n), BF16),
            pltpu.VMEM((rows, n), BF16),
            pltpu.VMEM((rows, B), F32),
            pltpu.VMEM((rows, B), F32),
            pltpu.VMEM((2 * B, B), BF16),
            pltpu.VMEM((rows, STEP), F32),
            pltpu.VMEM((rows, 2 * STEP), BF16),
            pltpu.SemaphoreType.DMA((2,)),
        ],
        compiler_params=params(28),
        cost_estimate=cost(9),
        name="cholesky_tail",
    )(*tail, low)


def solve_into(rhs, m, n, low_hbm, out_ref, low_ref, hl_ref, sem):
    starts = list(range(0, n, STEP))
    loads = []
    for r0 in starts:
        rows = slice(r0, min(r0 + STEP, n))
        if r0:
            loads.append((low_hbm.at[rows, :r0], low_ref.at[rows, :r0]))
        loads.append((low_hbm.at[rows, n : n + 2 * STEP], hl_ref.at[rows]))
    copies = [pltpu.make_async_copy(src, dst, sem.at[k]) for k, (src, dst) in enumerate(loads)]
    for copy in copies:
        copy.start()

    def stacked(x):
        return jnp.concatenate(split(x), 0)

    def fold(p):
        return p[:m] + p[m:]

    def inverted(x, rows, dims):
        w = rows.stop - rows.start
        xs = stacked(x)
        return fold(dot(xs, hl_ref[rows, :w], dims) + dot(xs, hl_ref[rows, STEP : STEP + w], dims))

    parts = [slice(r0, min(r0 + STEP, n)) for r0 in starts]
    acc = []
    for rows in parts:
        s = rhs(rows)
        for done, y in zip(parts, acc):
            if done is parts[0]:
                copies.pop(0).wait()
            s = s - fold(dot(stacked(y), low_ref[rows, done]))
        copies.pop(0).wait()
        acc.append(inverted(s, rows, NT))
    for k in reversed(range(len(parts))):
        z = inverted(acc[k], parts[k], NN)
        out_ref[:, parts[k]] = z
        zs = stacked(z)
        for c in range(k):
            acc[c] = acc[c] - fold(dot(zs, low_ref[parts[k], parts[c]], NN))


def solve_scratch(n):
    return [pltpu.VMEM((n, n), BF16), pltpu.VMEM((n, 2 * STEP), BF16), pltpu.SemaphoreType.DMA((2 * -(-n // STEP) - 1,))]


def solve_kernel(rhs_ref, low_ref, after_ref, out_ref, *scratch):
    m, n = rhs_ref.shape
    solve_into(lambda cols: rhs_ref[:, cols], m, n, low_ref, out_ref, *scratch)


def solve(rhs, low, after):
    return pl.pallas_call(
        solve_kernel,
        out_shape=jax.ShapeDtypeStruct(rhs.shape, F32),
        in_specs=[VM, HBM, ANY],
        out_specs=VM,
        scratch_shapes=solve_scratch(rhs.shape[1]),
        compiler_params=params(16),
        cost_estimate=cost(7),
        name="solve",
    )(rhs, low, after)


def route_kernel(block, owner_ref, total_ref, one_ref, two_ref, low_ref, same_ref, cross_ref, t_ref, r_ref, *scratch):
    m, wide = one_ref.shape
    n = t_ref.shape[1] - B
    right = jnp.concatenate([one_ref[...], two_ref[:, 2 * wide - n :]], 1) / total_ref[0]

    def rhs(cols):
        return right[:, cols]

    solve_into(rhs, m, n, low_ref, t_ref, *scratch)
    t_ref[:, n:] = jnp.zeros((m, t_ref.shape[1] - n), F32)
    lane = lax.broadcasted_iota(jnp.int32, (m, 2 * B), 1)
    for h, out_ref in enumerate((same_ref, cross_ref)):
        for q in range(owner_ref.shape[1]):
            to, off = block * q // B * B, block * q % B
            src = owner_ref[h, q] * block
            win = t_ref[:, pl.ds(pl.multiple_of(src // B * B, B), 2 * B)]
            win = pltpu.roll(win, (off + 2 * B - src % B) % (2 * B), 1)
            old = r_ref[:, to : to + 2 * B]
            r_ref[:, to : to + 2 * B] = jnp.where((lane >= off) & (lane < off + block), win, old)
        out_ref[...] = r_ref[:, : out_ref.shape[1]]


def solve_and_route(owner, total, one, two, low, n, block):
    m = one.shape[0]
    wide = -(-owner.shape[1] * block // B) * B
    out = jax.ShapeDtypeStruct((m, wide), F32)
    return pl.pallas_call(
        functools.partial(route_kernel, block),
        out_shape=(out, out),
        in_specs=[SM, SM, VM, VM, HBM],
        out_specs=(VM, VM),
        scratch_shapes=[pltpu.VMEM((m, n + B), F32), pltpu.VMEM((m, wide + B), F32)] + solve_scratch(n),
        compiler_params=params(16),
        cost_estimate=cost(9),
        name="solve_and_route",
    )(owner, total, one, two, low)


def sum_kernel(parts_ref, *refs):
    out_ref = refs[-1]
    acc = parts_ref[0]
    for k in range(1, parts_ref.shape[0]):
        acc = acc + parts_ref[k]
    out_ref[...] = acc


def damp_kernel(scale_ref, parts_ref, diag_ref, out_ref, done_ref, sum_ref, sem):
    acc = parts_ref[0]
    for k in range(1, parts_ref.shape[0]):
        acc = acc + parts_ref[k]
    sum_ref[...] = (acc / scale_ref[0] + scale_ref[1] * diag_ref[...]).astype(BF16)
    copies = [pltpu.make_async_copy(sum_ref, out_ref.at[k], sem.at[k]) for k in range(out_ref.shape[0])]
    for copy in copies:
        copy.start()
    done_ref[...] = jnp.zeros_like(done_ref)
    for copy in copies:
        copy.wait()


def damp_and_spread(scale, parts, diag):
    chips = parts.shape[0]
    return pl.pallas_call(
        damp_kernel,
        out_shape=(jax.ShapeDtypeStruct(parts.shape, BF16), TOKEN),
        in_specs=[SM, VM, VM],
        out_specs=(HBM, VM),
        scratch_shapes=[pltpu.VMEM(parts.shape[1:], BF16), pltpu.SemaphoreType.DMA((chips,))],
        compiler_params=params(60),
        cost_estimate=cost(3),
        name="damp_and_spread",
    )(scale, parts, diag)


def sum_parts(parts, *after):
    return pl.pallas_call(
        sum_kernel,
        out_shape=jax.ShapeDtypeStruct(parts.shape[1:], F32),
        in_specs=[VM] + [ANY] * len(after),
        out_specs=VM,
        compiler_params=params(16),
        cost_estimate=cost(3),
        name="sum_parts",
    )(parts, *after)


def rows_kernel(at_ref, core_ref, low_hbm, out_ref, s_ref, mine_ref, other_ref, sem):
    for copy in keep_blocks(mine_ref, other_ref, low_hbm, sem, True):
        copy.wait()
    m, n = out_ref.shape
    nb = n // B
    first = core_ref[0] == 0
    for i in range(nb):
        for j in range(i + 1):
            blk = block_of(mine_ref, other_ref, first, i, j)
            s_ref[i * B : (i + 1) * B, j * B : (j + 1) * B] = blk
            if i > j:
                s_ref[j * B : (j + 1) * B, i * B : (i + 1) * B] = blk.T
    at = at_ref[0]
    window = s_ref[pl.ds(pl.multiple_of(at // 8 * 8, 8), 32), :]
    shift = at % 8
    out = window[:m]
    for k in range(1, 8):
        out = jnp.where(shift == k, window[k : k + m], out)
    out_ref[...] = out


def rows_of(at, core, low, n, m, rows):
    return pl.pallas_call(
        rows_kernel,
        out_shape=jax.ShapeDtypeStruct((m, n), F32),
        in_specs=[SM, SM, HBM],
        out_specs=VM,
        scratch_shapes=[
            pltpu.VMEM((n + 8, n), F32),
            pltpu.VMEM((rows, B), BF16),
            pltpu.VMEM((rows, B), BF16),
            pltpu.SemaphoreType.DMA((8,)),
        ],
        compiler_params=params(20),
        cost_estimate=cost(3),
        name="rows",
    )(at, core, low)


def per_device(attn_out, out_grad, image_counts, column_owner, damping):
    n_dp = lax.axis_size("dp")
    dp_index = lax.axis_index("dp")
    grp_index = lax.axis_index("grp")
    per_dev, width = attn_out.shape
    block = width // n_dp
    chips = n_dp // 2
    core = dp_index % 2
    chip = dp_index // 2
    nb = width // B
    used = tri(nb, 0) * HALF // SLAB
    per_chip = -(-used // chips)
    same_core = [list(range(c, n_dp, 2)) for c in range(2)]
    swap_core = [(d, d ^ 1) for d in range(n_dp)]
    swap_grp = [(0, 1), (1, 0)]
    core_arr = core.astype(jnp.int32)[None]
    is_a = grp_index == 0

    def keep_of(grp, dp):
        return (lax.dynamic_index_in_dim(image_counts, grp * n_dp + dp, 0, keepdims=False) > 0).astype(F32)

    flip = n_dp // 2
    near = [(g * n_dp + d, (1 - g) * n_dp + d) for g in range(2) for d in range(n_dp)]
    far = [(g * n_dp + d, (1 - g) * n_dp + d ^ flip) for g in range(2) for d in range(n_dp)]
    both = ("grp", "dp")
    half = per_dev // 2

    def swap(rows):
        return lax.ppermute(rows[:half], both, near), lax.ppermute(rows[half:], both, far)

    def to_mate(rows):
        return lax.ppermute(rows, "dp", swap_core)

    first = jnp.where(is_a, attn_out, out_grad)
    second = jnp.where(is_a, out_grad, attn_out)
    from_near, from_far = swap(second)
    mine_rows = [first, to_mate(first), from_near, from_far, to_mate(from_near), to_mate(from_far)]
    first_later, _, _ = lax.optimization_barrier((first, from_near, from_far))
    next_near, next_far = swap(first_later)
    over, mate, away = 1 - grp_index, dp_index ^ 1, dp_index ^ flip
    keeps = jnp.stack([
        keep_of(grp_index, dp_index),
        keep_of(grp_index, mate),
        keep_of(over, dp_index),
        keep_of(over, away),
        keep_of(over, mate),
        keep_of(over, away ^ 1),
    ])
    total = (TOK * jnp.sum(image_counts)).astype(F32)
    part, squares = gram(core_arr, keeps, mine_rows, chips * per_chip)
    part, next_near, next_far = lax.optimization_barrier((part, next_near, next_far))
    other_rows = [second, to_mate(second), next_near, next_far, to_mate(next_near), to_mate(next_far)]
    got = lax.all_to_all(
        part.reshape(chips, per_chip * SLAB, B), "dp", split_axis=0, concat_axis=0, tiled=True, axis_index_groups=same_core
    )
    flat = chip * (per_chip * SLAB) + jnp.arange(per_chip * SLAB)
    t = flat // HALF
    on_diag = jnp.zeros(t.shape, bool)
    for i in range(nb):
        on_diag = on_diag | (t == tri(i, i))
    in_row = core * HALF + flat % HALF
    diag = (on_diag & (flat < used * SLAB))[:, None] & (in_row[:, None] == jnp.arange(B)[None, :])
    damp = jnp.where(is_a, damping[0], damping[1])
    spread, damp_done = damp_and_spread(jnp.stack([total, damp]), got, diag.astype(F32))
    mine = lax.all_to_all(spread, "dp", split_axis=0, concat_axis=0, tiled=True, axis_index_groups=same_core)
    mine = mine.reshape(chips * per_chip * SLAB, B)
    wide = (nb + 2) // 2 * B
    part_w = cross(core_arr, grp_index.astype(jnp.int32)[None], keeps, damp_done, mine_rows, other_rows, chips, wide)
    mine, part_w = lax.optimization_barrier((mine, part_w))
    theirs = lax.ppermute(mine, "dp", swap_core)
    cut = nb - 2
    low, *tail, chol_done = chol(core_arr, mine, theirs, width, cut)

    got_w = lax.all_to_all(part_w, "dp", split_axis=0, concat_axis=0, tiled=True, axis_index_groups=same_core)

    at = (dp_index * block).astype(jnp.int32)[None]

    order = column_owner.reshape(chips, 2)
    order = jnp.stack([jnp.where(core == 0, order[:, 0], order[:, 1]), jnp.where(core == 0, order[:, 1], order[:, 0])])
    my_w = sum_parts(got_w, chol_done)
    their_w = lax.ppermute(my_w, "grp", [(1, 0)])
    low = chol_tail(tail, low, width, cut)
    my_rows = rows_of(at, core_arr, low, width, ROWS, mine.shape[0])
    same, cross_t = solve_and_route(order, total[None], my_w, their_w, low, width, block)
    same = lax.ppermute(same, both, [(d, n_dp + d) for d in range(n_dp)])
    cross_t = lax.ppermute(cross_t, both, [(d, n_dp + (d ^ 1)) for d in range(n_dp)])
    is_first = core == 0
    pair = jnp.concatenate([jnp.where(is_first, same, cross_t), jnp.where(is_first, cross_t, same)])
    pair = pair[:, : chips * block].reshape(2 * ROWS, chips, block).transpose(1, 2, 0)
    squares = lax.dynamic_index_in_dim(squares[0].reshape(chips, 2, block), core, 1, keepdims=False)
    pair = jnp.concatenate([pair, squares[:, :, None]], axis=2)
    columns = lax.all_to_all(pair, "dp", split_axis=0, concat_axis=0, tiled=True, axis_index_groups=same_core)
    squares = jnp.sum(columns[:, :, 2 * ROWS], axis=0) / total
    columns = columns[:, :, : 2 * ROWS].transpose(1, 0, 2).reshape(block, n_dp * ROWS)[:, :width]
    columns = jnp.pad(columns, ((0, ROWS - block), (0, 0)))
    left = solve(columns, low, my_rows)[:block]
    here = (dp_index * block + jnp.arange(block))[:, None] == jnp.arange(width)[None, :]
    my_rows = jnp.where(here, squares[:, None], my_rows[:block])
    their_rows = lax.ppermute(my_rows, "grp", swap_grp)
    factors = jnp.stack([jnp.where(is_a, my_rows, their_rows), jnp.where(is_a, their_rows, my_rows)])
    back = lax.ppermute(left, "grp", [(1, 0)])
    preconditioned = jnp.where(is_a, back, left).T
    return (factors, preconditioned)


def solution(mesh):
    placed = (P(("grp", "dp"), None), P(("grp", "dp"), None), P(), P(), P())
    return jax.shard_map(
        per_device,
        mesh=mesh,
        in_specs=placed,
        out_specs=(P(None, "dp", None), P(None, "dp")),
        check_vma=False,
    )
```

```python
import functools

import jax
import jax.numpy as jnp
from jax import lax
from jax.experimental import pallas as pl
from jax.experimental.pallas import tpu as pltpu
from jax.sharding import PartitionSpec as P

TOK = 256
B = 128
HALF = 64
SLAB = 16
ROWS = 24
WIDE = 14336
STEP = 512
REST = 4096
MORE = 8192
F32 = jnp.float32
BF16 = jnp.bfloat16
NT = (((1,), (1,)), ((), ()))
NN = (((1,), (0,)), ((), ()))
TN = (((0,), (0,)), ((), ()))
VM = pl.BlockSpec(memory_space=pltpu.VMEM)
ANY = pl.BlockSpec(memory_space=pl.ANY)
HBM = pl.BlockSpec(memory_space=pltpu.HBM)
SM = pl.BlockSpec(memory_space=pltpu.SMEM)
TOKEN = jax.ShapeDtypeStruct((8, B), F32)
MIB = 1024 * 1024


def params(mib):
    return pltpu.CompilerParams(vmem_limit_bytes=mib * MIB)


def cost(micros):
    return pl.CostEstimate(flops=int(micros * 1.1e9), bytes_accessed=MIB, transcendentals=0)


def dot(a, b, dims=NT):
    return lax.dot_general(a, b, dims, preferred_element_type=F32)


def split(x):
    hi = x.astype(BF16)
    return hi, (x - hi.astype(F32)).astype(BF16)


def row(x, t):
    return jnp.broadcast_to(x[..., t : t + 1, :], x.shape)


def col(x, c):
    return jnp.broadcast_to(x[..., c : c + 1], x.shape)


def rounded(x):
    return x.astype(BF16).astype(F32)


def tri(i, j):
    return i * (i + 1) // 2 + j


def pieces_of(refs):
    own, mate, near, far, near_mate, far_mate = refs
    return [[(0, own)], [(1, mate)], [(2, near), (3, far)], [(4, near_mate), (5, far_mate)]]


def columns_of(group, cols, keep_ref=None):
    parts = [ref[:, cols] if keep_ref is None else ref[:, cols] * keep_ref[k].astype(BF16) for k, ref in group]
    return parts[0] if len(parts) == 1 else jnp.concatenate(parts, 0)


def gram_kernel(core_ref, keep_ref, *refs):
    pieces, (out_ref, squares_ref, tmp_ref) = pieces_of(refs[:6]), refs[6:]
    nb = refs[0].shape[1] // B
    start = pl.multiple_of(core_ref[0] * HALF, HALF)
    on = lax.broadcasted_iota(jnp.int32, (B, B), 0) == lax.broadcasted_iota(jnp.int32, (B, B), 1)
    used = tri(nb, 0) * HALF
    out_ref[used:, :] = jnp.zeros((out_ref.shape[0] - used, B), F32)
    for i in range(nb):
        wide = (i + 1) * B
        acc = None
        for group in pieces:
            p = dot(columns_of(group, slice(i * B, wide), keep_ref), columns_of(group, slice(0, wide)), TN)
            acc = p if acc is None else acc + p
        tmp_ref[:, :wide] = acc
        diag = jnp.sum(jnp.where(on, acc[:, i * B :], 0.0), axis=0, keepdims=True)
        squares_ref[:, i * B : wide] = jnp.broadcast_to(diag, (8, B))
        for j in range(i + 1):
            t = tri(i, j)
            out_ref[t * HALF : (t + 1) * HALF, :] = tmp_ref[pl.ds(start, HALF), j * B : (j + 1) * B]


def gram(core, keeps, pieces, slots):
    width = pieces[0].shape[1]
    return pl.pallas_call(
        gram_kernel,
        out_shape=(jax.ShapeDtypeStruct((slots * SLAB, B), F32), jax.ShapeDtypeStruct((8, width), F32)),
        in_specs=[SM, SM] + [VM] * 6,
        out_specs=(VM, VM),
        scratch_shapes=[pltpu.VMEM((B, width), F32)],
        compiler_params=params(40),
        cost_estimate=cost(4),
        name="gram",
    )(core, keeps, *pieces)


def cross_kernel(core_ref, grp_ref, keep_ref, after_ref, *refs):
    mine, other, (out_ref, tmp_ref) = pieces_of(refs[:6]), pieces_of(refs[6:12]), refs[12:]
    n = refs[0].shape[1]
    wide = out_ref.shape[2]

    def run(left, right, first):
        for i in range(n // B):
            acc = None
            for lg, rg in zip(left, right):
                p = dot(columns_of(lg, slice(i * B, (i + 1) * B), keep_ref), columns_of(rg, slice(first, first + wide)), TN)
                acc = p if acc is None else acc + p
            tmp_ref[i * B : (i + 1) * B, :] = acc

    pl.when(grp_ref[0] == 0)(lambda: run(other, mine, 0))
    pl.when(grp_ref[0] == 1)(lambda: run(mine, other, n - wide))
    tmp_ref[n:, :] = jnp.zeros((tmp_ref.shape[0] - n, wide), F32)
    for q in range(out_ref.shape[0]):
        out_ref[q] = tmp_ref[pl.ds(pl.multiple_of((2 * q + core_ref[0]) * ROWS, 8), ROWS), :]


def cross(core, grp, keeps, after, mine, other, chips, wide):
    return pl.pallas_call(
        cross_kernel,
        out_shape=jax.ShapeDtypeStruct((chips, ROWS, wide), F32),
        in_specs=[SM, SM, SM, ANY] + [VM] * 12,
        out_specs=VM,
        scratch_shapes=[pltpu.VMEM((2 * chips * ROWS, wide), F32)],
        compiler_params=params(40),
        cost_estimate=cost(30),
        name="cross",
    )(core, grp, keeps, after, *mine, *other)


def factor_diag(block):
    a = [block[8 * i : 8 * i + 8, :] for i in range(16)]
    lane = lax.broadcasted_iota(jnp.int32, (8, B), 1)
    sub = lax.broadcasted_iota(jnp.int32, (8, B), 0)
    x = [(lane == sub + 8 * g).astype(F32) for g in range(16)]
    inv, inv_r = [], []
    cg = [col(a[0], t) for t in range(8)]
    for g in range(16):
        here = (lane >= 8 * g) & (lane < 8 * g + 8)
        v = jnp.where(here, (lane == sub + 8 * g).astype(F32), a[g])
        xg = x[g]
        if g < 15:
            near = a[g + 1]
            cr = [col(near, 8 * g + t) for t in range(8)]
            nxt = [col(near, 8 * g + 8 + t) for t in range(8)]
            near, xr = jnp.where(here, 0.0, near), x[g + 1]
        rs, vs, xs, css = [], [], [], []
        for t in range(8):
            p = row(cg[t], t)
            r = lax.rsqrt(p)
            lt = jnp.where(sub > t, cg[t] * r, 0.0)
            vn = row(v, t) * r
            v = jnp.where(sub == t, vn, v - lt * vn)
            xn = row(xg, t) / rounded(p * r)
            xg = jnp.where(sub == t, xn, xg - rounded(lt) * xn)
            cs = {s: row(cg[s], t) * r for s in range(t + 1, 8)}
            for s in range(t + 1, 8):
                cg[s] = cg[s] - lt * cs[s]
            rs.append(r)
            vs.append(vn)
            xs.append(xn)
            css.append(cs)
            if g < 15:
                lr = cr[t] * r
                for s in range(8):
                    nxt[s] = nxt[s] - lr * row(lr, s)
                near = near - lr * vn
                xr = xr - rounded(lr) * xn
                for s in range(t + 1, 8):
                    cr[s] = cr[s] - lr * cs[s]
        inv.append(jnp.where(lane <= sub + 8 * g, v, 0.0))
        inv_r.append(xg)
        if g < 15:
            a[g + 1], x[g + 1] = near, xr
            cg = nxt
        for i in range(g + 2, 16):
            c = [col(a[i], 8 * g + t) for t in range(8)]
            ai, xi = jnp.where(here, 0.0, a[i]), x[i]
            for t in range(8):
                l = c[t] * rs[t]
                ai = ai - l * vs[t]
                xi = xi - rounded(l) * xs[t]
                for s in range(t + 1, 8):
                    c[s] = c[s] - l * css[t][s]
            a[i], x[i] = ai, xi
    return jnp.concatenate(inv, 0), jnp.concatenate(inv_r, 0)


def block_of(mine_ref, other_ref, first, i, j):
    t = tri(i, j) * HALF
    mine = mine_ref[t : t + HALF, :].astype(F32)
    other = other_ref[t : t + HALF, :].astype(F32)
    return jnp.concatenate([jnp.where(first, mine, other), jnp.where(first, other, mine)], 0)


def join_inverses(low_of, inv_ref, iv_ref, first, last):
    iv_ref[...] = jnp.zeros_like(iv_ref)
    for b in range(first, last, B):
        at = b % STEP
        iv_ref[b - first : b - first + B, at : at + B] = inv_ref[b - first : b - first + B, :]
    size = B
    while size < STEP:
        for r0 in range(first, last - size, 2 * size):
            r1 = r0 + size
            r2 = min(r1 + size, last)
            at = r0 % STEP
            i0, i1, i2 = r0 - first, r1 - first, r2 - first
            left = jnp.concatenate(split(iv_ref[i0:i1, at : at + size]), 1)
            p = dot(low_of(slice(r1, r2), slice(r0, r1)), left, NN)
            phi, plo = split(p[:, :size] + p[:, size:])
            bhi, blo = split(iv_ref[i1:i2, at + size : at + size + r2 - r1])
            iv_ref[i1:i2, at : at + size] = -(dot(bhi, phi, NN) + dot(bhi, plo, NN) + dot(blo, phi, NN))
        size *= 2


def halves_of(x):
    return jnp.concatenate(split(x), 1)


def block_of(mine_ref, other_ref, first, i, j):
    t = tri(i, j) * HALF
    mine = mine_ref[t : t + HALF, :].astype(F32)
    other = other_ref[t : t + HALF, :].astype(F32)
    return jnp.concatenate([jnp.where(first, mine, other), jnp.where(first, other, mine)], 0)


def factor_steps(first, last, nb, base, block, low_ref, lo_ref, inv_ref, s_ref, w_ref, each):
    def update(kk):
        r0 = kk * B
        at = r0 - base
        s = jnp.concatenate([block(i, kk) for i in range(kk, nb)], 0)
        if kk:
            wts = jnp.concatenate([low_ref[at : at + B, :r0], lo_ref[at : at + B, :r0]], 0)
            pr = dot(low_ref[at:, :r0], wts)
            s = s - (pr[:, :B] + pr[:, B:] + dot(lo_ref[at:, :r0], low_ref[at : at + B, :r0]))
        s_ref[at:, :] = s

    def panel(kk):
        r0 = kk * B
        r1 = r0 + B
        at = r1 - base
        shi, slo = split(s_ref[at:, :])
        pr = dot(shi, w_ref[...])
        lp = pr[:, :B] + pr[:, B:] + dot(slo, w_ref[:B, :])
        hi, lo = split(lp)
        low_ref[at:, r0:r1] = hi
        lo_ref[at:, r0:r1] = lo

    def step(k, _):
        for kk in range(first, last):
            pl.when(k == kk)(lambda kk=kk: update(kk))
        rows = pl.ds(pl.multiple_of(k * B - base, B), B)
        each(k, rows)
        linv, lrinv = factor_diag(s_ref[rows, :])
        inv_ref[rows, :] = lrinv
        hi, lo = split(linv)
        w_ref[:B, :] = hi
        w_ref[B:, :] = lo
        for kk in range(first, min(last, nb - 1)):
            pl.when(k == kk)(lambda kk=kk: panel(kk))
        return 0

    lax.fori_loop(first, last, step, 0)


def chol_kernel(
    cut, core_ref, mine_ref, other_ref, low_hbm, done_ref,
    low_ref, lo_ref, inv_ref, s_ref, w_ref, iv_ref, hl_ref, more_ref, sem, rest_sem,
):
    done_ref[...] = jnp.zeros_like(done_ref)
    n = low_ref.shape[0]
    nb = n // B
    first = core_ref[0] == 0
    whole = cut * B // STEP * STEP

    def row_copy(k, rows):
        return pltpu.make_async_copy(low_ref.at[rows], low_hbm.at[rows, :n], sem.at[k])

    factor_steps(
        0, cut, nb, 0, functools.partial(block_of, mine_ref, other_ref, first), low_ref, lo_ref, inv_ref, s_ref, w_ref,
        lambda k, rows: row_copy(k, rows).start(),
    )
    join_inverses(lambda rows, cols: low_ref[rows, cols], inv_ref, iv_ref, 0, whole)
    hl_ref[...] = halves_of(iv_ref[...])
    last = pltpu.make_async_copy(hl_ref, low_hbm.at[:whole, n : n + 2 * STEP], sem.at[cut])
    last.start()
    rest = [
        pltpu.make_async_copy(low_ref.at[cut * B :], low_hbm.at[cut * B : n, :n], rest_sem.at[0]),
        pltpu.make_async_copy(lo_ref.at[cut * B :], low_hbm.at[cut * B : n, REST : REST + n], rest_sem.at[1]),
    ]
    skip = cut * B - whole
    more_ref[:skip, : 2 * B] = halves_of(inv_ref[whole : cut * B, :])
    for i in range(cut, nb):
        for j in range(cut, i + 1):
            at = skip + (i - cut) * B
            more_ref[at : at + B, (j - cut) * B : (j - cut + 1) * B] = block_of(mine_ref, other_ref, first, i, j).astype(BF16)
    rest.append(pltpu.make_async_copy(more_ref, low_hbm.at[whole:n, MORE : MORE + more_ref.shape[1]], rest_sem.at[2]))
    for copy in rest:
        copy.start()
    for k in range(cut):
        row_copy(k, slice(k * B, (k + 1) * B)).wait()
    for copy in [last, *rest]:
        copy.wait()


def chol_tail_kernel(
    cut, n, in_hbm, low_hbm,
    low_ref, lo_ref, inv_ref, s_ref, w_ref, iv_ref, hl_ref, more_ref, sem,
):
    whole = cut * B // STEP * STEP
    skip = cut * B - whole
    loads = [
        pltpu.make_async_copy(in_hbm.at[whole:n, :n], low_ref, sem.at[0]),
        pltpu.make_async_copy(in_hbm.at[cut * B : n, REST : REST + n], lo_ref.at[skip:], sem.at[1]),
        pltpu.make_async_copy(in_hbm.at[whole:n, MORE : MORE + more_ref.shape[1]], more_ref, sem.at[2]),
    ]
    for copy in loads:
        copy.start()
    for copy in loads:
        copy.wait()
    inv_ref[:skip, :] = more_ref[:skip, :B].astype(F32) + more_ref[:skip, B : 2 * B].astype(F32)

    def block(i, j):
        at = skip + (i - cut) * B
        return more_ref[at : at + B, (j - cut) * B : (j - cut + 1) * B].astype(F32)

    factor_steps(cut, n // B, n // B, whole, block, low_ref, lo_ref, inv_ref, s_ref, w_ref, lambda k, rows: None)
    join_inverses(lambda rows, cols: low_ref[rows.start - whole : rows.stop - whole, cols], inv_ref, iv_ref, whole, n)
    hl_ref[...] = halves_of(iv_ref[...])
    copies = [
        pltpu.make_async_copy(low_ref, low_hbm.at[whole:n, :n], sem.at[0]),
        pltpu.make_async_copy(hl_ref, low_hbm.at[whole:n, n : n + 2 * STEP], sem.at[1]),
    ]
    for copy in copies:
        copy.start()
    for copy in copies:
        copy.wait()


def chol(core, mine, other, n, cut):
    whole = cut * B // STEP * STEP
    left = n - cut * B
    return pl.pallas_call(
        functools.partial(chol_kernel, cut),
        out_shape=(
            jax.ShapeDtypeStruct((n, WIDE), BF16),
            TOKEN,
        ),
        in_specs=[SM, VM, VM],
        out_specs=(HBM, VM),
        scratch_shapes=[
            pltpu.VMEM((n, n), BF16),
            pltpu.VMEM((n, n), BF16),
            pltpu.VMEM((n, B), F32),
            pltpu.VMEM((n, B), F32),
            pltpu.VMEM((2 * B, B), BF16),
            pltpu.VMEM((whole, STEP), F32),
            pltpu.VMEM((whole, 2 * STEP), BF16),
            pltpu.VMEM((n - whole, max(2 * B, left)), BF16),
            pltpu.SemaphoreType.DMA((cut + 1,)),
            pltpu.SemaphoreType.DMA((3,)),
        ],
        compiler_params=params(28),
        cost_estimate=cost(39),
        name="cholesky",
    )(core, mine, other)


def chol_tail(low, n, cut):
    rows = n - cut * B // STEP * STEP
    return pl.pallas_call(
        functools.partial(chol_tail_kernel, cut, n),
        out_shape=jax.ShapeDtypeStruct(low.shape, BF16),
        in_specs=[HBM],
        out_specs=HBM,
        input_output_aliases={0: 0},
        scratch_shapes=[
            pltpu.VMEM((rows, n), BF16),
            pltpu.VMEM((rows, n), BF16),
            pltpu.VMEM((rows, B), F32),
            pltpu.VMEM((rows, B), F32),
            pltpu.VMEM((2 * B, B), BF16),
            pltpu.VMEM((rows, STEP), F32),
            pltpu.VMEM((rows, 2 * STEP), BF16),
            pltpu.VMEM((rows, max(2 * B, n - cut * B)), BF16),
            pltpu.SemaphoreType.DMA((3,)),
        ],
        compiler_params=params(28),
        cost_estimate=cost(9),
        name="cholesky_tail",
    )(low)


def solve_into(rhs, m, n, low_hbm, out_ref, low_ref, hl_ref, sem):
    starts = list(range(0, n, STEP))
    loads = []
    for r0 in starts:
        rows = slice(r0, min(r0 + STEP, n))
        if r0:
            loads.append((low_hbm.at[rows, :r0], low_ref.at[rows, :r0]))
        loads.append((low_hbm.at[rows, n : n + 2 * STEP], hl_ref.at[rows]))
    copies = [pltpu.make_async_copy(src, dst, sem.at[k]) for k, (src, dst) in enumerate(loads)]
    for copy in copies:
        copy.start()

    def stacked(x):
        return jnp.concatenate(split(x), 0)

    def fold(p):
        return p[:m] + p[m:]

    def inverted(x, rows, dims):
        w = rows.stop - rows.start
        xs = stacked(x)
        return fold(dot(xs, hl_ref[rows, :w], dims) + dot(xs, hl_ref[rows, STEP : STEP + w], dims))

    parts = [slice(r0, min(r0 + STEP, n)) for r0 in starts]
    acc = []
    for rows in parts:
        s = rhs(rows)
        for done, y in zip(parts, acc):
            if done is parts[0]:
                copies.pop(0).wait()
            s = s - fold(dot(stacked(y), low_ref[rows, done]))
        copies.pop(0).wait()
        acc.append(inverted(s, rows, NT))
    for k in reversed(range(len(parts))):
        z = inverted(acc[k], parts[k], NN)
        out_ref[:, parts[k]] = z
        zs = stacked(z)
        for c in range(k):
            acc[c] = acc[c] - fold(dot(zs, low_ref[parts[k], parts[c]], NN))


def solve_scratch(n):
    return [pltpu.VMEM((n, n), BF16), pltpu.VMEM((n, 2 * STEP), BF16), pltpu.SemaphoreType.DMA((2 * -(-n // STEP) - 1,))]


def solve_kernel(rhs_ref, low_ref, after_ref, out_ref, *scratch):
    m, n = rhs_ref.shape
    solve_into(lambda cols: rhs_ref[:, cols], m, n, low_ref, out_ref, *scratch)


def solve(rhs, low, after):
    return pl.pallas_call(
        solve_kernel,
        out_shape=jax.ShapeDtypeStruct(rhs.shape, F32),
        in_specs=[VM, HBM, ANY],
        out_specs=VM,
        scratch_shapes=solve_scratch(rhs.shape[1]),
        compiler_params=params(16),
        cost_estimate=cost(7),
        name="solve",
    )(rhs, low, after)


def route_kernel(block, owner_ref, total_ref, one_ref, two_ref, low_ref, same_ref, cross_ref, t_ref, r_ref, *scratch):
    m, wide = one_ref.shape
    n = t_ref.shape[1] - B
    right = jnp.concatenate([one_ref[...], two_ref[:, 2 * wide - n :]], 1) / total_ref[0]

    def rhs(cols):
        return right[:, cols]

    solve_into(rhs, m, n, low_ref, t_ref, *scratch)
    t_ref[:, n:] = jnp.zeros((m, t_ref.shape[1] - n), F32)
    lane = lax.broadcasted_iota(jnp.int32, (m, 2 * B), 1)
    for h, out_ref in enumerate((same_ref, cross_ref)):
        for q in range(owner_ref.shape[1]):
            to, off = block * q // B * B, block * q % B
            src = owner_ref[h, q] * block
            win = t_ref[:, pl.ds(pl.multiple_of(src // B * B, B), 2 * B)]
            win = pltpu.roll(win, (off + 2 * B - src % B) % (2 * B), 1)
            old = r_ref[:, to : to + 2 * B]
            r_ref[:, to : to + 2 * B] = jnp.where((lane >= off) & (lane < off + block), win, old)
        out_ref[...] = r_ref[:, : out_ref.shape[1]]


def solve_and_route(owner, total, one, two, low, n, block):
    m = one.shape[0]
    wide = -(-owner.shape[1] * block // B) * B
    out = jax.ShapeDtypeStruct((m, wide), F32)
    return pl.pallas_call(
        functools.partial(route_kernel, block),
        out_shape=(out, out),
        in_specs=[SM, SM, VM, VM, HBM],
        out_specs=(VM, VM),
        scratch_shapes=[pltpu.VMEM((m, n + B), F32), pltpu.VMEM((m, wide + B), F32)] + solve_scratch(n),
        compiler_params=params(16),
        cost_estimate=cost(9),
        name="solve_and_route",
    )(owner, total, one, two, low)


def sum_kernel(parts_ref, *refs):
    out_ref = refs[-1]
    acc = parts_ref[0]
    for k in range(1, parts_ref.shape[0]):
        acc = acc + parts_ref[k]
    out_ref[...] = acc


def damp_kernel(scale_ref, parts_ref, diag_ref, out_ref, done_ref, sum_ref, sem):
    acc = parts_ref[0]
    for k in range(1, parts_ref.shape[0]):
        acc = acc + parts_ref[k]
    sum_ref[...] = (acc / scale_ref[0] + scale_ref[1] * diag_ref[...]).astype(BF16)
    copies = [pltpu.make_async_copy(sum_ref, out_ref.at[k], sem.at[k]) for k in range(out_ref.shape[0])]
    for copy in copies:
        copy.start()
    done_ref[...] = jnp.zeros_like(done_ref)
    for copy in copies:
        copy.wait()


def damp_and_spread(scale, parts, diag):
    chips = parts.shape[0]
    return pl.pallas_call(
        damp_kernel,
        out_shape=(jax.ShapeDtypeStruct(parts.shape, BF16), TOKEN),
        in_specs=[SM, VM, VM],
        out_specs=(HBM, VM),
        scratch_shapes=[pltpu.VMEM(parts.shape[1:], BF16), pltpu.SemaphoreType.DMA((chips,))],
        compiler_params=params(60),
        cost_estimate=cost(3),
        name="damp_and_spread",
    )(scale, parts, diag)


def sum_parts(parts, *after):
    return pl.pallas_call(
        sum_kernel,
        out_shape=jax.ShapeDtypeStruct(parts.shape[1:], F32),
        in_specs=[VM] + [ANY] * len(after),
        out_specs=VM,
        compiler_params=params(16),
        cost_estimate=cost(3),
        name="sum_parts",
    )(parts, *after)


def rows_kernel(at_ref, core_ref, mine_ref, other_ref, out_ref, s_ref):
    m, n = out_ref.shape
    nb = n // B
    first = core_ref[0] == 0
    for i in range(nb):
        for j in range(i + 1):
            blk = block_of(mine_ref, other_ref, first, i, j)
            s_ref[i * B : (i + 1) * B, j * B : (j + 1) * B] = blk
            if i > j:
                s_ref[j * B : (j + 1) * B, i * B : (i + 1) * B] = blk.T
    at = at_ref[0]
    window = s_ref[pl.ds(pl.multiple_of(at // 8 * 8, 8), 32), :]
    shift = at % 8
    out = window[:m]
    for k in range(1, 8):
        out = jnp.where(shift == k, window[k : k + m], out)
    out_ref[...] = out


def rows_of(at, core, mine, other, n, m):
    return pl.pallas_call(
        rows_kernel,
        out_shape=jax.ShapeDtypeStruct((m, n), F32),
        in_specs=[SM, SM, VM, VM],
        out_specs=VM,
        scratch_shapes=[pltpu.VMEM((n + 8, n), F32)],
        compiler_params=params(16),
        cost_estimate=cost(3),
        name="rows",
    )(at, core, mine, other)


def per_device(attn_out, out_grad, image_counts, column_owner, damping):
    n_dp = lax.axis_size("dp")
    dp_index = lax.axis_index("dp")
    grp_index = lax.axis_index("grp")
    per_dev, width = attn_out.shape
    block = width // n_dp
    chips = n_dp // 2
    core = dp_index % 2
    chip = dp_index // 2
    nb = width // B
    used = tri(nb, 0) * HALF // SLAB
    per_chip = -(-used // chips)
    same_core = [list(range(c, n_dp, 2)) for c in range(2)]
    swap_core = [(d, d ^ 1) for d in range(n_dp)]
    swap_grp = [(0, 1), (1, 0)]
    core_arr = core.astype(jnp.int32)[None]
    is_a = grp_index == 0

    def keep_of(grp, dp):
        return (lax.dynamic_index_in_dim(image_counts, grp * n_dp + dp, 0, keepdims=False) > 0).astype(F32)

    flip = n_dp // 2
    near = [(g * n_dp + d, (1 - g) * n_dp + d) for g in range(2) for d in range(n_dp)]
    far = [(g * n_dp + d, (1 - g) * n_dp + d ^ flip) for g in range(2) for d in range(n_dp)]
    both = ("grp", "dp")
    half = per_dev // 2

    def swap(rows):
        return lax.ppermute(rows[:half], both, near), lax.ppermute(rows[half:], both, far)

    def to_mate(rows):
        return lax.ppermute(rows, "dp", swap_core)

    first = jnp.where(is_a, attn_out, out_grad)
    second = jnp.where(is_a, out_grad, attn_out)
    from_near, from_far = swap(second)
    mine_rows = [first, to_mate(first), from_near, from_far, to_mate(from_near), to_mate(from_far)]
    first_later, _, _ = lax.optimization_barrier((first, from_near, from_far))
    next_near, next_far = swap(first_later)
    over, mate, away = 1 - grp_index, dp_index ^ 1, dp_index ^ flip
    keeps = jnp.stack([
        keep_of(grp_index, dp_index),
        keep_of(grp_index, mate),
        keep_of(over, dp_index),
        keep_of(over, away),
        keep_of(over, mate),
        keep_of(over, away ^ 1),
    ])
    total = (TOK * jnp.sum(image_counts)).astype(F32)
    part, squares = gram(core_arr, keeps, mine_rows, chips * per_chip)
    part, next_near, next_far = lax.optimization_barrier((part, next_near, next_far))
    other_rows = [second, to_mate(second), next_near, next_far, to_mate(next_near), to_mate(next_far)]
    got = lax.all_to_all(
        part.reshape(chips, per_chip * SLAB, B), "dp", split_axis=0, concat_axis=0, tiled=True, axis_index_groups=same_core
    )
    flat = chip * (per_chip * SLAB) + jnp.arange(per_chip * SLAB)
    t = flat // HALF
    on_diag = jnp.zeros(t.shape, bool)
    for i in range(nb):
        on_diag = on_diag | (t == tri(i, i))
    in_row = core * HALF + flat % HALF
    diag = (on_diag & (flat < used * SLAB))[:, None] & (in_row[:, None] == jnp.arange(B)[None, :])
    damp = jnp.where(is_a, damping[0], damping[1])
    spread, damp_done = damp_and_spread(jnp.stack([total, damp]), got, diag.astype(F32))
    mine = lax.all_to_all(spread, "dp", split_axis=0, concat_axis=0, tiled=True, axis_index_groups=same_core)
    mine = mine.reshape(chips * per_chip * SLAB, B)
    wide = (nb + 2) // 2 * B
    part_w = cross(core_arr, grp_index.astype(jnp.int32)[None], keeps, damp_done, mine_rows, other_rows, chips, wide)
    mine, part_w = lax.optimization_barrier((mine, part_w))
    theirs = lax.ppermute(mine, "dp", swap_core)
    cut = nb - 2
    low, chol_done = chol(core_arr, mine, theirs, width, cut)

    got_w = lax.all_to_all(part_w, "dp", split_axis=0, concat_axis=0, tiled=True, axis_index_groups=same_core)

    at = (dp_index * block).astype(jnp.int32)[None]

    order = column_owner.reshape(chips, 2)
    order = jnp.stack([jnp.where(core == 0, order[:, 0], order[:, 1]), jnp.where(core == 0, order[:, 1], order[:, 0])])
    my_w = sum_parts(got_w, chol_done)
    their_w = lax.ppermute(my_w, "grp", [(1, 0)])
    low = chol_tail(low, width, cut)
    my_rows = rows_of(at, core_arr, mine, theirs, width, ROWS)
    same, cross_t = solve_and_route(order, total[None], my_w, their_w, low, width, block)
    same = lax.ppermute(same, both, [(d, n_dp + d) for d in range(n_dp)])
    cross_t = lax.ppermute(cross_t, both, [(d, n_dp + (d ^ 1)) for d in range(n_dp)])
    is_first = core == 0
    pair = jnp.concatenate([jnp.where(is_first, same, cross_t), jnp.where(is_first, cross_t, same)])
    pair = pair[:, : chips * block].reshape(2 * ROWS, chips, block).transpose(1, 2, 0)
    squares = lax.dynamic_index_in_dim(squares[0].reshape(chips, 2, block), core, 1, keepdims=False)
    pair = jnp.concatenate([pair, squares[:, :, None]], axis=2)
    columns = lax.all_to_all(pair, "dp", split_axis=0, concat_axis=0, tiled=True, axis_index_groups=same_core)
    squares = jnp.sum(columns[:, :, 2 * ROWS], axis=0) / total
    columns = columns[:, :, : 2 * ROWS].transpose(1, 0, 2).reshape(block, n_dp * ROWS)[:, :width]
    columns = jnp.pad(columns, ((0, ROWS - block), (0, 0)))
    left = solve(columns, low, my_rows)[:block]
    here = (dp_index * block + jnp.arange(block))[:, None] == jnp.arange(width)[None, :]
    my_rows = jnp.where(here, squares[:, None], my_rows[:block])
    their_rows = lax.ppermute(my_rows, "grp", swap_grp)
    factors = jnp.stack([jnp.where(is_a, my_rows, their_rows), jnp.where(is_a, their_rows, my_rows)])
    back = lax.ppermute(left, "grp", [(1, 0)])
    preconditioned = jnp.where(is_a, back, left).T
    return (factors, preconditioned)


def solution(mesh):
    placed = (P(("grp", "dp"), None), P(("grp", "dp"), None), P(), P(), P())
    return jax.shard_map(
        per_device,
        mesh=mesh,
        in_specs=placed,
        out_specs=(P(None, "dp", None), P(None, "dp")),
        check_vma=False,
    )
```

```python
import functools

import jax
import jax.numpy as jnp
from jax import lax
from jax.experimental import pallas as pl
from jax.experimental.pallas import tpu as pltpu
from jax.sharding import PartitionSpec as P

TOK = 256
B = 128
HALF = 64
SLAB = 16
ROWS = 24
WIDE = 14336
STEP = 512
REST = 4096
MORE = 8192
F32 = jnp.float32
BF16 = jnp.bfloat16
NT = (((1,), (1,)), ((), ()))
NN = (((1,), (0,)), ((), ()))
TN = (((0,), (0,)), ((), ()))
VM = pl.BlockSpec(memory_space=pltpu.VMEM)
ANY = pl.BlockSpec(memory_space=pl.ANY)
HBM = pl.BlockSpec(memory_space=pltpu.HBM)
SM = pl.BlockSpec(memory_space=pltpu.SMEM)
TOKEN = jax.ShapeDtypeStruct((8, B), F32)
MIB = 1024 * 1024


def params(mib):
    return pltpu.CompilerParams(vmem_limit_bytes=mib * MIB)


def cost(micros):
    return pl.CostEstimate(flops=int(micros * 1.1e9), bytes_accessed=MIB, transcendentals=0)


def dot(a, b, dims=NT):
    return lax.dot_general(a, b, dims, preferred_element_type=F32)


def split(x):
    hi = x.astype(BF16)
    return hi, (x - hi.astype(F32)).astype(BF16)


def row(x, t):
    return jnp.broadcast_to(x[..., t : t + 1, :], x.shape)


def col(x, c):
    return jnp.broadcast_to(x[..., c : c + 1], x.shape)


def rounded(x):
    return x.astype(BF16).astype(F32)


def tri(i, j):
    return i * (i + 1) // 2 + j


def pieces_of(refs):
    own, mate, near, far, near_mate, far_mate = refs
    return [[(0, own)], [(1, mate)], [(2, near), (3, far)], [(4, near_mate), (5, far_mate)]]


def columns_of(group, cols, keep_ref=None):
    parts = [ref[:, cols] if keep_ref is None else ref[:, cols] * keep_ref[k].astype(BF16) for k, ref in group]
    return parts[0] if len(parts) == 1 else jnp.concatenate(parts, 0)


def gram_kernel(core_ref, keep_ref, *refs):
    pieces, (out_ref, squares_ref, tmp_ref) = pieces_of(refs[:6]), refs[6:]
    nb = refs[0].shape[1] // B
    start = pl.multiple_of(core_ref[0] * HALF, HALF)
    on = lax.broadcasted_iota(jnp.int32, (B, B), 0) == lax.broadcasted_iota(jnp.int32, (B, B), 1)
    used = tri(nb, 0) * HALF
    out_ref[used:, :] = jnp.zeros((out_ref.shape[0] - used, B), F32)
    for i in range(nb):
        wide = (i + 1) * B
        acc = None
        for group in pieces:
            p = dot(columns_of(group, slice(i * B, wide), keep_ref), columns_of(group, slice(0, wide)), TN)
            acc = p if acc is None else acc + p
        tmp_ref[:, :wide] = acc
        diag = jnp.sum(jnp.where(on, acc[:, i * B :], 0.0), axis=0, keepdims=True)
        squares_ref[:, i * B : wide] = jnp.broadcast_to(diag, (8, B))
        for j in range(i + 1):
            t = tri(i, j)
            out_ref[t * HALF : (t + 1) * HALF, :] = tmp_ref[pl.ds(start, HALF), j * B : (j + 1) * B]


def gram(core, keeps, pieces, slots):
    width = pieces[0].shape[1]
    return pl.pallas_call(
        gram_kernel,
        out_shape=(jax.ShapeDtypeStruct((slots * SLAB, B), F32), jax.ShapeDtypeStruct((8, width), F32)),
        in_specs=[SM, SM] + [VM] * 6,
        out_specs=(VM, VM),
        scratch_shapes=[pltpu.VMEM((B, width), F32)],
        compiler_params=params(40),
        cost_estimate=cost(4),
        name="gram",
    )(core, keeps, *pieces)


def cross_kernel(core_ref, grp_ref, keep_ref, after_ref, *refs):
    mine, other, (out_ref, tmp_ref) = pieces_of(refs[:6]), pieces_of(refs[6:12]), refs[12:]
    n = refs[0].shape[1]
    wide = out_ref.shape[2]

    def run(left, right, first):
        for i in range(n // B):
            acc = None
            for lg, rg in zip(left, right):
                p = dot(columns_of(lg, slice(i * B, (i + 1) * B), keep_ref), columns_of(rg, slice(first, first + wide)), TN)
                acc = p if acc is None else acc + p
            tmp_ref[i * B : (i + 1) * B, :] = acc

    pl.when(grp_ref[0] == 0)(lambda: run(other, mine, 0))
    pl.when(grp_ref[0] == 1)(lambda: run(mine, other, n - wide))
    tmp_ref[n:, :] = jnp.zeros((tmp_ref.shape[0] - n, wide), F32)
    for q in range(out_ref.shape[0]):
        out_ref[q] = tmp_ref[pl.ds(pl.multiple_of((2 * q + core_ref[0]) * ROWS, 8), ROWS), :]


def cross(core, grp, keeps, after, mine, other, chips, wide):
    return pl.pallas_call(
        cross_kernel,
        out_shape=jax.ShapeDtypeStruct((chips, ROWS, wide), F32),
        in_specs=[SM, SM, SM, ANY] + [VM] * 12,
        out_specs=VM,
        scratch_shapes=[pltpu.VMEM((2 * chips * ROWS, wide), F32)],
        compiler_params=params(40),
        cost_estimate=cost(30),
        name="cross",
    )(core, grp, keeps, after, *mine, *other)


def factor_diag(block):
    a = [block[8 * i : 8 * i + 8, :] for i in range(16)]
    lane = lax.broadcasted_iota(jnp.int32, (8, B), 1)
    sub = lax.broadcasted_iota(jnp.int32, (8, B), 0)
    x = [(lane == sub + 8 * g).astype(F32) for g in range(16)]
    inv, inv_r = [], []
    cg = [col(a[0], t) for t in range(8)]
    for g in range(16):
        here = (lane >= 8 * g) & (lane < 8 * g + 8)
        v = jnp.where(here, (lane == sub + 8 * g).astype(F32), a[g])
        xg = x[g]
        if g < 15:
            near = a[g + 1]
            cr = [col(near, 8 * g + t) for t in range(8)]
            nxt = [col(near, 8 * g + 8 + t) for t in range(8)]
            near, xr = jnp.where(here, 0.0, near), x[g + 1]
        rs, vs, xs, css = [], [], [], []
        for t in range(8):
            p = row(cg[t], t)
            r = lax.rsqrt(p)
            lt = jnp.where(sub > t, cg[t] * r, 0.0)
            vn = row(v, t) * r
            v = jnp.where(sub == t, vn, v - lt * vn)
            xn = row(xg, t) / rounded(p * r)
            xg = jnp.where(sub == t, xn, xg - rounded(lt) * xn)
            cs = {s: row(cg[s], t) * r for s in range(t + 1, 8)}
            for s in range(t + 1, 8):
                cg[s] = cg[s] - lt * cs[s]
            rs.append(r)
            vs.append(vn)
            xs.append(xn)
            css.append(cs)
            if g < 15:
                lr = cr[t] * r
                for s in range(8):
                    nxt[s] = nxt[s] - lr * row(lr, s)
                near = near - lr * vn
                xr = xr - rounded(lr) * xn
                for s in range(t + 1, 8):
                    cr[s] = cr[s] - lr * cs[s]
        inv.append(jnp.where(lane <= sub + 8 * g, v, 0.0))
        inv_r.append(xg)
        if g < 15:
            a[g + 1], x[g + 1] = near, xr
            cg = nxt
        for i in range(g + 2, 16):
            c = [col(a[i], 8 * g + t) for t in range(8)]
            ai, xi = jnp.where(here, 0.0, a[i]), x[i]
            for t in range(8):
                l = c[t] * rs[t]
                ai = ai - l * vs[t]
                xi = xi - rounded(l) * xs[t]
                for s in range(t + 1, 8):
                    c[s] = c[s] - l * css[t][s]
            a[i], x[i] = ai, xi
    return jnp.concatenate(inv, 0), jnp.concatenate(inv_r, 0)


def block_of(mine_ref, other_ref, first, i, j):
    t = tri(i, j) * HALF
    mine = mine_ref[t : t + HALF, :].astype(F32)
    other = other_ref[t : t + HALF, :].astype(F32)
    return jnp.concatenate([jnp.where(first, mine, other), jnp.where(first, other, mine)], 0)


def join_inverses(low_of, inv_ref, iv_ref, first, last):
    iv_ref[...] = jnp.zeros_like(iv_ref)
    for b in range(first, last, B):
        at = b % STEP
        iv_ref[b - first : b - first + B, at : at + B] = inv_ref[b - first : b - first + B, :]
    size = B
    while size < STEP:
        for r0 in range(first, last - size, 2 * size):
            r1 = r0 + size
            r2 = min(r1 + size, last)
            at = r0 % STEP
            i0, i1, i2 = r0 - first, r1 - first, r2 - first
            left = jnp.concatenate(split(iv_ref[i0:i1, at : at + size]), 1)
            p = dot(low_of(slice(r1, r2), slice(r0, r1)), left, NN)
            phi, plo = split(p[:, :size] + p[:, size:])
            bhi, blo = split(iv_ref[i1:i2, at + size : at + size + r2 - r1])
            iv_ref[i1:i2, at : at + size] = -(dot(bhi, phi, NN) + dot(bhi, plo, NN) + dot(blo, phi, NN))
        size *= 2


def halves_of(x):
    return jnp.concatenate(split(x), 1)


def block_of(mine_ref, other_ref, first, i, j):
    t = tri(i, j) * HALF
    mine = mine_ref[t : t + HALF, :].astype(F32)
    other = other_ref[t : t + HALF, :].astype(F32)
    return jnp.concatenate([jnp.where(first, mine, other), jnp.where(first, other, mine)], 0)


def factor_steps(first, last, nb, base, block, low_ref, lo_ref, inv_ref, s_ref, w_ref, each):
    def update(kk):
        r0 = kk * B
        at = r0 - base
        s = jnp.concatenate([block(i, kk) for i in range(kk, nb)], 0)
        if kk:
            wts = jnp.concatenate([low_ref[at : at + B, :r0], lo_ref[at : at + B, :r0]], 0)
            pr = dot(low_ref[at:, :r0], wts)
            s = s - (pr[:, :B] + pr[:, B:] + dot(lo_ref[at:, :r0], low_ref[at : at + B, :r0]))
        s_ref[at:, :] = s

    def panel(kk):
        r0 = kk * B
        r1 = r0 + B
        at = r1 - base
        shi, slo = split(s_ref[at:, :])
        pr = dot(shi, w_ref[...])
        lp = pr[:, :B] + pr[:, B:] + dot(slo, w_ref[:B, :])
        hi, lo = split(lp)
        low_ref[at:, r0:r1] = hi
        lo_ref[at:, r0:r1] = lo

    def step(k, _):
        for kk in range(first, last):
            pl.when(k == kk)(lambda kk=kk: update(kk))
        rows = pl.ds(pl.multiple_of(k * B - base, B), B)
        each(k, rows)
        linv, lrinv = factor_diag(s_ref[rows, :])
        inv_ref[rows, :] = lrinv
        hi, lo = split(linv)
        w_ref[:B, :] = hi
        w_ref[B:, :] = lo
        for kk in range(first, min(last, nb - 1)):
            pl.when(k == kk)(lambda kk=kk: panel(kk))
        return 0

    lax.fori_loop(first, last, step, 0)


def chol_kernel(
    cut, core_ref, mine_ref, other_ref, low_hbm, done_ref,
    low_ref, lo_ref, inv_ref, s_ref, w_ref, iv_ref, hl_ref, more_ref, sem, rest_sem,
):
    done_ref[...] = jnp.zeros_like(done_ref)
    n = low_ref.shape[0]
    nb = n // B
    first = core_ref[0] == 0
    whole = cut * B // STEP * STEP

    def row_copy(k, rows):
        return pltpu.make_async_copy(low_ref.at[rows], low_hbm.at[rows, :n], sem.at[k])

    factor_steps(
        0, cut, nb, 0, functools.partial(block_of, mine_ref, other_ref, first), low_ref, lo_ref, inv_ref, s_ref, w_ref,
        lambda k, rows: row_copy(k, rows).start(),
    )
    join_inverses(lambda rows, cols: low_ref[rows, cols], inv_ref, iv_ref, 0, whole)
    hl_ref[...] = halves_of(iv_ref[...])
    last = pltpu.make_async_copy(hl_ref, low_hbm.at[:whole, n : n + 2 * STEP], sem.at[cut])
    last.start()
    rest = [
        pltpu.make_async_copy(low_ref.at[cut * B :], low_hbm.at[cut * B : n, :n], rest_sem.at[0]),
        pltpu.make_async_copy(lo_ref.at[cut * B :], low_hbm.at[cut * B : n, REST : REST + n], rest_sem.at[1]),
    ]
    skip = cut * B - whole
    more_ref[:skip, : 2 * B] = halves_of(inv_ref[whole : cut * B, :])
    for i in range(cut, nb):
        for j in range(cut, i + 1):
            at = skip + (i - cut) * B
            more_ref[at : at + B, (j - cut) * B : (j - cut + 1) * B] = block_of(mine_ref, other_ref, first, i, j).astype(BF16)
    rest.append(pltpu.make_async_copy(more_ref, low_hbm.at[whole:n, MORE : MORE + more_ref.shape[1]], rest_sem.at[2]))
    for copy in rest:
        copy.start()
    for k in range(cut):
        row_copy(k, slice(k * B, (k + 1) * B)).wait()
    for copy in [last, *rest]:
        copy.wait()


def chol_tail_kernel(
    cut, n, in_hbm, low_hbm,
    low_ref, lo_ref, inv_ref, s_ref, w_ref, iv_ref, hl_ref, more_ref, sem,
):
    whole = cut * B // STEP * STEP
    skip = cut * B - whole
    loads = [
        pltpu.make_async_copy(in_hbm.at[whole:n, :n], low_ref, sem.at[0]),
        pltpu.make_async_copy(in_hbm.at[cut * B : n, REST : REST + n], lo_ref.at[skip:], sem.at[1]),
        pltpu.make_async_copy(in_hbm.at[whole:n, MORE : MORE + more_ref.shape[1]], more_ref, sem.at[2]),
    ]
    for copy in loads:
        copy.start()
    for copy in loads:
        copy.wait()
    inv_ref[:skip, :] = more_ref[:skip, :B].astype(F32) + more_ref[:skip, B : 2 * B].astype(F32)

    def block(i, j):
        at = skip + (i - cut) * B
        return more_ref[at : at + B, (j - cut) * B : (j - cut + 1) * B].astype(F32)

    factor_steps(cut, n // B, n // B, whole, block, low_ref, lo_ref, inv_ref, s_ref, w_ref, lambda k, rows: None)
    join_inverses(lambda rows, cols: low_ref[rows.start - whole : rows.stop - whole, cols], inv_ref, iv_ref, whole, n)
    hl_ref[...] = halves_of(iv_ref[...])
    copies = [
        pltpu.make_async_copy(low_ref, low_hbm.at[whole:n, :n], sem.at[0]),
        pltpu.make_async_copy(hl_ref, low_hbm.at[whole:n, n : n + 2 * STEP], sem.at[1]),
    ]
    for copy in copies:
        copy.start()
    for copy in copies:
        copy.wait()


def chol(core, mine, other, n, cut):
    whole = cut * B // STEP * STEP
    left = n - cut * B
    return pl.pallas_call(
        functools.partial(chol_kernel, cut),
        out_shape=(
            jax.ShapeDtypeStruct((n, WIDE), BF16),
            TOKEN,
        ),
        in_specs=[SM, VM, VM],
        out_specs=(HBM, VM),
        scratch_shapes=[
            pltpu.VMEM((n, n), BF16),
            pltpu.VMEM((n, n), BF16),
            pltpu.VMEM((n, B), F32),
            pltpu.VMEM((n, B), F32),
            pltpu.VMEM((2 * B, B), BF16),
            pltpu.VMEM((whole, STEP), F32),
            pltpu.VMEM((whole, 2 * STEP), BF16),
            pltpu.VMEM((n - whole, max(2 * B, left)), BF16),
            pltpu.SemaphoreType.DMA((cut + 1,)),
            pltpu.SemaphoreType.DMA((3,)),
        ],
        compiler_params=params(28),
        cost_estimate=cost(39),
        name="cholesky",
    )(core, mine, other)


def chol_tail(low, n, cut):
    rows = n - cut * B // STEP * STEP
    return pl.pallas_call(
        functools.partial(chol_tail_kernel, cut, n),
        out_shape=jax.ShapeDtypeStruct(low.shape, BF16),
        in_specs=[HBM],
        out_specs=HBM,
        input_output_aliases={0: 0},
        scratch_shapes=[
            pltpu.VMEM((rows, n), BF16),
            pltpu.VMEM((rows, n), BF16),
            pltpu.VMEM((rows, B), F32),
            pltpu.VMEM((rows, B), F32),
            pltpu.VMEM((2 * B, B), BF16),
            pltpu.VMEM((rows, STEP), F32),
            pltpu.VMEM((rows, 2 * STEP), BF16),
            pltpu.VMEM((rows, max(2 * B, n - cut * B)), BF16),
            pltpu.SemaphoreType.DMA((3,)),
        ],
        compiler_params=params(28),
        cost_estimate=cost(9),
        name="cholesky_tail",
    )(low)


def solve_into(rhs, m, n, low_hbm, out_ref, low_ref, hl_ref, sem):
    starts = list(range(0, n, STEP))
    loads = []
    for r0 in starts:
        rows = slice(r0, min(r0 + STEP, n))
        if r0:
            loads.append((low_hbm.at[rows, :r0], low_ref.at[rows, :r0]))
        loads.append((low_hbm.at[rows, n : n + 2 * STEP], hl_ref.at[rows]))
    copies = [pltpu.make_async_copy(src, dst, sem.at[k]) for k, (src, dst) in enumerate(loads)]
    for copy in copies:
        copy.start()

    def stacked(x):
        return jnp.concatenate(split(x), 0)

    def fold(p):
        return p[:m] + p[m:]

    def inverted(x, rows, dims):
        w = rows.stop - rows.start
        xs = stacked(x)
        return fold(dot(xs, hl_ref[rows, :w], dims) + dot(xs, hl_ref[rows, STEP : STEP + w], dims))

    parts = [slice(r0, min(r0 + STEP, n)) for r0 in starts]
    acc = []
    for rows in parts:
        s = rhs(rows)
        for done, y in zip(parts, acc):
            if done is parts[0]:
                copies.pop(0).wait()
            s = s - fold(dot(stacked(y), low_ref[rows, done]))
        copies.pop(0).wait()
        acc.append(inverted(s, rows, NT))
    for k in reversed(range(len(parts))):
        z = inverted(acc[k], parts[k], NN)
        out_ref[:, parts[k]] = z
        zs = stacked(z)
        for c in range(k):
            acc[c] = acc[c] - fold(dot(zs, low_ref[parts[k], parts[c]], NN))


def solve_scratch(n):
    return [pltpu.VMEM((n, n), BF16), pltpu.VMEM((n, 2 * STEP), BF16), pltpu.SemaphoreType.DMA((2 * -(-n // STEP) - 1,))]


def solve_kernel(grp_ref, rhs_ref, low_ref, after_ref, out_ref, *scratch):
    m, n = rhs_ref.shape
    pl.when(grp_ref[0] == 1)(lambda: solve_into(lambda cols: rhs_ref[:, cols], m, n, low_ref, out_ref, *scratch))


def solve(grp, rhs, low, after):
    return pl.pallas_call(
        solve_kernel,
        out_shape=jax.ShapeDtypeStruct(rhs.shape, F32),
        in_specs=[SM, VM, HBM, ANY],
        out_specs=VM,
        scratch_shapes=solve_scratch(rhs.shape[1]),
        compiler_params=params(16),
        cost_estimate=cost(7),
        name="solve",
    )(grp, rhs, low, after)


def route_kernel(block, grp_ref, *refs):
    pl.when(grp_ref[0] == 0)(lambda: route(block, *refs))


def route(block, owner_ref, total_ref, one_ref, two_ref, low_ref, same_ref, cross_ref, t_ref, r_ref, *scratch):
    m, wide = one_ref.shape
    n = t_ref.shape[1] - B
    right = jnp.concatenate([one_ref[...], two_ref[:, 2 * wide - n :]], 1) / total_ref[0]

    def rhs(cols):
        return right[:, cols]

    solve_into(rhs, m, n, low_ref, t_ref, *scratch)
    t_ref[:, n:] = jnp.zeros((m, t_ref.shape[1] - n), F32)
    lane = lax.broadcasted_iota(jnp.int32, (m, 2 * B), 1)
    for h, out_ref in enumerate((same_ref, cross_ref)):
        for q in range(owner_ref.shape[1]):
            to, off = block * q // B * B, block * q % B
            src = owner_ref[h, q] * block
            win = t_ref[:, pl.ds(pl.multiple_of(src // B * B, B), 2 * B)]
            win = pltpu.roll(win, (off + 2 * B - src % B) % (2 * B), 1)
            old = r_ref[:, to : to + 2 * B]
            r_ref[:, to : to + 2 * B] = jnp.where((lane >= off) & (lane < off + block), win, old)
        out_ref[...] = r_ref[:, : out_ref.shape[1]]


def solve_and_route(grp, owner, total, one, two, low, n, block):
    m = one.shape[0]
    wide = -(-owner.shape[1] * block // B) * B
    out = jax.ShapeDtypeStruct((m, wide), F32)
    return pl.pallas_call(
        functools.partial(route_kernel, block),
        out_shape=(out, out),
        in_specs=[SM, SM, SM, VM, VM, HBM],
        out_specs=(VM, VM),
        scratch_shapes=[pltpu.VMEM((m, n + B), F32), pltpu.VMEM((m, wide + B), F32)] + solve_scratch(n),
        compiler_params=params(16),
        cost_estimate=cost(9),
        name="solve_and_route",
    )(grp, owner, total, one, two, low)


def sum_kernel(parts_ref, *refs):
    out_ref = refs[-1]
    acc = parts_ref[0]
    for k in range(1, parts_ref.shape[0]):
        acc = acc + parts_ref[k]
    out_ref[...] = acc


def damp_kernel(scale_ref, parts_ref, diag_ref, out_ref, done_ref, sum_ref, sem):
    acc = parts_ref[0]
    for k in range(1, parts_ref.shape[0]):
        acc = acc + parts_ref[k]
    sum_ref[...] = (acc / scale_ref[0] + scale_ref[1] * diag_ref[...]).astype(BF16)
    copies = [pltpu.make_async_copy(sum_ref, out_ref.at[k], sem.at[k]) for k in range(out_ref.shape[0])]
    for copy in copies:
        copy.start()
    done_ref[...] = jnp.zeros_like(done_ref)
    for copy in copies:
        copy.wait()


def damp_and_spread(scale, parts, diag):
    chips = parts.shape[0]
    return pl.pallas_call(
        damp_kernel,
        out_shape=(jax.ShapeDtypeStruct(parts.shape, BF16), TOKEN),
        in_specs=[SM, VM, VM],
        out_specs=(HBM, VM),
        scratch_shapes=[pltpu.VMEM(parts.shape[1:], BF16), pltpu.SemaphoreType.DMA((chips,))],
        compiler_params=params(60),
        cost_estimate=cost(3),
        name="damp_and_spread",
    )(scale, parts, diag)


def sum_parts(parts, *after):
    return pl.pallas_call(
        sum_kernel,
        out_shape=jax.ShapeDtypeStruct(parts.shape[1:], F32),
        in_specs=[VM] + [ANY] * len(after),
        out_specs=VM,
        compiler_params=params(16),
        cost_estimate=cost(3),
        name="sum_parts",
    )(parts, *after)


def rows_kernel(at_ref, core_ref, mine_ref, other_ref, out_ref, s_ref):
    m, n = out_ref.shape
    nb = n // B
    first = core_ref[0] == 0
    for i in range(nb):
        for j in range(i + 1):
            blk = block_of(mine_ref, other_ref, first, i, j)
            s_ref[i * B : (i + 1) * B, j * B : (j + 1) * B] = blk
            if i > j:
                s_ref[j * B : (j + 1) * B, i * B : (i + 1) * B] = blk.T
    at = at_ref[0]
    window = s_ref[pl.ds(pl.multiple_of(at // 8 * 8, 8), 32), :]
    shift = at % 8
    out = window[:m]
    for k in range(1, 8):
        out = jnp.where(shift == k, window[k : k + m], out)
    out_ref[...] = out


def rows_of(at, core, mine, other, n, m):
    return pl.pallas_call(
        rows_kernel,
        out_shape=jax.ShapeDtypeStruct((m, n), F32),
        in_specs=[SM, SM, VM, VM],
        out_specs=VM,
        scratch_shapes=[pltpu.VMEM((n + 8, n), F32)],
        compiler_params=params(16),
        cost_estimate=cost(3),
        name="rows",
    )(at, core, mine, other)


def per_device(attn_out, out_grad, image_counts, column_owner, damping):
    n_dp = lax.axis_size("dp")
    dp_index = lax.axis_index("dp")
    grp_index = lax.axis_index("grp")
    per_dev, width = attn_out.shape
    block = width // n_dp
    chips = n_dp // 2
    core = dp_index % 2
    chip = dp_index // 2
    nb = width // B
    used = tri(nb, 0) * HALF // SLAB
    per_chip = -(-used // chips)
    same_core = [list(range(c, n_dp, 2)) for c in range(2)]
    swap_core = [(d, d ^ 1) for d in range(n_dp)]
    swap_grp = [(0, 1), (1, 0)]
    core_arr = core.astype(jnp.int32)[None]
    grp_arr = grp_index.astype(jnp.int32)[None]
    is_a = grp_index == 0

    def keep_of(grp, dp):
        return (lax.dynamic_index_in_dim(image_counts, grp * n_dp + dp, 0, keepdims=False) > 0).astype(F32)

    flip = n_dp // 2
    near = [(g * n_dp + d, (1 - g) * n_dp + d) for g in range(2) for d in range(n_dp)]
    far = [(g * n_dp + d, (1 - g) * n_dp + d ^ flip) for g in range(2) for d in range(n_dp)]
    both = ("grp", "dp")
    half = per_dev // 2

    def swap(rows):
        return lax.ppermute(rows[:half], both, near), lax.ppermute(rows[half:], both, far)

    def to_mate(rows):
        return lax.ppermute(rows, "dp", swap_core)

    first = jnp.where(is_a, attn_out, out_grad)
    second = jnp.where(is_a, out_grad, attn_out)
    from_near, from_far = swap(second)
    mine_rows = [first, to_mate(first), from_near, from_far, to_mate(from_near), to_mate(from_far)]
    first_later, _, _ = lax.optimization_barrier((first, from_near, from_far))
    next_near, next_far = swap(first_later)
    over, mate, away = 1 - grp_index, dp_index ^ 1, dp_index ^ flip
    keeps = jnp.stack([
        keep_of(grp_index, dp_index),
        keep_of(grp_index, mate),
        keep_of(over, dp_index),
        keep_of(over, away),
        keep_of(over, mate),
        keep_of(over, away ^ 1),
    ])
    total = (TOK * jnp.sum(image_counts)).astype(F32)
    part, squares = gram(core_arr, keeps, mine_rows, chips * per_chip)
    part, next_near, next_far = lax.optimization_barrier((part, next_near, next_far))
    other_rows = [second, to_mate(second), next_near, next_far, to_mate(next_near), to_mate(next_far)]
    got = lax.all_to_all(
        part.reshape(chips, per_chip * SLAB, B), "dp", split_axis=0, concat_axis=0, tiled=True, axis_index_groups=same_core
    )
    flat = chip * (per_chip * SLAB) + jnp.arange(per_chip * SLAB)
    t = flat // HALF
    on_diag = jnp.zeros(t.shape, bool)
    for i in range(nb):
        on_diag = on_diag | (t == tri(i, i))
    in_row = core * HALF + flat % HALF
    diag = (on_diag & (flat < used * SLAB))[:, None] & (in_row[:, None] == jnp.arange(B)[None, :])
    damp = jnp.where(is_a, damping[0], damping[1])
    spread, damp_done = damp_and_spread(jnp.stack([total, damp]), got, diag.astype(F32))
    mine = lax.all_to_all(spread, "dp", split_axis=0, concat_axis=0, tiled=True, axis_index_groups=same_core)
    mine = mine.reshape(chips * per_chip * SLAB, B)
    wide = (nb + 2) // 2 * B
    part_w = cross(core_arr, grp_arr, keeps, damp_done, mine_rows, other_rows, chips, wide)
    mine, part_w = lax.optimization_barrier((mine, part_w))
    theirs = lax.ppermute(mine, "dp", swap_core)
    cut = nb - 2
    low, chol_done = chol(core_arr, mine, theirs, width, cut)

    got_w = lax.all_to_all(part_w, "dp", split_axis=0, concat_axis=0, tiled=True, axis_index_groups=same_core)

    at = (dp_index * block).astype(jnp.int32)[None]

    order = column_owner.reshape(chips, 2)
    order = jnp.stack([jnp.where(core == 0, order[:, 0], order[:, 1]), jnp.where(core == 0, order[:, 1], order[:, 0])])
    my_w = sum_parts(got_w, chol_done)
    their_w = lax.ppermute(my_w, "grp", [(1, 0)])
    low = chol_tail(low, width, cut)
    my_rows = rows_of(at, core_arr, mine, theirs, width, ROWS)
    same, cross_t = solve_and_route(grp_arr, order, total[None], my_w, their_w, low, width, block)
    same = lax.ppermute(same, both, [(d, n_dp + d) for d in range(n_dp)])
    cross_t = lax.ppermute(cross_t, both, [(d, n_dp + (d ^ 1)) for d in range(n_dp)])
    is_first = core == 0
    pair = jnp.concatenate([jnp.where(is_first, same, cross_t), jnp.where(is_first, cross_t, same)])
    pair = pair[:, : chips * block].reshape(2 * ROWS, chips, block).transpose(1, 2, 0)
    squares = lax.dynamic_index_in_dim(squares[0].reshape(chips, 2, block), core, 1, keepdims=False)
    pair = jnp.concatenate([pair, squares[:, :, None]], axis=2)
    columns = lax.all_to_all(pair, "dp", split_axis=0, concat_axis=0, tiled=True, axis_index_groups=same_core)
    squares = jnp.sum(columns[:, :, 2 * ROWS], axis=0) / total
    columns = columns[:, :, : 2 * ROWS].transpose(1, 0, 2).reshape(block, n_dp * ROWS)[:, :width]
    columns = jnp.pad(columns, ((0, ROWS - block), (0, 0)))
    left = solve(grp_arr, columns, low, my_rows)[:block]
    here = (dp_index * block + jnp.arange(block))[:, None] == jnp.arange(width)[None, :]
    my_rows = jnp.where(here, squares[:, None], my_rows[:block])
    their_rows = lax.ppermute(my_rows, "grp", swap_grp)
    factors = jnp.stack([jnp.where(is_a, my_rows, their_rows), jnp.where(is_a, their_rows, my_rows)])
    back = lax.ppermute(left, "grp", [(1, 0)])
    preconditioned = jnp.where(is_a, back, left).T
    return (factors, preconditioned)


def solution(mesh):
    placed = (P(("grp", "dp"), None), P(("grp", "dp"), None), P(), P(), P())
    return jax.shard_map(
        per_device,
        mesh=mesh,
        in_specs=placed,
        out_specs=(P(None, "dp", None), P(None, "dp")),
        check_vma=False,
    )
```

```python
import functools

import jax
import jax.numpy as jnp
from jax import lax
from jax.experimental import pallas as pl
from jax.experimental.pallas import tpu as pltpu
from jax.sharding import PartitionSpec as P

TOK = 256
B = 128
HALF = 64
SLAB = 16
ROWS = 24
WIDE = 14336
STEP = 512
REST = 4096
MORE = 8192
F32 = jnp.float32
BF16 = jnp.bfloat16
NT = (((1,), (1,)), ((), ()))
NN = (((1,), (0,)), ((), ()))
TN = (((0,), (0,)), ((), ()))
VM = pl.BlockSpec(memory_space=pltpu.VMEM)
ANY = pl.BlockSpec(memory_space=pl.ANY)
HBM = pl.BlockSpec(memory_space=pltpu.HBM)
SM = pl.BlockSpec(memory_space=pltpu.SMEM)
TOKEN = jax.ShapeDtypeStruct((8, B), F32)
MIB = 1024 * 1024


def params(mib):
    return pltpu.CompilerParams(vmem_limit_bytes=mib * MIB)


def cost(micros):
    return pl.CostEstimate(flops=int(micros * 1.1e9), bytes_accessed=MIB, transcendentals=0)


def dot(a, b, dims=NT):
    return lax.dot_general(a, b, dims, preferred_element_type=F32)


def split(x):
    hi = x.astype(BF16)
    return hi, (x - hi.astype(F32)).astype(BF16)


def row(x, t):
    return jnp.broadcast_to(x[..., t : t + 1, :], x.shape)


def col(x, c):
    return jnp.broadcast_to(x[..., c : c + 1], x.shape)


def rounded(x):
    return x.astype(BF16).astype(F32)


def tri(i, j):
    return i * (i + 1) // 2 + j


def pieces_of(refs):
    own, mate, near, far, near_mate, far_mate = refs
    return [[(0, own)], [(1, mate)], [(2, near), (3, far)], [(4, near_mate), (5, far_mate)]]


def columns_of(group, cols, keep_ref=None):
    parts = [ref[:, cols] if keep_ref is None else ref[:, cols] * keep_ref[k].astype(BF16) for k, ref in group]
    return parts[0] if len(parts) == 1 else jnp.concatenate(parts, 0)


def gram_kernel(core_ref, keep_ref, *refs):
    pieces, (out_ref, squares_ref, tmp_ref) = pieces_of(refs[:6]), refs[6:]
    nb = refs[0].shape[1] // B
    start = pl.multiple_of(core_ref[0] * HALF, HALF)
    on = lax.broadcasted_iota(jnp.int32, (B, B), 0) == lax.broadcasted_iota(jnp.int32, (B, B), 1)
    used = tri(nb, 0) * HALF
    out_ref[used:, :] = jnp.zeros((out_ref.shape[0] - used, B), F32)
    for i in range(nb):
        wide = (i + 1) * B
        acc = None
        for group in pieces:
            p = dot(columns_of(group, slice(i * B, wide), keep_ref), columns_of(group, slice(0, wide)), TN)
            acc = p if acc is None else acc + p
        tmp_ref[:, :wide] = acc
        diag = jnp.sum(jnp.where(on, acc[:, i * B :], 0.0), axis=0, keepdims=True)
        squares_ref[:, i * B : wide] = jnp.broadcast_to(diag, (8, B))
        for j in range(i + 1):
            t = tri(i, j)
            out_ref[t * HALF : (t + 1) * HALF, :] = tmp_ref[pl.ds(start, HALF), j * B : (j + 1) * B]


def gram(core, keeps, pieces, slots):
    width = pieces[0].shape[1]
    return pl.pallas_call(
        gram_kernel,
        out_shape=(jax.ShapeDtypeStruct((slots * SLAB, B), F32), jax.ShapeDtypeStruct((8, width), F32)),
        in_specs=[SM, SM] + [VM] * 6,
        out_specs=(VM, VM),
        scratch_shapes=[pltpu.VMEM((B, width), F32)],
        compiler_params=params(40),
        cost_estimate=cost(4),
        name="gram",
    )(core, keeps, *pieces)


def cross_kernel(core_ref, grp_ref, keep_ref, after_ref, *refs):
    mine, other, (out_ref, tmp_ref) = pieces_of(refs[:6]), pieces_of(refs[6:12]), refs[12:]
    n = refs[0].shape[1]
    wide = out_ref.shape[2]

    def run(left, right, first):
        for i in range(n // B):
            acc = None
            for lg, rg in zip(left, right):
                p = dot(columns_of(lg, slice(i * B, (i + 1) * B), keep_ref), columns_of(rg, slice(first, first + wide)), TN)
                acc = p if acc is None else acc + p
            tmp_ref[i * B : (i + 1) * B, :] = acc

    pl.when(grp_ref[0] == 0)(lambda: run(other, mine, 0))
    pl.when(grp_ref[0] == 1)(lambda: run(mine, other, n - wide))
    tmp_ref[n:, :] = jnp.zeros((tmp_ref.shape[0] - n, wide), F32)
    for q in range(out_ref.shape[0]):
        out_ref[q] = tmp_ref[pl.ds(pl.multiple_of((2 * q + core_ref[0]) * ROWS, 8), ROWS), :]


def cross(core, grp, keeps, after, mine, other, chips, wide):
    return pl.pallas_call(
        cross_kernel,
        out_shape=jax.ShapeDtypeStruct((chips, ROWS, wide), F32),
        in_specs=[SM, SM, SM, ANY] + [VM] * 12,
        out_specs=VM,
        scratch_shapes=[pltpu.VMEM((2 * chips * ROWS, wide), F32)],
        compiler_params=params(40),
        cost_estimate=cost(30),
        name="cross",
    )(core, grp, keeps, after, *mine, *other)


def factor_diag(block):
    a = [block[8 * i : 8 * i + 8, :] for i in range(16)]
    lane = lax.broadcasted_iota(jnp.int32, (8, B), 1)
    sub = lax.broadcasted_iota(jnp.int32, (8, B), 0)
    x = [(lane == sub + 8 * g).astype(F32) for g in range(16)]
    inv, inv_r = [], []
    cg = [col(a[0], t) for t in range(8)]
    for g in range(16):
        here = (lane >= 8 * g) & (lane < 8 * g + 8)
        v = jnp.where(here, (lane == sub + 8 * g).astype(F32), a[g])
        xg = x[g]
        if g < 15:
            near = a[g + 1]
            cr = [col(near, 8 * g + t) for t in range(8)]
            nxt = [col(near, 8 * g + 8 + t) for t in range(8)]
            near, xr = jnp.where(here, 0.0, near), x[g + 1]
        rs, vs, xs, css = [], [], [], []
        for t in range(8):
            p = row(cg[t], t)
            r = lax.rsqrt(p)
            lt = jnp.where(sub > t, cg[t] * r, 0.0)
            vn = row(v, t) * r
            v = jnp.where(sub == t, vn, v - lt * vn)
            xn = row(xg, t) / rounded(p * r)
            xg = jnp.where(sub == t, xn, xg - rounded(lt) * xn)
            cs = {s: row(cg[s], t) * r for s in range(t + 1, 8)}
            for s in range(t + 1, 8):
                cg[s] = cg[s] - lt * cs[s]
            rs.append(r)
            vs.append(vn)
            xs.append(xn)
            css.append(cs)
            if g < 15:
                lr = cr[t] * r
                for s in range(8):
                    nxt[s] = nxt[s] - lr * row(lr, s)
                near = near - lr * vn
                xr = xr - rounded(lr) * xn
                for s in range(t + 1, 8):
                    cr[s] = cr[s] - lr * cs[s]
        inv.append(jnp.where(lane <= sub + 8 * g, v, 0.0))
        inv_r.append(xg)
        if g < 15:
            a[g + 1], x[g + 1] = near, xr
            cg = nxt
        for i in range(g + 2, 16):
            c = [col(a[i], 8 * g + t) for t in range(8)]
            ai, xi = jnp.where(here, 0.0, a[i]), x[i]
            for t in range(8):
                l = c[t] * rs[t]
                ai = ai - l * vs[t]
                xi = xi - rounded(l) * xs[t]
                for s in range(t + 1, 8):
                    c[s] = c[s] - l * css[t][s]
            a[i], x[i] = ai, xi
    return jnp.concatenate(inv, 0), jnp.concatenate(inv_r, 0)


def block_of(mine_ref, other_ref, first, i, j):
    t = tri(i, j) * HALF
    mine = mine_ref[t : t + HALF, :].astype(F32)
    other = other_ref[t : t + HALF, :].astype(F32)
    return jnp.concatenate([jnp.where(first, mine, other), jnp.where(first, other, mine)], 0)


def join_inverses(low_of, inv_ref, iv_ref, first, last):
    iv_ref[...] = jnp.zeros_like(iv_ref)
    for b in range(first, last, B):
        at = b % STEP
        iv_ref[b - first : b - first + B, at : at + B] = inv_ref[b - first : b - first + B, :]
    size = B
    while size < STEP:
        for r0 in range(first, last - size, 2 * size):
            r1 = r0 + size
            r2 = min(r1 + size, last)
            at = r0 % STEP
            i0, i1, i2 = r0 - first, r1 - first, r2 - first
            left = jnp.concatenate(split(iv_ref[i0:i1, at : at + size]), 1)
            p = dot(low_of(slice(r1, r2), slice(r0, r1)), left, NN)
            phi, plo = split(p[:, :size] + p[:, size:])
            bhi, blo = split(iv_ref[i1:i2, at + size : at + size + r2 - r1])
            iv_ref[i1:i2, at : at + size] = -(dot(bhi, phi, NN) + dot(bhi, plo, NN) + dot(blo, phi, NN))
        size *= 2


def halves_of(x):
    return jnp.concatenate(split(x), 1)


def block_of(mine_ref, other_ref, first, i, j):
    t = tri(i, j) * HALF
    mine = mine_ref[t : t + HALF, :].astype(F32)
    other = other_ref[t : t + HALF, :].astype(F32)
    return jnp.concatenate([jnp.where(first, mine, other), jnp.where(first, other, mine)], 0)


def factor_steps(first, last, nb, base, block, low_ref, lo_ref, inv_ref, s_ref, w_ref, each):
    def update(kk):
        r0 = kk * B
        at = r0 - base
        s = jnp.concatenate([block(i, kk) for i in range(kk, nb)], 0)
        if kk:
            wts = jnp.concatenate([low_ref[at : at + B, :r0], lo_ref[at : at + B, :r0]], 0)
            pr = dot(low_ref[at:, :r0], wts)
            s = s - (pr[:, :B] + pr[:, B:] + dot(lo_ref[at:, :r0], low_ref[at : at + B, :r0]))
        s_ref[at:, :] = s

    def panel(kk):
        r0 = kk * B
        r1 = r0 + B
        at = r1 - base
        shi, slo = split(s_ref[at:, :])
        pr = dot(shi, w_ref[...])
        lp = pr[:, :B] + pr[:, B:] + dot(slo, w_ref[:B, :])
        hi, lo = split(lp)
        low_ref[at:, r0:r1] = hi
        lo_ref[at:, r0:r1] = lo

    def step(k, _):
        for kk in range(first, last):
            pl.when(k == kk)(lambda kk=kk: update(kk))
        rows = pl.ds(pl.multiple_of(k * B - base, B), B)
        each(k, rows)
        linv, lrinv = factor_diag(s_ref[rows, :])
        inv_ref[rows, :] = lrinv
        hi, lo = split(linv)
        w_ref[:B, :] = hi
        w_ref[B:, :] = lo
        for kk in range(first, min(last, nb - 1)):
            pl.when(k == kk)(lambda kk=kk: panel(kk))
        return 0

    lax.fori_loop(first, last, step, 0)


def chol_kernel(
    cut, core_ref, mine_ref, other_ref, low_hbm, done_ref,
    low_ref, lo_ref, inv_ref, s_ref, w_ref, iv_ref, hl_ref, more_ref, sem, rest_sem,
):
    done_ref[...] = jnp.zeros_like(done_ref)
    n = low_ref.shape[0]
    nb = n // B
    first = core_ref[0] == 0
    whole = cut * B // STEP * STEP

    def row_copy(k, rows):
        return pltpu.make_async_copy(low_ref.at[rows], low_hbm.at[rows, :n], sem.at[k])

    factor_steps(
        0, cut, nb, 0, functools.partial(block_of, mine_ref, other_ref, first), low_ref, lo_ref, inv_ref, s_ref, w_ref,
        lambda k, rows: row_copy(k, rows).start(),
    )
    join_inverses(lambda rows, cols: low_ref[rows, cols], inv_ref, iv_ref, 0, whole)
    hl_ref[...] = halves_of(iv_ref[...])
    last = pltpu.make_async_copy(hl_ref, low_hbm.at[:whole, n : n + 2 * STEP], sem.at[cut])
    last.start()
    rest = [
        pltpu.make_async_copy(low_ref.at[cut * B :], low_hbm.at[cut * B : n, :n], rest_sem.at[0]),
        pltpu.make_async_copy(lo_ref.at[cut * B :], low_hbm.at[cut * B : n, REST : REST + n], rest_sem.at[1]),
    ]
    skip = cut * B - whole
    more_ref[:skip, : 2 * B] = halves_of(inv_ref[whole : cut * B, :])
    for i in range(cut, nb):
        for j in range(cut, i + 1):
            at = skip + (i - cut) * B
            more_ref[at : at + B, (j - cut) * B : (j - cut + 1) * B] = block_of(mine_ref, other_ref, first, i, j).astype(BF16)
    rest.append(pltpu.make_async_copy(more_ref, low_hbm.at[whole:n, MORE : MORE + more_ref.shape[1]], rest_sem.at[2]))
    for copy in rest:
        copy.start()
    for k in range(cut):
        row_copy(k, slice(k * B, (k + 1) * B)).wait()
    for copy in [last, *rest]:
        copy.wait()


def chol_tail_kernel(
    cut, n, in_hbm, low_hbm,
    low_ref, lo_ref, inv_ref, s_ref, w_ref, iv_ref, hl_ref, more_ref, sem,
):
    whole = cut * B // STEP * STEP
    skip = cut * B - whole
    loads = [
        pltpu.make_async_copy(in_hbm.at[whole:n, :n], low_ref, sem.at[0]),
        pltpu.make_async_copy(in_hbm.at[cut * B : n, REST : REST + n], lo_ref.at[skip:], sem.at[1]),
        pltpu.make_async_copy(in_hbm.at[whole:n, MORE : MORE + more_ref.shape[1]], more_ref, sem.at[2]),
    ]
    for copy in loads:
        copy.start()
    for copy in loads:
        copy.wait()
    inv_ref[:skip, :] = more_ref[:skip, :B].astype(F32) + more_ref[:skip, B : 2 * B].astype(F32)

    def block(i, j):
        at = skip + (i - cut) * B
        return more_ref[at : at + B, (j - cut) * B : (j - cut + 1) * B].astype(F32)

    factor_steps(cut, n // B, n // B, whole, block, low_ref, lo_ref, inv_ref, s_ref, w_ref, lambda k, rows: None)
    join_inverses(lambda rows, cols: low_ref[rows.start - whole : rows.stop - whole, cols], inv_ref, iv_ref, whole, n)
    hl_ref[...] = halves_of(iv_ref[...])
    copies = [
        pltpu.make_async_copy(low_ref, low_hbm.at[whole:n, :n], sem.at[0]),
        pltpu.make_async_copy(hl_ref, low_hbm.at[whole:n, n : n + 2 * STEP], sem.at[1]),
    ]
    for copy in copies:
        copy.start()
    for copy in copies:
        copy.wait()


def chol(core, mine, other, n, cut):
    whole = cut * B // STEP * STEP
    left = n - cut * B
    return pl.pallas_call(
        functools.partial(chol_kernel, cut),
        out_shape=(
            jax.ShapeDtypeStruct((n, WIDE), BF16),
            TOKEN,
        ),
        in_specs=[SM, VM, VM],
        out_specs=(HBM, VM),
        scratch_shapes=[
            pltpu.VMEM((n, n), BF16),
            pltpu.VMEM((n, n), BF16),
            pltpu.VMEM((n, B), F32),
            pltpu.VMEM((n, B), F32),
            pltpu.VMEM((2 * B, B), BF16),
            pltpu.VMEM((whole, STEP), F32),
            pltpu.VMEM((whole, 2 * STEP), BF16),
            pltpu.VMEM((n - whole, max(2 * B, left)), BF16),
            pltpu.SemaphoreType.DMA((cut + 1,)),
            pltpu.SemaphoreType.DMA((3,)),
        ],
        compiler_params=params(28),
        cost_estimate=cost(39),
        name="cholesky",
    )(core, mine, other)


def chol_tail(low, n, cut):
    rows = n - cut * B // STEP * STEP
    return pl.pallas_call(
        functools.partial(chol_tail_kernel, cut, n),
        out_shape=jax.ShapeDtypeStruct(low.shape, BF16),
        in_specs=[HBM],
        out_specs=HBM,
        input_output_aliases={0: 0},
        scratch_shapes=[
            pltpu.VMEM((rows, n), BF16),
            pltpu.VMEM((rows, n), BF16),
            pltpu.VMEM((rows, B), F32),
            pltpu.VMEM((rows, B), F32),
            pltpu.VMEM((2 * B, B), BF16),
            pltpu.VMEM((rows, STEP), F32),
            pltpu.VMEM((rows, 2 * STEP), BF16),
            pltpu.VMEM((rows, max(2 * B, n - cut * B)), BF16),
            pltpu.SemaphoreType.DMA((3,)),
        ],
        compiler_params=params(28),
        cost_estimate=cost(9),
        name="cholesky_tail",
    )(low)


def solve_into(rhs, m, n, low_hbm, out_ref, low_ref, hl_ref, sem):
    starts = list(range(0, n, STEP))
    loads = []
    for r0 in starts:
        rows = slice(r0, min(r0 + STEP, n))
        if r0:
            loads.append((low_hbm.at[rows, :r0], low_ref.at[rows, :r0]))
        loads.append((low_hbm.at[rows, n : n + 2 * STEP], hl_ref.at[rows]))
    copies = [pltpu.make_async_copy(src, dst, sem.at[k]) for k, (src, dst) in enumerate(loads)]
    for copy in copies:
        copy.start()

    def stacked(x):
        return jnp.concatenate(split(x), 0)

    def fold(p):
        return p[:m] + p[m:]

    def inverted(x, rows, dims):
        w = rows.stop - rows.start
        xs = stacked(x)
        return fold(dot(xs, hl_ref[rows, :w], dims) + dot(xs, hl_ref[rows, STEP : STEP + w], dims))

    parts = [slice(r0, min(r0 + STEP, n)) for r0 in starts]
    acc = []
    for rows in parts:
        s = rhs(rows)
        for done, y in zip(parts, acc):
            if done is parts[0]:
                copies.pop(0).wait()
            s = s - fold(dot(stacked(y), low_ref[rows, done]))
        copies.pop(0).wait()
        acc.append(inverted(s, rows, NT))
    for k in reversed(range(len(parts))):
        z = inverted(acc[k], parts[k], NN)
        out_ref[:, parts[k]] = z
        zs = stacked(z)
        for c in range(k):
            acc[c] = acc[c] - fold(dot(zs, low_ref[parts[k], parts[c]], NN))


def solve_scratch(n):
    return [pltpu.VMEM((n, n), BF16), pltpu.VMEM((n, 2 * STEP), BF16), pltpu.SemaphoreType.DMA((2 * -(-n // STEP) - 1,))]


def solve_kernel(grp_ref, rhs_ref, low_ref, after_ref, out_ref, *scratch):
    m, n = rhs_ref.shape
    pl.when(grp_ref[0] == 1)(lambda: solve_into(lambda cols: rhs_ref[:, cols], m, n, low_ref, out_ref, *scratch))


def solve(grp, rhs, low, after):
    return pl.pallas_call(
        solve_kernel,
        out_shape=jax.ShapeDtypeStruct(rhs.shape, F32),
        in_specs=[SM, VM, HBM, ANY],
        out_specs=VM,
        scratch_shapes=solve_scratch(rhs.shape[1]),
        compiler_params=params(16),
        cost_estimate=cost(7),
        name="solve",
    )(grp, rhs, low, after)


def route_kernel(block, grp_ref, *refs):
    pl.when(grp_ref[0] == 0)(lambda: route(block, *refs))


def route(block, owner_ref, total_ref, one_ref, two_ref, low_ref, same_ref, cross_ref, t_ref, r_ref, *scratch):
    m, wide = one_ref.shape
    n = t_ref.shape[1] - B
    right = jnp.concatenate([one_ref[...], two_ref[:, 2 * wide - n :]], 1) / total_ref[0]

    def rhs(cols):
        return right[:, cols]

    solve_into(rhs, m, n, low_ref, t_ref, *scratch)
    t_ref[:, n:] = jnp.zeros((m, t_ref.shape[1] - n), F32)
    lane = lax.broadcasted_iota(jnp.int32, (m, 2 * B), 1)
    for h, out_ref in enumerate((same_ref, cross_ref)):
        for q in range(owner_ref.shape[1]):
            to, off = block * q // B * B, block * q % B
            src = owner_ref[h, q] * block
            win = t_ref[:, pl.ds(pl.multiple_of(src // B * B, B), 2 * B)]
            win = pltpu.roll(win, (off + 2 * B - src % B) % (2 * B), 1)
            old = r_ref[:, to : to + 2 * B]
            r_ref[:, to : to + 2 * B] = jnp.where((lane >= off) & (lane < off + block), win, old)
        out_ref[...] = r_ref[:, : out_ref.shape[1]]


def solve_and_route(grp, owner, total, one, two, low, n, block):
    m = one.shape[0]
    wide = -(-owner.shape[1] * block // B) * B
    out = jax.ShapeDtypeStruct((m, wide), F32)
    return pl.pallas_call(
        functools.partial(route_kernel, block),
        out_shape=(out, out),
        in_specs=[SM, SM, SM, VM, VM, HBM],
        out_specs=(VM, VM),
        scratch_shapes=[pltpu.VMEM((m, n + B), F32), pltpu.VMEM((m, wide + B), F32)] + solve_scratch(n),
        compiler_params=params(16),
        cost_estimate=cost(9),
        name="solve_and_route",
    )(grp, owner, total, one, two, low)


def sum_kernel(parts_ref, *refs):
    out_ref, buf_ref, sem = refs[-3:]
    out_ref[...] = summed(parts_ref, buf_ref, sem)


def summed(parts_hbm, buf_ref, sem):
    count = parts_hbm.shape[0]
    step = count // sem.shape[0]
    copies = [
        pltpu.make_async_copy(parts_hbm.at[k : k + step], buf_ref.at[k : k + step], sem.at[k // step])
        for k in range(0, count, step)
    ]
    for copy in copies:
        copy.start()
    acc = None
    for k in range(count):
        if k % step == 0:
            copies[k // step].wait()
        acc = buf_ref[k] if acc is None else acc + buf_ref[k]
    return acc


def damp_kernel(scale_ref, parts_ref, diag_ref, out_ref, done_ref, sum_ref, buf_ref, sem, buf_sem):
    acc = summed(parts_ref, buf_ref, buf_sem)
    sum_ref[...] = (acc / scale_ref[0] + scale_ref[1] * diag_ref[...]).astype(BF16)
    copies = [pltpu.make_async_copy(sum_ref, out_ref.at[k], sem.at[k]) for k in range(out_ref.shape[0])]
    for copy in copies:
        copy.start()
    done_ref[...] = jnp.zeros_like(done_ref)
    for copy in copies:
        copy.wait()


def damp_and_spread(scale, parts, diag):
    chips = parts.shape[0]
    return pl.pallas_call(
        damp_kernel,
        out_shape=(jax.ShapeDtypeStruct(parts.shape, BF16), TOKEN),
        in_specs=[SM, HBM, VM],
        out_specs=(HBM, VM),
        scratch_shapes=[
            pltpu.VMEM(parts.shape[1:], BF16),
            pltpu.VMEM(parts.shape, F32),
            pltpu.SemaphoreType.DMA((chips,)),
            pltpu.SemaphoreType.DMA((4,)),
        ],
        compiler_params=params(60),
        cost_estimate=cost(3),
        name="damp_and_spread",
    )(scale, parts, diag)


def sum_parts(parts, *after):
    return pl.pallas_call(
        sum_kernel,
        out_shape=jax.ShapeDtypeStruct(parts.shape[1:], F32),
        in_specs=[HBM] + [ANY] * len(after),
        out_specs=VM,
        scratch_shapes=[pltpu.VMEM(parts.shape, F32), pltpu.SemaphoreType.DMA((4,))],
        compiler_params=params(16),
        cost_estimate=cost(3),
        name="sum_parts",
    )(parts, *after)


def rows_kernel(at_ref, core_ref, mine_ref, other_ref, out_ref, s_ref):
    m, n = out_ref.shape
    nb = n // B
    first = core_ref[0] == 0
    for i in range(nb):
        for j in range(i + 1):
            blk = block_of(mine_ref, other_ref, first, i, j)
            s_ref[i * B : (i + 1) * B, j * B : (j + 1) * B] = blk
            if i > j:
                s_ref[j * B : (j + 1) * B, i * B : (i + 1) * B] = blk.T
    at = at_ref[0]
    window = s_ref[pl.ds(pl.multiple_of(at // 8 * 8, 8), 32), :]
    shift = at % 8
    out = window[:m]
    for k in range(1, 8):
        out = jnp.where(shift == k, window[k : k + m], out)
    out_ref[...] = out


def rows_of(at, core, mine, other, n, m):
    return pl.pallas_call(
        rows_kernel,
        out_shape=jax.ShapeDtypeStruct((m, n), F32),
        in_specs=[SM, SM, VM, VM],
        out_specs=VM,
        scratch_shapes=[pltpu.VMEM((n + 8, n), F32)],
        compiler_params=params(16),
        cost_estimate=cost(3),
        name="rows",
    )(at, core, mine, other)


def per_device(attn_out, out_grad, image_counts, column_owner, damping):
    n_dp = lax.axis_size("dp")
    dp_index = lax.axis_index("dp")
    grp_index = lax.axis_index("grp")
    per_dev, width = attn_out.shape
    block = width // n_dp
    chips = n_dp // 2
    core = dp_index % 2
    chip = dp_index // 2
    nb = width // B
    used = tri(nb, 0) * HALF // SLAB
    per_chip = -(-used // chips)
    same_core = [list(range(c, n_dp, 2)) for c in range(2)]
    swap_core = [(d, d ^ 1) for d in range(n_dp)]
    swap_grp = [(0, 1), (1, 0)]
    core_arr = core.astype(jnp.int32)[None]
    grp_arr = grp_index.astype(jnp.int32)[None]
    is_a = grp_index == 0

    def keep_of(grp, dp):
        return (lax.dynamic_index_in_dim(image_counts, grp * n_dp + dp, 0, keepdims=False) > 0).astype(F32)

    flip = n_dp // 2
    near = [(g * n_dp + d, (1 - g) * n_dp + d) for g in range(2) for d in range(n_dp)]
    far = [(g * n_dp + d, (1 - g) * n_dp + d ^ flip) for g in range(2) for d in range(n_dp)]
    both = ("grp", "dp")
    half = per_dev // 2

    def swap(rows):
        return lax.ppermute(rows[:half], both, near), lax.ppermute(rows[half:], both, far)

    def to_mate(rows):
        return lax.ppermute(rows, "dp", swap_core)

    first = jnp.where(is_a, attn_out, out_grad)
    second = jnp.where(is_a, out_grad, attn_out)
    from_near, from_far = swap(second)
    mine_rows = [first, to_mate(first), from_near, from_far, to_mate(from_near), to_mate(from_far)]
    first_later, _, _ = lax.optimization_barrier((first, from_near, from_far))
    next_near, next_far = swap(first_later)
    over, mate, away = 1 - grp_index, dp_index ^ 1, dp_index ^ flip
    keeps = jnp.stack([
        keep_of(grp_index, dp_index),
        keep_of(grp_index, mate),
        keep_of(over, dp_index),
        keep_of(over, away),
        keep_of(over, mate),
        keep_of(over, away ^ 1),
    ])
    total = (TOK * jnp.sum(image_counts)).astype(F32)
    part, squares = gram(core_arr, keeps, mine_rows, chips * per_chip)
    part, next_near, next_far = lax.optimization_barrier((part, next_near, next_far))
    other_rows = [second, to_mate(second), next_near, next_far, to_mate(next_near), to_mate(next_far)]
    got = lax.all_to_all(
        part.reshape(chips, per_chip * SLAB, B), "dp", split_axis=0, concat_axis=0, tiled=True, axis_index_groups=same_core
    )
    flat = chip * (per_chip * SLAB) + jnp.arange(per_chip * SLAB)
    t = flat // HALF
    on_diag = jnp.zeros(t.shape, bool)
    for i in range(nb):
        on_diag = on_diag | (t == tri(i, i))
    in_row = core * HALF + flat % HALF
    diag = (on_diag & (flat < used * SLAB))[:, None] & (in_row[:, None] == jnp.arange(B)[None, :])
    damp = jnp.where(is_a, damping[0], damping[1])
    spread, damp_done = damp_and_spread(jnp.stack([total, damp]), got, diag.astype(F32))
    mine = lax.all_to_all(spread, "dp", split_axis=0, concat_axis=0, tiled=True, axis_index_groups=same_core)
    mine = mine.reshape(chips * per_chip * SLAB, B)
    wide = (nb + 2) // 2 * B
    part_w = cross(core_arr, grp_arr, keeps, damp_done, mine_rows, other_rows, chips, wide)
    mine, part_w = lax.optimization_barrier((mine, part_w))
    theirs = lax.ppermute(mine, "dp", swap_core)
    cut = nb - 2
    low, chol_done = chol(core_arr, mine, theirs, width, cut)

    got_w = lax.all_to_all(part_w, "dp", split_axis=0, concat_axis=0, tiled=True, axis_index_groups=same_core)

    at = (dp_index * block).astype(jnp.int32)[None]

    order = column_owner.reshape(chips, 2)
    order = jnp.stack([jnp.where(core == 0, order[:, 0], order[:, 1]), jnp.where(core == 0, order[:, 1], order[:, 0])])
    my_w = sum_parts(got_w, chol_done)
    their_w = lax.ppermute(my_w, "grp", [(1, 0)])
    low = chol_tail(low, width, cut)
    my_rows = rows_of(at, core_arr, mine, theirs, width, ROWS)
    same, cross_t = solve_and_route(grp_arr, order, total[None], my_w, their_w, low, width, block)
    same = lax.ppermute(same, both, [(d, n_dp + d) for d in range(n_dp)])
    cross_t = lax.ppermute(cross_t, both, [(d, n_dp + (d ^ 1)) for d in range(n_dp)])
    is_first = core == 0
    pair = jnp.concatenate([jnp.where(is_first, same, cross_t), jnp.where(is_first, cross_t, same)])
    pair = pair[:, : chips * block].reshape(2 * ROWS, chips, block).transpose(1, 2, 0)
    squares = lax.dynamic_index_in_dim(squares[0].reshape(chips, 2, block), core, 1, keepdims=False)
    pair = jnp.concatenate([pair, squares[:, :, None]], axis=2)
    columns = lax.all_to_all(pair, "dp", split_axis=0, concat_axis=0, tiled=True, axis_index_groups=same_core)
    squares = jnp.sum(columns[:, :, 2 * ROWS], axis=0) / total
    columns = columns[:, :, : 2 * ROWS].transpose(1, 0, 2).reshape(block, n_dp * ROWS)[:, :width]
    columns = jnp.pad(columns, ((0, ROWS - block), (0, 0)))
    left = solve(grp_arr, columns, low, my_rows)[:block]
    here = (dp_index * block + jnp.arange(block))[:, None] == jnp.arange(width)[None, :]
    my_rows = jnp.where(here, squares[:, None], my_rows[:block])
    their_rows = lax.ppermute(my_rows, "grp", swap_grp)
    factors = jnp.stack([jnp.where(is_a, my_rows, their_rows), jnp.where(is_a, their_rows, my_rows)])
    back = lax.ppermute(left, "grp", [(1, 0)])
    preconditioned = jnp.where(is_a, back, left).T
    return (factors, preconditioned)


def solution(mesh):
    placed = (P(("grp", "dp"), None), P(("grp", "dp"), None), P(), P(), P())
    return jax.shard_map(
        per_device,
        mesh=mesh,
        in_specs=placed,
        out_specs=(P(None, "dp", None), P(None, "dp")),
        check_vma=False,
    )
```
